32 devices in a mesh: dp: 2 (over core), blk: 4 (over y, x), tensor: 4 (over z).
Axes of the slice: x: 2, y: 2, z: 4, core: 2. Of those that a mesh axis runs over, the one named last changes fastest.
Arguments:
- tokens: bfloat16 [4, 2048, 768], P('dp', 'blk', 'tensor'), may hold values from -6 to 6
- segment_ids: int32 [4, 2048], P('dp', 'blk'), may hold values from 0 to 2047, as said below
- input_weight: bfloat16 [3, 768, 768], P(None, None, 'tensor'), may hold values from -0.21875 to 0.21875
- input_bias: float32 [2, 768], P(None, 'tensor'), may hold values from -3 to 3
- output_weight: bfloat16 [768, 768], P('tensor'), may hold values from -1.75 to 1.75
- output_bias: float32 [768], replicated, may hold values from -3 to 3
- first_gain: float32 [768], replicated, may hold values from 0.5 to 1.5
- first_shift: float32 [768], replicated, may hold values from -3 to 3
- up_weight: bfloat16 [768, 3072], P(None, 'tensor'), may hold values from -0.21875 to 0.21875
- up_bias: float32 [3072], P('tensor'), may hold values from -3 to 3
- down_weight: bfloat16 [3072, 768], P('tensor'), may hold values from -0.109375 to 0.109375
- down_bias: float32 [768], replicated, may hold values from -3 to 3
- second_gain: float32 [768], replicated, may hold values from 0.5 to 1.5
- second_shift: float32 [768], replicated, may hold values from -3 to 3
- cotangent: bfloat16 [4, 2048, 768], P('dp', 'blk', 'tensor'), may hold values from -6 to 6
Outputs:
- layer_output: bfloat16 [4, 2048, 768], P('dp', 'blk', 'tensor')
- tokens_grad: float32 [4, 2048, 768], P('dp', 'blk', 'tensor')
- input_weight_grad: float32 [3, 768, 768], P(None, None, 'tensor')
- input_bias_grad: float32 [2, 768], P(None, 'tensor')
- output_weight_grad: float32 [768, 768], P('tensor')
- output_bias_grad: float32 [768], replicated
- first_gain_grad: float32 [768], replicated
- first_shift_grad: float32 [768], replicated
- up_weight_grad: float32 [768, 3072], P(None, 'tensor')
- up_bias_grad: float32 [3072], P('tensor')
- down_weight_grad: float32 [3072, 768], P('tensor')
- down_bias_grad: float32 [768], replicated
- second_gain_grad: float32 [768], replicated
- second_shift_grad: float32 [768], replicated
The draws below stay inside these ranges and needn't reach their ends.
Inputs may be any that keep to these rules, and one draw needn't show every extreme that they name: `segment_ids`: tokens with equal ids form one document. Passages are contiguous runs about 144 tokens long, and each passage's id is the position of its first token, except that one document per row, with id 0, is made of the row's first passage, the passage that holds position 2046 and some passages between them. The row's last position, 2047, is a passage of its own with that id.
All inputs are finite; a program needn't handle non-finite values.
Results may differ from the reference program's by a relative error of at most 0.022.
Values may be sent and summed in bfloat16 or wider, within the bound.
A program may use at most 128 MiB of HBM per device.

```python
import math
import jax
import jax.numpy as jnp
from jax import lax

D = 768
HEADS = 12
HEAD_DIM = 64
FF = 3072
PASSAGE = 144
ROWS = 4
SEQ = 2048


def draw_segment_ids(key, part):
    key = jax.random.fold_in(key, 7)
    cut_key, doc_key = jax.random.split(key)
    position = jnp.broadcast_to(jnp.arange(SEQ, dtype=jnp.int32)[None, :], (ROWS, SEQ))
    boundary = (jax.random.randint(cut_key, (ROWS, SEQ), 0, PASSAGE) == 0) | (position == 0) | (position == SEQ - 1)
    starts = lax.cummax(jnp.where(boundary, position, 0), axis=1)
    joined = jax.random.randint(doc_key, (ROWS, SEQ), 0, 4) == 0
    joined = jnp.take_along_axis(joined, starts, axis=1) & (starts != SEQ - 1)
    near_last = starts[:, -2:-1]
    return jnp.where(joined | (starts == near_last), 0, starts).astype(jnp.int32)


def levels(own_key, shape, cuts, low, largest):
    loudness, own = 1.0, jax.random.fold_in(own_key, 6)
    for dim, blocks in cuts:
        heights = jnp.exp(jax.random.uniform(jax.random.fold_in(own, dim), (blocks,), jnp.float32, low / len(cuts), largest / len(cuts)))
        loudness = loudness * jnp.repeat(heights, shape[dim] // blocks).reshape([-1 if axis == dim else 1 for axis in range(len(shape))])
    return loudness


def gaussian(stream_key, extent, scale, most, shards=(), kind=jnp.bfloat16):
    array = scale * jax.random.normal(stream_key, extent, jnp.float32)
    if shards:
        array = array * levels(stream_key, extent, shards, -0.22, 0.18)
    return jnp.clip(array, -most, most).astype(kind)


def setup_inputs(seed: int = 0) -> dict:
    key_list = jax.random.split(jax.random.key(seed), 16)
    return {
        "tokens": gaussian(key_list[0], (ROWS, SEQ, D), 1.0, 6.0, ((0, 2), (1, 4), (2, 4))),
        "segment_ids": draw_segment_ids(jax.random.fold_in(key_list[15], 71), 0),
        "input_weight": gaussian(key_list[2], (3, D, D), D ** -0.5, 0.21875, ((2, 4),)),
        "input_bias": gaussian(key_list[3], (2, D), 0.5, 3.0, ((1, 4),), jnp.float32),
        "output_weight": gaussian(key_list[4], (D, D), (D // 64) ** -0.5, 1.75, ((0, 4),)),
        "output_bias": gaussian(key_list[5], (D,), 0.5, 3.0, (), jnp.float32),
        "first_gain": jnp.clip(1.0 + 0.1 * jax.random.normal(key_list[6], (D,), jnp.float32), 0.5, 1.5),
        "first_shift": gaussian(key_list[7], (D,), 0.5, 3.0, (), jnp.float32),
        "up_weight": gaussian(key_list[8], (D, FF), D ** -0.5, 0.21875, ((1, 4),)),
        "up_bias": gaussian(key_list[9], (FF,), 0.5, 3.0, ((0, 4),), jnp.float32),
        "down_weight": gaussian(key_list[10], (FF, D), FF ** -0.5, 0.109375, ((0, 4),)),
        "down_bias": gaussian(key_list[11], (D,), 0.5, 3.0, (), jnp.float32),
        "second_gain": jnp.clip(1.0 + 0.1 * jax.random.normal(key_list[12], (D,), jnp.float32), 0.5, 1.5),
        "second_shift": gaussian(key_list[13], (D,), 0.5, 3.0, (), jnp.float32),
        "cotangent": gaussian(key_list[14], (ROWS, SEQ, D), 1.0, 6.0, ((0, 2), (1, 4), (2, 4))),
    }


@jax.custom_vjp
def low(v):
    return lax.optimization_barrier(v.astype(jnp.bfloat16)).astype(jnp.float32)

@jax.custom_vjp
def low_back(v):
    return v

def low_keep(v):
    return (low(v), None)

def low_pass(kept, grad):
    return (grad,)

def back_keep(v):
    return (v, None)

def back_low(kept, grad):
    return (low(grad),)
low.defvjp(low_keep, low_pass)
low_back.defvjp(back_keep, back_low)
layer_eps = 1e-12
highest = lax.Precision.HIGHEST

def layer_norm(residual, gain_vector, shift_vector):
    center = residual - lax.optimization_barrier(jnp.mean(residual, -1, keepdims=True))
    spread = lax.optimization_barrier(jnp.mean(center * center, -1, keepdims=True))
    return center * lax.rsqrt(spread + layer_eps) * gain_vector + shift_vector

def marked(tensor_value):
    return low_back(low(tensor_value))

def attend(queries, keys_all, values_all, segments):
    block_width = math.gcd(SEQ, 512)
    score_scale = HEAD_DIM ** (-0.5)
    query_blocks = queries.reshape(SEQ // block_width, block_width, HEADS, HEAD_DIM)
    segment_blocks = segments.reshape(SEQ // block_width, block_width)
    key_heads = keys_all.reshape(SEQ, HEADS, HEAD_DIM)
    value_heads = values_all.reshape(SEQ, HEADS, HEAD_DIM)

    def one_block(pieces):
        query_block, segment_block = pieces
        scores = low_back(jnp.einsum('qhd,khd->hqk', query_block, key_heads, precision=highest) * score_scale)
        allowed = (segment_block[:, None] == segments[None, :])[None]
        masked = jnp.where(allowed, scores, -1e+30)
        running = lax.optimization_barrier(jnp.max(masked, -1, keepdims=True))
        shifted = jnp.where(allowed, jnp.exp(masked - running), 0.0)
        weights = shifted / lax.optimization_barrier(jnp.sum(shifted, -1, keepdims=True))
        return jnp.einsum('hqk,khd->qhd', low(weights), value_heads, precision=highest)
    context = lax.map(jax.checkpoint(one_block), (query_blocks, segment_blocks))
    return context.reshape(SEQ, D)

def row_forward(tokens_row, segments, weight_set):
    input_weight, input_bias, output_weight, output_bias, first_gain, first_shift, up_weight, up_bias, down_weight, down_bias, second_gain, second_shift = weight_set
    queries = marked(jnp.dot(tokens_row, input_weight[0], precision=highest) + input_bias[0])
    keys_all = marked(jnp.dot(tokens_row, input_weight[1], precision=highest))
    values_all = marked(jnp.dot(tokens_row, input_weight[2], precision=highest) + input_bias[1])
    context = marked(attend(queries, keys_all, values_all, segments))
    attended = low_back(jnp.dot(context, output_weight, precision=highest) + output_bias)
    hidden = layer_norm(tokens_row + attended, first_gain, first_shift)
    before = low_back(jnp.dot(low(hidden), up_weight, precision=highest) + up_bias)
    active = low(jax.nn.gelu(before, approximate=False))
    feed_output = low_back(jnp.dot(active, down_weight, precision=highest) + down_bias)
    return layer_norm(hidden + feed_output, second_gain, second_shift)

def reference(tokens, segment_ids, input_weight, input_bias, output_weight, output_bias, first_gain, first_shift, up_weight, up_bias, down_weight, down_bias, second_gain, second_shift, cotangent):
    params = tuple((weight_arg.astype(jnp.float32) for weight_arg in (input_weight, input_bias, output_weight, output_bias, first_gain, first_shift, up_weight, up_bias, down_weight, down_bias, second_gain, second_shift)))

    def row_step(totals, pieces):
        tokens_row, segments, cotangent_row = pieces
        output_row, pullback = jax.vjp(lambda inner_tokens, weight_set: row_forward(inner_tokens, segments, weight_set), tokens_row, params)
        row_tokens_grad, params_grad = pullback(cotangent_row)
        totals = jax.tree.map(jnp.add, totals, params_grad)
        return (totals, (output_row.astype(jnp.bfloat16), row_tokens_grad))
    zero_grads = jax.tree.map(jnp.zeros_like, params)
    totals, (layer_output, tokens_grad) = lax.scan(row_step, zero_grads, (tokens.astype(jnp.float32), segment_ids, cotangent.astype(jnp.float32)))
    return (layer_output, tokens_grad, totals[0], totals[1], totals[2], totals[3], totals[4], totals[5], totals[6], totals[7], totals[8], totals[9], totals[10], totals[11])
```

```python
import functools

import jax
import jax.numpy as jnp
from jax import lax
from jax.experimental import pallas as pl
from jax.experimental.pallas import tpu as pltpu
from jax.sharding import PartitionSpec as P

HEAD_DIM = 64
EPS = 1e-12
MASKED = -1e30
MESH = pl.DeviceIdType.MESH
bf16 = jnp.bfloat16
f32 = jnp.float32
VMEM_LIMIT = 60 * 2**20


def dot(a, b, ca, cb):
    return lax.dot_general(a, b, (((ca,), (cb,)), ((), ())), preferred_element_type=f32)


def aligned(index, size):
    return pl.multiple_of(index * size, size)


def cut(index, size):
    return pl.ds(aligned(index, size), size)


class Sems:
    def __init__(self, ref=None):
        self.ref = ref
        self.used = 0

    def take(self, count):
        first = self.used
        self.used += count
        return first


class Swap:
    def __init__(self, sems, axis, n, src, dst, xor=False, stride=1):
        self.sems, self.axis, self.n, self.src, self.dst, self.xor = sems, axis, n, src, dst, xor
        self.stride = stride
        self.me = lax.axis_index(axis)
        self.send, self.recv = sems.take(n), sems.take(n)

    def to(self, k):
        return self.me ^ (k * self.stride) if self.xor else lax.rem(self.me + k, self.n)

    def source(self, k):
        return self.me ^ (k * self.stride) if self.xor else lax.rem(self.me + self.n - k, self.n)

    def copy(self, k, dst_index):
        return pltpu.make_async_remote_copy(
            self.src(self.to(k)),
            self.dst(dst_index),
            self.sems.ref.at[self.send + k],
            self.sems.ref.at[self.recv + k],
            device_id={self.axis: self.to(k)},
            device_id_type=MESH,
        )

    def start_one(self, k):
        self.copy(k, self.me).start()

    def start(self):
        each(1, self.n, self.start_one)

    def wait(self, k):
        self.copy(k, self.source(k)).wait_recv()

    def wait_all(self):
        each(1, self.n, self.wait)

    def done(self):
        each(1, self.n, lambda k: self.copy(k, self.me).wait_send())


def each(low, high, body):
    if high - low <= 4:
        for k in range(low, high):
            body(k)
    else:

        def step(k, carry):
            body(k)
            return carry

        lax.fori_loop(low, high, step, 0)


class Line:
    def __init__(self, sems, n, view, own):
        self.sems, self.n, self.view, self.own = sems, n, view, own
        self.t = lax.axis_index("tensor")
        self.recv, self.right, self.left = sems.take(n), sems.take(n), sems.take(n)

    def copy(self, chunk, right, k):
        return pltpu.make_async_remote_copy(
            self.own if k == 0 else self.view(chunk),
            self.view(chunk),
            self.sems.ref.at[(self.right if right else self.left) + k],
            self.sems.ref.at[self.recv + chunk],
            device_id={"tensor": self.t + 1 if right else self.t - 1},
            device_id_type=MESH,
        )

    def start(self):
        t, n = self.t, self.n
        pl.when(t < n - 1)(lambda: self.copy(t, True, 0).start())
        pl.when(t > 0)(lambda: self.copy(t, False, 0).start())

    def step(self, k):
        t, n = self.t, self.n

        @pl.when(t >= k)
        def _():
            self.copy(t - k, True, k).wait_recv()
            pl.when(t < n - 1)(lambda: self.copy(t - k, True, k).start())

        @pl.when(t + k < n)
        def _():
            self.copy(t + k, False, k).wait_recv()
            pl.when(t > 0)(lambda: self.copy(t + k, False, k).start())

    def done(self):
        t, n = self.t, self.n
        for k in range(n):
            pl.when((t >= k) & (t < n - 1))(lambda k=k: self.copy(t - k, True, k).wait_send())
            pl.when((t + k < n) & (t > 0))(lambda k=k: self.copy(t + k, False, k).wait_send())


class Plane:
    def __init__(self, sems, n, view, own):
        self.sems, self.n, self.view, self.own = sems, n, view, own
        self.b = lax.axis_index("blk")
        self.send, self.recv = sems.take(2 * n), sems.take(2 * n)

    def copy(self, k, half, origin, to, own):
        return pltpu.make_async_remote_copy(
            self.own(half) if own else self.view(origin, half),
            self.view(origin, half),
            self.sems.ref.at[self.send + 2 * k + half],
            self.sems.ref.at[self.recv + 2 * k + half],
            device_id={"blk": to},
            device_id_type=MESH,
        )

    def ours(self, k, half):
        return self.copy(k, half, self.b, self.b ^ k, True)

    def passed(self, half):
        origin, to = (self.b ^ 1, self.b ^ 2) if half == 0 else (self.b ^ 2, self.b ^ 1)
        return self.copy(3, half, origin, to, False)

    def start(self):
        if self.n == 4:
            for k, half in ((1, 0), (2, 1), (1, 1), (2, 0)):
                self.ours(k, half).start()
        else:

            def go(k):
                self.ours(k, 0).start()
                self.ours(k, 1).start()

            each(1, self.n, go)

    def landed(self, k, half):
        self.copy(k, half, self.b ^ k, self.b ^ k, True).wait_recv()

    def forward(self):
        if self.n == 4:
            self.landed(1, 0)
            self.passed(0).start()
            self.landed(2, 1)
            self.passed(1).start()

    def wait(self, k):
        if self.n != 4:
            self.landed(k, 0)
            self.landed(k, 1)
        elif k == 1:
            self.landed(1, 1)
        elif k == 2:
            self.landed(2, 0)
        else:
            self.landed(3, 0)
            self.landed(3, 1)

    def wait_all(self):
        each(1, self.n, self.wait)

    def done(self):
        if self.n == 4:
            for k, half in ((1, 0), (2, 1), (1, 1), (2, 0)):
                self.ours(k, half).wait_send()
            self.passed(0).wait_send()
            self.passed(1).wait_send()
        else:

            def go(k):
                self.ours(k, 0).wait_send()
                self.ours(k, 1).wait_send()

            each(1, self.n, go)


class Dims:
    def __init__(self, mesh, rows, tok, width, ff):
        self.z, self.nb, self.nc = mesh.shape["tensor"], mesh.shape["blk"], mesh.shape["dp"]
        self.rows, self.tok, self.lw, self.ff = rows, tok, width, ff
        self.d = width * self.z
        self.heads = width // HEAD_DIM
        self.pt = tok // self.z
        self.own = rows * self.pt
        self.hf = ff // 2
        self.hid = self.hf * self.z
        self.uq, self.dq, self.oq, self.ol = self.d // 4, self.hf // 4, width // 4, self.d // 2
        self.wr = 3 * width


def enter(dm, dp=True, blk=True, tensor=True):
    barrier = pltpu.get_barrier_semaphore()
    count = 0
    for axis, n, wanted in (("dp", dm.nc, dp), ("blk", dm.nb, blk), ("tensor", dm.z, tensor)):
        if not wanted:
            continue
        me = lax.axis_index(axis)

        def greet(k, axis=axis, n=n, me=me):
            pl.semaphore_signal(barrier, inc=1, device_id={axis: lax.rem(me + k, n)}, device_id_type=MESH)

        each(1, n, greet)
        count += n - 1
    pl.semaphore_wait(barrier, count)


def mask_bias(segg, r, key_block, own_block, tok):
    key_row = segg[key_block, r : r + 1, :]
    column = jnp.transpose(jnp.broadcast_to(key_row.astype(f32), (128, tok)))
    wide = jnp.concatenate([column] * (tok // 128), axis=1)
    query_row = segg[own_block, r : r + 1, :].astype(f32)
    return jnp.where(wide == query_row, 0.0, MASKED)


def forward_kernel(
    dm, tok, seg, w, bcol, ub, cot, up, down, wo,
    xT, xO, qT, kv, segg, ctxr, lse, ctxT, cotT, ubH, upH, downH, woF,
    wT, ctxs, m_s, l_s, acc, ub8, local, sem_ref,
):
    t, b, c = lax.axis_index("tensor"), lax.axis_index("blk"), lax.axis_index("dp")
    q = lax.rem(b, 4)
    sems = Sems(sem_ref)
    lw, pt = dm.lw, dm.pt
    enter(dm)

    token_lines = []
    for r in range(dm.rows):
        xT[r, cut(t, lw), :] = tok[r]
        token_lines.append(
            Line(sems, dm.z, lambda i, r=r: xT.at[r, cut(i, lw), :], xT.at[r, cut(t, lw), :])
        )
    token_lines[0].start()

    segg[b] = jnp.zeros((8, dm.tok), jnp.int32)
    segg[b, 0 : dm.rows, :] = seg[...]
    seg_swap = Swap(sems, "blk", dm.nb, lambda to: segg.at[b], lambda i: segg.at[i], xor=True)
    seg_swap.start()
    ub8[...] = jnp.broadcast_to(ub[:, cut(c, dm.hf)], (8, dm.hf))
    ubH[t] = ub8[...]
    ub_swap = Swap(sems, "tensor", dm.z, lambda to: ub8, lambda i: ubH.at[i])
    ub_swap.start()

    up_own = up.at[cut(q, dm.uq), cut(c, dm.hf)]
    down_own = down.at[pl.ds(pl.multiple_of(dm.hf * c + dm.dq * q, dm.dq), dm.dq), :]
    wo_own = wo.at[cut(q, dm.oq), cut(c, dm.ol)]

    def up_piece(i):
        return upH.at[cut(q, dm.uq), cut(i, dm.hf)]

    def down_piece(i):
        return downH.at[i, cut(q, dm.dq), :]

    def wo_piece(i):
        return woF.at[i, cut(q, dm.oq), cut(c, dm.ol)]

    local_copies = [
        pltpu.make_async_copy(src, dst, local.at[n])
        for n, (src, dst) in enumerate(
            ((up_own, up_piece(t)), (down_own, down_piece(t)), (wo_own, wo_piece(t)))
        )
    ]
    for copy in local_copies:
        copy.start()
    up_line = Line(sems, dm.z, up_piece, up_own)
    down_line = Line(sems, dm.z, down_piece, down_own)
    wo_line = Line(sems, dm.z, wo_piece, wo_own)

    def up_view(i, half):
        return upH.at[cut(lax.rem(i, 4), dm.uq), pl.ds(2 * dm.hf * half, 2 * dm.hf)]

    def down_view(i, half):
        return downH.at[pl.ds(2 * half, 2), cut(lax.rem(i, 4), dm.dq), :]

    def wo_view(i, half):
        return woF.at[pl.ds(2 * half, 2), cut(lax.rem(i, 4), dm.oq), cut(c, dm.ol)]

    up_plane = Plane(sems, 4, up_view, lambda half: up_view(b, half))
    down_plane = Plane(sems, 4, down_view, lambda half: down_view(b, half))
    wo_plane = Plane(sems, 4, wo_view, lambda half: wo_view(b, half))
    wo_pair = Swap(
        sems, "dp", dm.nc, lambda to: woF.at[:, :, cut(c, dm.ol)], lambda i: woF.at[:, :, cut(i, dm.ol)]
    )

    cot_swap = Swap(
        sems,
        "tensor",
        dm.z,
        lambda to: cot.at[:, :, cut(to, pt)],
        lambda i: cotT.at[:, cut(i, lw), :],
    )
    kv_planes = [
        Plane(
            sems,
            dm.nb,
            lambda i, half, r=r: kv.at[r, i, pl.ds(lw * half, lw), :],
            lambda half, r=r: kv.at[r, b, pl.ds(lw * half, lw), :],
        )
        for r in range(dm.rows)
    ]
    ctx_swaps = [
        Swap(
            sems,
            "tensor",
            dm.z,
            lambda to, r=r: ctxs.at[r, :, cut(to, pt)],
            lambda i, r=r: ctxT.at[r, cut(i, lw), :],
        )
        for r in range(dm.rows)
    ]

    for r in range(dm.rows):
        cotT[r, cut(t, lw), :] = cot[r, :, cut(t, pt)]
    for m in range(3):
        wT[pl.ds(lw * m, lw), :] = jnp.transpose(w[m])

    def project(r):
        y = dot(wT[...], xT[r], 1, 0)
        qT[r] = (y[:lw] + bcol[0][:, :1]).astype(bf16) * bf16(HEAD_DIM**-0.5)
        kv[r, b, 0:lw, :] = y[lw : 2 * lw].astype(bf16)
        kv[r, b, lw : 2 * lw, :] = (y[2 * lw :] + bcol[1][:, :1]).astype(bf16)
        xO[r] = xT[r, :, cut(t, pt)]
        for h in range(dm.heads):
            m_s[r, h] = jnp.full((8, dm.tok), MASKED, f32)
            l_s[r, h] = jnp.zeros((8, dm.tok), f32)
            acc[r, h] = jnp.zeros((HEAD_DIM, dm.tok), f32)

    def attend(r, block):
        bias = mask_bias(segg, r, block, b, dm.tok)
        for h in range(dm.heads):
            k = kv[r, block, pl.ds(HEAD_DIM * h, HEAD_DIM), :]
            v = kv[r, block, pl.ds(lw + HEAD_DIM * h, HEAD_DIM), :]
            s = dot(k, qT[r, pl.ds(HEAD_DIM * h, HEAD_DIM), :], 0, 0) + bias
            old = m_s[r, h, :1]
            new = jnp.maximum(old, jnp.max(s, 0, keepdims=True))
            p = jnp.exp(s - new)
            scale = jnp.exp(old - new)
            l_s[r, h, :1] = l_s[r, h, :1] * scale + jnp.sum(p, 0, keepdims=True)
            m_s[r, h, :1] = new
            acc[r, h] = acc[r, h] * scale + dot(v, p.astype(bf16), 1, 0)

    def others(r, first):
        def body(k):
            kv_planes[r].wait(k)
            attend(r, b ^ k)

        each(first, dm.nb, body)

    def finish(r):
        for h in range(dm.heads):
            denominator = l_s[r, h, :1]
            ctx = acc[r, h] / denominator
            ctxr[r, pl.ds(HEAD_DIM * h, HEAD_DIM), :] = ctx
            ctxs[r, pl.ds(HEAD_DIM * h, HEAD_DIM), :] = ctx.astype(bf16)
            lse[r, h : h + 1, :] = m_s[r, h, :1] + jnp.log(denominator)
        ctxT[r, cut(t, lw), :] = ctxs[r, :, cut(t, pt)]
        ctx_swaps[r].start()

    token_lines[0].step(1)
    token_lines[0].step(2)
    token_lines[1].start()
    token_lines[0].step(3)
    project(0)
    kv_planes[0].start()
    token_lines[1].step(1)
    seg_swap.wait_all()
    attend(0, b)
    token_lines[1].step(2)
    kv_planes[0].forward()
    wo_line.start()
    token_lines[1].step(3)
    up_line.start()
    project(1)
    kv_planes[1].start()
    wo_line.step(1)
    attend(1, b)
    wo_line.step(2)
    down_line.start()
    up_line.step(1)
    others(0, 1)
    finish(0)
    wo_line.step(3)
    for copy in local_copies:
        copy.wait()
    kv_planes[1].forward()
    wo_plane.start()
    up_line.step(2)
    down_line.step(1)
    cot_swap.start()
    up_line.step(3)
    up_plane.start()
    others(1, 1)
    finish(1)
    wo_plane.forward()
    down_line.step(2)
    wo_plane.wait_all()
    wo_pair.start()
    up_plane.forward()
    down_line.step(3)
    down_plane.start()
    down_plane.forward()
    up_plane.wait_all()
    down_plane.wait_all()
    wo_pair.wait_all()
    for swap in (*ctx_swaps, cot_swap, ub_swap):
        swap.wait_all()
    for transfer in (*token_lines, up_line, down_line, wo_line, up_plane, down_plane, wo_plane,
                     *kv_planes, *ctx_swaps, cot_swap, ub_swap, seg_swap, wo_pair):
        transfer.done()


def run_forward(dm, tok, seg, w, bcol, ub, cot, up, down, wo):
    shape = jax.ShapeDtypeStruct
    vmem, hbm = pl.BlockSpec(memory_space=pltpu.VMEM), pl.BlockSpec(memory_space=pl.ANY)
    outs = (
        (shape((dm.rows, dm.d, dm.tok), bf16), vmem),
        (shape((dm.rows, dm.d, dm.pt), bf16), vmem),
        (shape((dm.rows, dm.lw, dm.tok), bf16), vmem),
        (shape((dm.rows, dm.nb, 2 * dm.lw, dm.tok), bf16), vmem),
        (shape((dm.nb, 8, dm.tok), jnp.int32), vmem),
        (shape((dm.rows, dm.lw, dm.tok), f32), vmem),
        (shape((dm.rows, 8, dm.tok), f32), vmem),
        (shape((dm.rows, dm.d, dm.pt), bf16), vmem),
        (shape((dm.rows, dm.d, dm.pt), bf16), vmem),
        (shape((dm.z, 8, dm.hf), f32), vmem),
        (shape((dm.d, dm.hid), bf16), hbm),
        (shape((dm.z, dm.hf, dm.d), bf16), hbm),
        (shape((dm.z, dm.lw, dm.d), bf16), hbm),
    )
    stats = pltpu.VMEM((dm.rows, dm.heads, 8, dm.tok), f32)
    return pl.pallas_call(
        functools.partial(forward_kernel, dm),
        name="encoder_forward",
        out_shape=[o[0] for o in outs],
        in_specs=[vmem] * 6 + [hbm] * 3,
        out_specs=[o[1] for o in outs],
        scratch_shapes=[
            pltpu.VMEM((3 * dm.lw, dm.d), bf16),
            pltpu.VMEM((dm.rows, dm.lw, dm.tok), bf16),
            stats,
            stats,
            pltpu.VMEM((dm.rows, dm.heads, HEAD_DIM, dm.tok), f32),
            pltpu.VMEM((8, dm.hf), f32),
            pltpu.SemaphoreType.DMA((3,)),
            pltpu.SemaphoreType.DMA((160 + 10 * dm.nb,)),
        ],
        compiler_params=pltpu.CompilerParams(
            collective_id=0, has_side_effects=True, vmem_limit_bytes=VMEM_LIMIT
        ),
    )(tok, seg, w, bcol, ub, cot, up, down, wo)


def middle_kernel(
    dm, ctxT, xO, cotT, woF, upH, downH, ubH, vec,
    loT, doT, frT, dG, uG, oG, sv,
    hl, gp, act, bg, fgf, fs_s, fs_r, z1_s, z2_s, srg_s, hid_s, outT, cgT, og_s, og_r, sem_ref,
):
    t, c = lax.axis_index("tensor"), lax.axis_index("dp")
    sems = Sems(sem_ref)
    lw, pt, own, d = dm.lw, dm.pt, dm.own, dm.d
    mine, other = cut(c, own), cut(1 - c, own)
    enter(dm, blk=False)
    out_b, g1, s1, down_b, g2, s2 = (vec[n : n + 1, :] for n in range(6))

    def pair(src, dst):
        return Swap(sems, "dp", dm.nc, src, dst)

    hl_pair = pair(lambda to: hl.at[mine], lambda i: hl.at[cut(i, own)])
    feed_pair = pair(lambda to: fs_s.at[0], lambda i: fs_r.at[0])
    fg_pair = pair(lambda to: fgf.at[mine], lambda i: fgf.at[cut(i, own)])
    part_pair = pair(lambda to: fs_s.at[1], lambda i: fs_r.at[1])
    og_pair = pair(lambda to: og_s, lambda i: og_r)
    out_swaps = [
        Swap(sems, "tensor", dm.z,
             lambda to, r=r: outT.at[r, cut(to, lw), :],
             lambda i, r=r: loT.at[r, :, cut(i, pt)])
        for r in range(dm.rows)
    ]
    grad_swaps = [
        Swap(sems, "tensor", dm.z,
             lambda to, r=r: cgT.at[r, cut(to, lw), :],
             lambda i, r=r: doT.at[r, :, cut(i, pt)])
        for r in range(dm.rows)
    ]

    def stats(x):
        center = x - jnp.mean(x, -1, keepdims=True)
        inverse = lax.rsqrt(jnp.mean(center * center, -1, keepdims=True) + EPS)
        return center * inverse, inverse

    def norm_back(g, gain, z, inverse):
        e = g * gain
        return (e - jnp.mean(e, -1, keepdims=True) - z * jnp.mean(e * z, -1, keepdims=True)) * inverse

    def total(x):
        return jnp.sum(x, 0, keepdims=True)

    inverse1 = []
    for r in range(dm.rows):
        rows = pl.ds(pt * r, pt)
        attended = dot(ctxT[r], woF[...], 0, 0) + out_b
        z, inv = stats(jnp.transpose(xO[r].astype(f32)) + attended)
        inverse1.append(inv)
        z1_s[rows, :] = z
        hidden = z * g1 + s1
        hid_s[rows, :] = hidden
        hl[pl.ds(pl.multiple_of(own * c + pt * r, pt), pt), :] = hidden.astype(bf16)
    hl_pair.start()

    def expand(rows):
        for n in range(dm.z):
            cols = pl.ds(dm.hf * n, dm.hf)
            v = dot(hl[rows, :], upH[:, cols], 1, 0) + ubH[n, :1, :]
            phi = 0.5 + 0.5 * lax.erf(v * (0.5**0.5))
            act[rows, cols] = (v * phi).astype(bf16)
            gp[rows, cols] = phi + v * (jnp.exp(-0.5 * v * v) * 0.3989422804014327)

    expand(mine)
    hl_pair.wait_all()
    expand(other)
    fs_s[0] = dot(act[other, :], downH[...], 1, 0).astype(bf16)
    feed_pair.start()
    feed = dot(act[mine, :], downH[...], 1, 0) + down_b
    feed_pair.wait_all()
    z2, inverse2 = stats(hid_s[...] + (feed + fs_r[0].astype(f32)))
    out = z2 * g2 + s2
    g = jnp.concatenate([jnp.transpose(cotT[r].astype(f32)) for r in range(dm.rows)], 0)
    sv[...] = jnp.zeros_like(sv)
    sv[0:1, :] = total(g * z2)
    sv[1:2, :] = total(g)
    resid = norm_back(g, g2, z2, inverse2)
    srg_s[...] = resid
    low = resid.astype(bf16)
    fgf[mine, :] = low
    fg_pair.start()
    sv[2:3, :] = total(low.astype(f32))
    for r in range(dm.rows):
        outT[r] = jnp.transpose(out[pt * r : pt * (r + 1)]).astype(bf16)
        loT[r, :, cut(t, pt)] = outT[r, cut(t, lw), :]
        out_swaps[r].start()

    def contract(rows):
        for n in range(dm.z):
            cols = pl.ds(dm.hf * n, dm.hf)
            grad = dot(fgf[rows, :], downH[cols, :], 1, 1)
            bg[rows, cols] = (grad * gp[rows, cols]).astype(bf16)

    contract(mine)
    fg_pair.wait_all()
    contract(other)
    fs_s[1] = dot(bg[other, :], upH[...], 1, 1).astype(bf16)
    part_pair.start()
    part = dot(bg[mine, :], upH[...], 1, 1)
    part_pair.wait_all()
    hidden_grad = srg_s[...] + (part + fs_r[1].astype(f32))
    z1 = z1_s[...]
    sv[3:4, :] = total(hidden_grad * z1)
    sv[4:5, :] = total(hidden_grad)
    first = norm_back(hidden_grad, g1, z1, jnp.concatenate(inverse1, 0))
    low = first.astype(bf16)
    sv[5:6, :] = total(low.astype(f32))
    for r in range(dm.rows):
        cgT[r] = dot(woF[...], low[pt * r : pt * (r + 1)], 1, 1).astype(bf16)
        doT[r, :, cut(t, pt)] = cgT[r, cut(t, lw), :]
        grad_swaps[r].start()
        frT[r] = jnp.transpose(first[pt * r : pt * (r + 1)])

    out_grad = sum(dot(ctxT[r], low[pt * r : pt * (r + 1)], 1, 0) for r in range(dm.rows))
    oG[...] = jnp.where(c == 0, out_grad[:, : dm.ol], out_grad[:, dm.ol :]).astype(bf16)
    og_s[...] = jnp.where(c == 0, out_grad[:, dm.ol :], out_grad[:, : dm.ol]).astype(bf16)
    og_pair.start()
    for n in range(dm.z):
        cols = pl.ds(dm.hf * n, dm.hf)
        dG[cols, :] = dot(act[:, cols], fgf[...], 0, 0).astype(bf16)
        grad = bg[:, cols]
        uG[:, cols] = dot(hl[...], grad, 0, 0).astype(bf16)
        bias_sum = total(grad.astype(f32))
        row = 6 + 2 * c + n // 2
        sv[pl.ds(row, 1), pl.ds(dm.hf * (n % 2), dm.hf)] = bias_sum
    og_pair.wait_all()
    oG[...] = (oG[...].astype(f32) + og_r[...].astype(f32)).astype(bf16)
    for swap in (*out_swaps, *grad_swaps):
        swap.wait_all()
    for swap in (hl_pair, feed_pair, fg_pair, part_pair, og_pair, *out_swaps, *grad_swaps):
        swap.done()


def run_middle(dm, ctxT, xO, cotT, woF, upH, downH, ubH, vec):
    shape = jax.ShapeDtypeStruct
    vmem = pl.BlockSpec(memory_space=pltpu.VMEM)
    outs = (
        shape((dm.rows, dm.lw, dm.tok), bf16),
        shape((dm.rows, dm.lw, dm.tok), bf16),
        shape((dm.rows, dm.d, dm.pt), f32),
        shape((dm.hid, dm.d), bf16),
        shape((dm.d, dm.hid), bf16),
        shape((dm.d, dm.ol), bf16),
        shape((16, dm.d), f32),
    )
    both = 2 * dm.own
    return pl.pallas_call(
        functools.partial(middle_kernel, dm),
        name="feed_forward",
        out_shape=outs,
        in_specs=[vmem] * 8,
        out_specs=[vmem] * len(outs),
        scratch_shapes=[
            pltpu.VMEM((both, dm.d), bf16),
            pltpu.VMEM((both, dm.hid), f32),
            pltpu.VMEM((both, dm.hid), bf16),
            pltpu.VMEM((both, dm.hid), bf16),
            pltpu.VMEM((both, dm.d), bf16),
            pltpu.VMEM((2, dm.own, dm.d), bf16),
            pltpu.VMEM((2, dm.own, dm.d), bf16),
            pltpu.VMEM((dm.own, dm.d), f32),
            pltpu.VMEM((dm.own, dm.d), f32),
            pltpu.VMEM((dm.own, dm.d), f32),
            pltpu.VMEM((dm.own, dm.d), f32),
            pltpu.VMEM((dm.rows, dm.d, dm.pt), bf16),
            pltpu.VMEM((dm.rows, dm.d, dm.pt), bf16),
            pltpu.VMEM((dm.d, dm.ol), bf16),
            pltpu.VMEM((dm.d, dm.ol), bf16),
            pltpu.SemaphoreType.DMA((100,)),
        ],
        compiler_params=pltpu.CompilerParams(
            collective_id=1, has_side_effects=True, vmem_limit_bytes=VMEM_LIMIT
        ),
    )(ctxT, xO, cotT, woF, upH, downH, ubH, vec)


def backward_kernel(
    dm, qT, kv, segg, lse, ctxr, doT, xT, w, frT, uG, dG, oG, sv,
    tgT, wF, fu, fd, fo, svF, bvF,
    dkv_s, dkv_r, own_kv, dq_s, low_s, delta, tp_s, tp_r,
    ur, dr, orr, us, ds_, os_, u2, d2, o2, vp, vb, vz, vs, wS, wR, w1, wr, bv_s, bvp, bvb, w_acc, gu, gd, go, gw, kvc, local, sem_ref,
):
    t, b, c = lax.axis_index("tensor"), lax.axis_index("blk"), lax.axis_index("dp")
    q = lax.rem(b, 4)
    sems = Sems(sem_ref)
    lw, pt, rows = dm.lw, dm.pt, dm.rows
    enter(dm)

    quarter = lambda i: lax.rem(i, 4)
    first_stage = (
        Swap(sems, "blk", 4, lambda to: uG.at[cut(quarter(to), dm.uq), :], lambda i: ur.at[quarter(i)], xor=True),
        Swap(sems, "blk", 4, lambda to: dG.at[:, cut(quarter(to), dm.dq), :], lambda i: dr.at[quarter(i)], xor=True),
        Swap(sems, "blk", 4, lambda to: oG.at[:, cut(quarter(to), dm.oq), :], lambda i: orr.at[quarter(i)], xor=True),
    )
    second_stage = (
        Swap(sems, "tensor", dm.z, lambda to: us.at[:, cut(to, dm.hf)], lambda i: u2.at[i]),
        Swap(sems, "tensor", dm.z, lambda to: ds_.at[to], lambda i: d2.at[i]),
        Swap(sems, "tensor", dm.z, lambda to: os_.at[to], lambda i: o2.at[i]),
    )
    groups = dm.nb // 4
    mine_u = (cut(q, dm.uq), cut(c, dm.hf))
    mine_d = (pl.ds(pl.multiple_of(dm.hf * c + dm.dq * q, dm.dq), dm.dq), slice(None))
    mine_o = (cut(q, dm.oq), cut(c, dm.ol))
    group_stage = tuple(
        Swap(sems, "blk", groups, lambda to, ref=ref, at=at: ref.at[at], lambda i, got=got: got.at[i // 4], True, 4)
        for ref, at, got in ((fu, mine_u, gu), (fd, mine_d, gd), (fo, mine_o, go))
    )
    split_u, split_o = dm.uq // 2, 128

    def fu_view(i, half):
        return fu.at[pl.ds(pl.multiple_of(dm.uq * quarter(i) + split_u * half, split_u), split_u), cut(c, dm.hf)]

    def fd_view(i, half):
        start = pl.multiple_of(dm.hf * c + dm.dq * quarter(i), dm.dq)
        return fd.at[pl.ds(start, dm.dq), pl.ds(dm.d // 2 * half, dm.d // 2)]

    def fo_view(i, half):
        start = pl.multiple_of(dm.ol * c + split_o * half, 128)
        return fo.at[cut(quarter(i), dm.oq), pl.ds(start, dm.ol - split_o if half else split_o)]

    third_stage = tuple(
        Plane(sems, 4, view, lambda half, view=view: view(b, half)) for view in (fu_view, fd_view, fo_view)
    )
    last_stage = (
        Swap(sems, "dp", dm.nc, lambda to: fu.at[:, cut(c, dm.hf)], lambda i: fu.at[:, cut(i, dm.hf)]),
        Swap(sems, "dp", dm.nc, lambda to: fd.at[cut(c, dm.hf), :], lambda i: fd.at[cut(i, dm.hf), :]),
        Swap(sems, "dp", dm.nc, lambda to: fo.at[:, cut(c, dm.ol)], lambda i: fo.at[:, cut(i, dm.ol)]),
    )
    vec_pair = Swap(sems, "dp", dm.nc, lambda to: sv, lambda i: vp)
    vec_blk = Swap(sems, "blk", dm.nb, lambda to: vs.at[0], lambda i: vb.at[i], xor=True)
    vec_z = Swap(sems, "tensor", dm.z, lambda to: vs.at[1], lambda i: vz.at[i])
    bv_pair = Swap(sems, "dp", dm.nc, lambda to: bv_s.at[0], lambda i: bvp)
    bv_blk = Swap(sems, "blk", dm.nb, lambda to: bv_s.at[1], lambda i: bvb.at[i], xor=True)
    kv_swaps = [
        Swap(sems, "blk", dm.nb, lambda to, r=r: dkv_s.at[r, to], lambda i, r=r: dkv_r.at[r, i], xor=True)
        for r in range(rows)
    ]
    tok_swaps = [
        Swap(sems, "tensor", dm.z, lambda to, r=r: tp_s.at[r, cut(to, lw), :], lambda i, r=r: tp_r.at[r, i])
        for r in range(rows)
    ]
    half_w, wq_r, wq_l = dm.wr // 2, dm.wr // 4, dm.d // 2
    w_pair = Swap(sems, "dp", dm.nc, lambda to: wS.at[cut(to, half_w), :], lambda i: wR)

    def w_at(i):
        return lax.div(quarter(i), 2), lax.rem(i, 2)

    w_blk = Swap(
        sems, "blk", 4,
        lambda to: w1.at[cut(w_at(to)[0], wq_r), cut(w_at(to)[1], wq_l)],
        lambda i: wr.at[quarter(i)], xor=True,
    )
    w_split = 80

    def wf_view(i, half):
        start = pl.multiple_of(half_w * c + wq_r * w_at(i)[0] + w_split * half, 16)
        return wF.at[pl.ds(start, wq_r - w_split if half else w_split), cut(w_at(i)[1], wq_l)]

    start_r, start_l = w_at(b)
    w_mine = (pl.ds(pl.multiple_of(half_w * c + wq_r * start_r, 16), wq_r), cut(start_l, wq_l))
    w_group = Swap(sems, "blk", groups, lambda to: wF.at[w_mine], lambda i: gw.at[i // 4], True, 4)
    w_plane = Plane(sems, 4, wf_view, lambda half: wf_view(b, half))
    w_last = Swap(sems, "dp", dm.nc, lambda to: wF.at[cut(c, half_w), :], lambda i: wF.at[cut(i, half_w), :])

    for swap in first_stage:
        swap.start()
    own_parts = [
        pltpu.make_async_copy(src, dst, local.at[n])
        for n, (src, dst) in enumerate(
            (
                (uG.at[cut(q, dm.uq), :], ur.at[q]),
                (dG.at[:, cut(q, dm.dq), :], dr.at[q]),
                (oG.at[:, cut(q, dm.oq), :], orr.at[q]),
            )
        )
    ]
    for copy in own_parts:
        copy.start()
    vec_pair.start()

    def prepare(r):
        for h in range(dm.heads):
            feats = pl.ds(HEAD_DIM * h, HEAD_DIM)
            delta[r, h : h + 1, :] = jnp.sum(doT[r, feats, :].astype(f32) * ctxr[r, feats, :], 0, keepdims=True)
        dq_s[r] = jnp.zeros((lw, dm.tok), f32)

    def attend(r, block, keep):
        chunk = kv.at[r, block]
        if dm.nb > 4:
            load = pltpu.make_async_copy(chunk, kvc, local.at[3])
            load.start()
            load.wait()
            chunk = kvc
        bias = mask_bias(segg, r, block, b, dm.tok)
        for h in range(dm.heads):
            feats = pl.ds(HEAD_DIM * h, HEAD_DIM)
            more = pl.ds(lw + HEAD_DIM * h, HEAD_DIM)
            k, v = chunk[feats, :], chunk[more, :]
            qh, do = qT[r, feats, :], doT[r, feats, :]
            p = jnp.exp(dot(k, qh, 0, 0) + bias - lse[r, h : h + 1, :])
            ds = (p * (dot(v, do, 0, 0) - delta[r, h : h + 1, :])).astype(bf16)
            dq_s[r, feats, :] += dot(k, ds, 1, 0)
            dk, dv = dot(qh, ds, 1, 1), dot(do, p.astype(bf16), 1, 1)
            if keep:
                own_kv[r, feats, :] = dk
                own_kv[r, more, :] = dv
            else:
                dkv_s[r, block, feats, :] = dk.astype(bf16)
                dkv_s[r, block, more, :] = dv.astype(bf16)

    def attention(r):
        prepare(r)

        def body(k):
            attend(r, b ^ k, False)
            kv_swaps[r].start_one(k)

        each(1, dm.nb, body)
        attend(r, b, True)

    def project(r):
        def add(k):
            kv_swaps[r].wait(k)
            own_kv[r] += dkv_r[r, b ^ k].astype(f32)

        each(1, dm.nb, add)
        low_s[r, 0:lw, :] = (dq_s[r] * HEAD_DIM**-0.5).astype(bf16)
        low_s[r, lw:, :] = own_kv[r].astype(bf16)
        part = sum(dot(w[m], low_s[r, pl.ds(lw * m, lw), :], 1, 0) for m in range(3))
        tp_s[r] = part.astype(bf16)
        tp_s[r, :, cut(t, pt)] = (
            dot_sum(w, low_s.at[r, :, cut(t, pt)], lw) + frT[r]
        ).astype(bf16)
        tok_swaps[r].start()
        ones = jnp.ones((16, dm.tok), bf16)
        for n, m in ((0, 0), (1, 2)):
            sums = dot(ones, low_s[r, pl.ds(lw * m, lw), :], 1, 1)
            if r == 0:
                bv_s[0, n : n + 1, 0:lw] = sums[:1]
            else:
                bv_s[0, n : n + 1, 0:lw] += sums[:1]
        grads = dot(low_s[r], xT[r], 1, 1)
        if r == 0:
            w_acc[...] = grads
        else:
            w_acc[...] += grads

    def add_up(own, parts, n):
        total = own.astype(f32)
        for k in range(n):
            total = total + parts(k)
        return total

    def reduce_first():
        for swap in first_stage:
            swap.wait_all()
        for copy in own_parts:
            copy.wait()
        for got, dst in ((ur, us), (dr, ds_), (orr, os_)):
            dst[...] = add_up(got[0], lambda k, got=got: got[k + 1].astype(f32), 3).astype(bf16)
        for swap in second_stage:
            swap.start()

    def group_sum(own, got):
        return add_up(own, lambda k: got[(b ^ (4 * (k + 1))) // 4].astype(f32), groups - 1)

    def others_sum(got, n, me):
        return lambda k: got[lax.rem(me + 1 + k, n)].astype(f32)

    def reduce_second():
        for swap in second_stage:
            swap.wait_all()
        fu[mine_u] = add_up(us[:, cut(t, dm.hf)], others_sum(u2, dm.z, t), dm.z - 1).astype(bf16)
        fd[mine_d] = add_up(ds_[t], others_sum(d2, dm.z, t), dm.z - 1).astype(bf16)
        fo[mine_o] = add_up(os_[t], others_sum(o2, dm.z, t), dm.z - 1).astype(bf16)
        if groups > 1:
            for swap in group_stage:
                swap.start()
            for swap in group_stage:
                swap.wait_all()
                swap.done()
            for ref, at, got in ((fu, mine_u, gu), (fd, mine_d, gd), (fo, mine_o, go)):
                ref[at] = group_sum(ref[at], got).astype(bf16)
        for plane in third_stage:
            plane.start()

    attention(0)
    attention(1)
    vec_pair.wait_all()
    vs[0] = sv[...] + vp[...]
    vec_blk.start()
    project(0)
    reduce_first()
    project(1)
    wS[...] = w_acc[...].astype(bf16)
    w_pair.start()
    bv_pair.start()
    vec_blk.wait_all()
    vs[1] = vs[0]

    def add_vec(k):
        vs[1] += vb[b ^ k]

    each(1, dm.nb, add_vec)
    vec_z.start()
    w_pair.wait_all()
    w1[...] = (w_acc[cut(c, half_w), :] + wR[...].astype(f32)).astype(bf16)
    w_blk.start()
    bv_pair.wait_all()
    bv_s[1] = bv_s[0] + bvp[...]
    bv_blk.start()
    reduce_second()
    for r in range(rows):
        tok_swaps[r].wait_all()
        total = tp_s[r, cut(t, lw), :].astype(f32)
        for k in range(1, dm.z):
            total = total + tp_r[r, lax.rem(t + k, dm.z)].astype(f32)
        tgT[r] = total
    w_blk.wait_all()
    mine = w1[cut(start_r, wq_r), cut(start_l, wq_l)]
    wF[w_mine] = add_up(
        mine, lambda k: wr[q ^ (k + 1)].astype(f32), 3
    ).astype(bf16)
    if groups > 1:
        w_group.start()
        w_group.wait_all()
        w_group.done()
        wF[w_mine] = group_sum(wF[w_mine], gw).astype(bf16)
    w_plane.start()
    for plane in third_stage:
        plane.forward()
    w_plane.forward()
    vec_z.wait_all()
    svF[...] = add_up(vs[1], others_sum(vz, dm.z, t), dm.z - 1)
    bv_blk.wait_all()
    bvF[...] = bv_s[1]

    def add_bias(k):
        bvF[...] += bvb[b ^ k]

    each(1, dm.nb, add_bias)
    for plane, swap in zip((*third_stage, w_plane), (*last_stage, w_last), strict=True):
        plane.wait_all()
        swap.start()
    for swap in (*last_stage, w_last):
        swap.wait_all()
    for transfer in (*first_stage, *second_stage, *third_stage, *last_stage, vec_pair, vec_blk, vec_z, bv_pair,
                     bv_blk, *kv_swaps, *tok_swaps, w_pair, w_blk, w_plane, w_last):
        transfer.done()


def dot_sum(w, low, lw):
    return sum(dot(w[m], low[pl.ds(lw * m, lw), :], 1, 0) for m in range(3))


def run_backward(dm, qT, kv, segg, lse, ctxr, doT, xT, w, frT, uG, dG, oG, sv):
    shape = jax.ShapeDtypeStruct
    vmem, hbm = pl.BlockSpec(memory_space=pltpu.VMEM), pl.BlockSpec(memory_space=pl.ANY)
    outs = (
        shape((dm.rows, dm.lw, dm.tok), f32),
        shape((dm.wr, dm.d), bf16),
        shape((dm.d, dm.ff), bf16),
        shape((dm.ff, dm.d), bf16),
        shape((dm.lw, dm.d), bf16),
        shape((16, dm.d), f32),
        shape((8, 256), f32),
    )
    rows, lw, tok, d = dm.rows, dm.lw, dm.tok, dm.d
    V = pltpu.VMEM
    return pl.pallas_call(
        functools.partial(backward_kernel, dm),
        name="encoder_backward",
        out_shape=outs,
        in_specs=[vmem, hbm if dm.nb > 4 else vmem] + [vmem] * 7 + [hbm] * 3 + [vmem],
        out_specs=[vmem] * len(outs),
        scratch_shapes=[
            V((rows, dm.nb, 2 * lw, tok), bf16),
            V((rows, dm.nb, 2 * lw, tok), bf16),
            V((rows, 2 * lw, tok), f32),
            V((rows, lw, tok), f32),
            V((rows, 3 * lw, tok), bf16),
            V((rows, 8, tok), f32),
            V((rows, d, tok), bf16),
            V((rows, dm.z, lw, tok), bf16),
            V((4, dm.uq, dm.hid), bf16),
            V((4, dm.z, dm.dq, d), bf16),
            V((4, dm.z, dm.oq, dm.ol), bf16),
            V((dm.uq, dm.hid), bf16),
            V((dm.z, dm.dq, d), bf16),
            V((dm.z, dm.oq, dm.ol), bf16),
            V((dm.z, dm.uq, dm.hf), bf16),
            V((dm.z, dm.dq, d), bf16),
            V((dm.z, dm.oq, dm.ol), bf16),
            V((16, d), f32),
            V((dm.nb, 16, d), f32),
            V((dm.z, 16, d), f32),
            V((2, 16, d), f32),
            V((dm.wr, d), bf16),
            V((dm.wr // 2, d), bf16),
            V((dm.wr // 2, d), bf16),
            V((4, dm.wr // 4, d // 2), bf16),
            V((2, 8, 256), f32),
            V((8, 256), f32),
            V((dm.nb, 8, 256), f32),
            V((dm.wr, d), f32),
            V((dm.nb // 4, dm.uq, dm.hf), bf16),
            V((dm.nb // 4, dm.dq, d), bf16),
            V((dm.nb // 4, dm.oq, dm.ol), bf16),
            V((dm.nb // 4, dm.wr // 4, d // 2), bf16),
            V((2 * lw, tok), bf16),
            pltpu.SemaphoreType.DMA((4,)),
            pltpu.SemaphoreType.DMA((220 + 8 * dm.nb,)),
        ],
        compiler_params=pltpu.CompilerParams(
            collective_id=2, has_side_effects=True, vmem_limit_bytes=VMEM_LIMIT
        ),
    )(qT, kv, segg, lse, ctxr, doT, xT, w, frT, uG, dG, oG, sv)


def shards(
    mesh, tokens, segment_ids, input_weight, input_bias, output_weight, output_bias, first_gain, first_shift,
    up_weight, up_bias, down_weight, down_bias, second_gain, second_shift, cotangent,
):
    dm = Dims(mesh, *tokens.shape, up_weight.shape[1])
    tokT = jnp.transpose(tokens, (0, 2, 1))
    cotT = jnp.transpose(cotangent, (0, 2, 1))
    bcol = jnp.broadcast_to(input_bias[:, :, None], (2, dm.lw, 128))
    xT, xO, qT, kv, segg, ctxr, lse, ctxT, cotT, ubH, upH, downH, woF = run_forward(
        dm, tokT, segment_ids, input_weight, bcol, up_bias[None], cotT, up_weight, down_weight, output_weight
    )
    vec = jnp.stack(
        [output_bias, first_gain, first_shift, down_bias, second_gain, second_shift, output_bias, output_bias]
    )
    loT, doT, frT, dG, uG, oG, sv = run_middle(
        dm, ctxT, xO, cotT, woF.reshape(dm.d, dm.d), upH, downH.reshape(dm.hid, dm.d), ubH, vec
    )
    tgT, wF, fu, fd, fo, svF, bvF = run_backward(
        dm, qT, kv, segg, lse, ctxr, doT, xT, input_weight, frT, uG, dG.reshape(dm.z, dm.hf, dm.d),
        oG.reshape(dm.z, dm.lw, dm.ol), sv,
    )
    up_bias_grad = lax.dynamic_index_in_dim(
        svF[6:10].reshape(2, dm.z, dm.hf), lax.axis_index("tensor"), 1, False
    ).reshape(dm.ff)
    return (
        jnp.transpose(loT, (0, 2, 1)),
        jnp.transpose(tgT, (0, 2, 1)),
        jnp.transpose(wF.reshape(3, dm.lw, dm.d), (0, 2, 1)).astype(f32),
        bvF[:2, : dm.lw],
        fo.astype(f32),
        svF[5],
        svF[3],
        svF[4],
        fu.astype(f32),
        up_bias_grad,
        fd.astype(f32),
        svF[2],
        svF[0],
        svF[1],
    )


def solution(mesh):
    rows = P("dp", "blk", "tensor")
    placed = (
        rows, P("dp", "blk"), P(None, None, "tensor"), P(None, "tensor"), P("tensor", None), P(), P(), P(),
        P(None, "tensor"), P("tensor"), P("tensor", None), P(), P(), P(), rows,
    )
    results = (
        rows, rows, P(None, None, "tensor"), P(None, "tensor"), P("tensor", None), P(), P(), P(),
        P(None, "tensor"), P("tensor"), P("tensor", None), P(), P(), P(),
    )
    return jax.shard_map(
        functools.partial(shards, mesh), mesh=mesh, in_specs=placed, out_specs=results, check_vma=False
    )
```

```python
import functools

import jax
import jax.numpy as jnp
from jax import lax
from jax.experimental import pallas as pl
from jax.experimental.pallas import tpu as pltpu
from jax.sharding import PartitionSpec as P

HEAD_DIM = 64
EPS = 1e-12
MASKED = -1e30
MESH = pl.DeviceIdType.MESH
bf16 = jnp.bfloat16
f32 = jnp.float32
VMEM_LIMIT = 60 * 2**20


def dot(a, b, ca, cb):
    return lax.dot_general(a, b, (((ca,), (cb,)), ((), ())), preferred_element_type=f32)


def aligned(index, size):
    return pl.multiple_of(index * size, size)


def cut(index, size):
    return pl.ds(aligned(index, size), size)


class Sems:
    def __init__(self, ref=None):
        self.ref = ref
        self.used = 0

    def take(self, count):
        first = self.used
        self.used += count
        return first


class Swap:
    def __init__(self, sems, axis, n, src, dst, xor=False, stride=1):
        self.sems, self.axis, self.n, self.src, self.dst, self.xor = sems, axis, n, src, dst, xor
        self.stride = stride
        self.me = lax.axis_index(axis)
        self.send, self.recv = sems.take(n), sems.take(n)

    def to(self, k):
        return self.me ^ (k * self.stride) if self.xor else lax.rem(self.me + k, self.n)

    def source(self, k):
        return self.me ^ (k * self.stride) if self.xor else lax.rem(self.me + self.n - k, self.n)

    def copy(self, k, dst_index):
        return pltpu.make_async_remote_copy(
            self.src(self.to(k)),
            self.dst(dst_index),
            self.sems.ref.at[self.send + k],
            self.sems.ref.at[self.recv + k],
            device_id={self.axis: self.to(k)},
            device_id_type=MESH,
        )

    def start_one(self, k):
        self.copy(k, self.me).start()

    def start(self):
        each(1, self.n, self.start_one)

    def wait(self, k):
        self.copy(k, self.source(k)).wait_recv()

    def wait_all(self):
        each(1, self.n, self.wait)

    def done(self):
        each(1, self.n, lambda k: self.copy(k, self.me).wait_send())


def each(low, high, body):
    if high - low <= 4:
        for k in range(low, high):
            body(k)
    else:

        def step(k, carry):
            body(k)
            return carry

        lax.fori_loop(low, high, step, 0)


class Line:
    def __init__(self, sems, n, view, own):
        self.sems, self.n, self.view, self.own = sems, n, view, own
        self.t = lax.axis_index("tensor")
        self.recv, self.right, self.left = sems.take(n), sems.take(n), sems.take(n)

    def copy(self, chunk, right, k):
        return pltpu.make_async_remote_copy(
            self.own if k == 0 else self.view(chunk),
            self.view(chunk),
            self.sems.ref.at[(self.right if right else self.left) + k],
            self.sems.ref.at[self.recv + chunk],
            device_id={"tensor": self.t + 1 if right else self.t - 1},
            device_id_type=MESH,
        )

    def start(self):
        t, n = self.t, self.n
        pl.when(t < n - 1)(lambda: self.copy(t, True, 0).start())
        pl.when(t > 0)(lambda: self.copy(t, False, 0).start())

    def step(self, k):
        t, n = self.t, self.n

        @pl.when(t >= k)
        def _():
            self.copy(t - k, True, k).wait_recv()
            pl.when(t < n - 1)(lambda: self.copy(t - k, True, k).start())

        @pl.when(t + k < n)
        def _():
            self.copy(t + k, False, k).wait_recv()
            pl.when(t > 0)(lambda: self.copy(t + k, False, k).start())

    def done(self):
        t, n = self.t, self.n
        for k in range(n):
            pl.when((t >= k) & (t < n - 1))(lambda k=k: self.copy(t - k, True, k).wait_send())
            pl.when((t + k < n) & (t > 0))(lambda k=k: self.copy(t + k, False, k).wait_send())


class Plane:
    def __init__(self, sems, n, view, own):
        self.sems, self.n, self.view, self.own = sems, n, view, own
        self.b = lax.axis_index("blk")
        self.send, self.recv = sems.take(2 * n), sems.take(2 * n)

    def copy(self, k, half, origin, to, own):
        return pltpu.make_async_remote_copy(
            self.own(half) if own else self.view(origin, half),
            self.view(origin, half),
            self.sems.ref.at[self.send + 2 * k + half],
            self.sems.ref.at[self.recv + 2 * k + half],
            device_id={"blk": to},
            device_id_type=MESH,
        )

    def ours(self, k, half):
        return self.copy(k, half, self.b, self.b ^ k, True)

    def passed(self, half):
        origin, to = (self.b ^ 1, self.b ^ 2) if half == 0 else (self.b ^ 2, self.b ^ 1)
        return self.copy(3, half, origin, to, False)

    def start(self):
        if self.n == 4:
            for k, half in ((1, 0), (2, 1), (1, 1), (2, 0)):
                self.ours(k, half).start()
        else:

            def go(k):
                self.ours(k, 0).start()
                self.ours(k, 1).start()

            each(1, self.n, go)

    def landed(self, k, half):
        self.copy(k, half, self.b ^ k, self.b ^ k, True).wait_recv()

    def forward(self):
        if self.n == 4:
            self.landed(1, 0)
            self.passed(0).start()
            self.landed(2, 1)
            self.passed(1).start()

    def wait(self, k):
        if self.n != 4:
            self.landed(k, 0)
            self.landed(k, 1)
        elif k == 1:
            self.landed(1, 1)
        elif k == 2:
            self.landed(2, 0)
        else:
            self.landed(3, 0)
            self.landed(3, 1)

    def wait_all(self):
        each(1, self.n, self.wait)

    def done(self):
        if self.n == 4:
            for k, half in ((1, 0), (2, 1), (1, 1), (2, 0)):
                self.ours(k, half).wait_send()
            self.passed(0).wait_send()
            self.passed(1).wait_send()
        else:

            def go(k):
                self.ours(k, 0).wait_send()
                self.ours(k, 1).wait_send()

            each(1, self.n, go)


class Fold:
    def __init__(self, sems, part, relay, inbox):
        self.sems, self.part, self.relay, self.inbox = sems, part, relay, inbox
        self.b = lax.axis_index("blk")
        self.send, self.recv = sems.take(6), sems.take(6)

    def copy(self, n, src, dst, k):
        return pltpu.make_async_remote_copy(
            src,
            dst,
            self.sems.ref.at[self.send + n],
            self.sems.ref.at[self.recv + n],
            device_id={"blk": self.b ^ k},
            device_id_type=MESH,
        )

    def across(self, half):
        return self.copy(half, self.part(self.b ^ 3, half), self.relay(half), half + 1)

    def near(self, half):
        return self.copy(2 + half, self.part(self.b ^ (half + 1), half), self.inbox(half), half + 1)

    def folded(self, half):
        return self.copy(4 + half, self.relay(half), self.inbox(2 + half), 2 - half)

    def fold(self, half):
        self.across(half).wait_recv()
        part, relay = self.part(self.b ^ (2 - half), half), self.relay(half)
        relay[...] = (part[...].astype(f32) + relay[...].astype(f32)).astype(bf16)
        self.folded(half).start()

    def wait(self, half):
        self.near(half).wait_recv()
        self.folded(half).wait_recv()

    def received(self, half):
        return self.inbox(half)[...].astype(f32) + self.inbox(2 + half)[...].astype(f32)

    def done(self):
        for half in (0, 1):
            for transfer in (self.across, self.near, self.folded):
                transfer(half).wait_send()


class Dims:
    def __init__(self, mesh, rows, tok, width, ff):
        self.z, self.nb, self.nc = mesh.shape["tensor"], mesh.shape["blk"], mesh.shape["dp"]
        self.rows, self.tok, self.lw, self.ff = rows, tok, width, ff
        self.d = width * self.z
        self.heads = width // HEAD_DIM
        self.pt = tok // self.z
        self.own = rows * self.pt
        self.hf = ff // 2
        self.hid = self.hf * self.z
        self.uq, self.dq, self.oq, self.ol = self.d // 4, self.hf // 4, width // 4, self.d // 2
        self.wr = 3 * width


def enter(dm, dp=True, blk=True, tensor=True):
    barrier = pltpu.get_barrier_semaphore()
    count = 0
    for axis, n, wanted in (("dp", dm.nc, dp), ("blk", dm.nb, blk), ("tensor", dm.z, tensor)):
        if not wanted:
            continue
        me = lax.axis_index(axis)

        def greet(k, axis=axis, n=n, me=me):
            pl.semaphore_signal(barrier, inc=1, device_id={axis: lax.rem(me + k, n)}, device_id_type=MESH)

        each(1, n, greet)
        count += n - 1
    pl.semaphore_wait(barrier, count)


def mask_bias(segg, r, key_block, own_block, tok):
    key_row = segg[key_block, r : r + 1, :]
    column = jnp.transpose(jnp.broadcast_to(key_row.astype(f32), (128, tok)))
    wide = jnp.concatenate([column] * (tok // 128), axis=1)
    query_row = segg[own_block, r : r + 1, :].astype(f32)
    return jnp.where(wide == query_row, 0.0, MASKED)


def forward_kernel(
    dm, tok, seg, w, bcol, ub, cot, up, down, wo,
    xT, xO, qT, kv, segg, ctxr, lse, ctxT, cotT, ubH, upH, downH, woF,
    wT, ctxs, m_s, l_s, acc, ub8, local, sem_ref,
):
    t, b, c = lax.axis_index("tensor"), lax.axis_index("blk"), lax.axis_index("dp")
    q = lax.rem(b, 4)
    sems = Sems(sem_ref)
    lw, pt = dm.lw, dm.pt
    enter(dm)

    token_lines = []
    for r in range(dm.rows):
        xT[r, cut(t, lw), :] = tok[r]
        token_lines.append(
            Line(sems, dm.z, lambda i, r=r: xT.at[r, cut(i, lw), :], xT.at[r, cut(t, lw), :])
        )
    token_lines[0].start()

    segg[b] = jnp.zeros((8, dm.tok), jnp.int32)
    segg[b, 0 : dm.rows, :] = seg[...]
    seg_swap = Swap(sems, "blk", dm.nb, lambda to: segg.at[b], lambda i: segg.at[i], xor=True)
    seg_swap.start()
    ub8[...] = jnp.broadcast_to(ub[:, cut(c, dm.hf)], (8, dm.hf))
    ubH[t] = ub8[...]
    ub_swap = Swap(sems, "tensor", dm.z, lambda to: ub8, lambda i: ubH.at[i])
    ub_swap.start()

    up_own = up.at[cut(q, dm.uq), cut(c, dm.hf)]
    down_own = down.at[pl.ds(pl.multiple_of(dm.hf * c + dm.dq * q, dm.dq), dm.dq), :]
    wo_own = wo.at[cut(q, dm.oq), cut(c, dm.ol)]

    def up_piece(i):
        return upH.at[cut(q, dm.uq), cut(i, dm.hf)]

    def down_piece(i):
        return downH.at[i, cut(q, dm.dq), :]

    def wo_piece(i):
        return woF.at[i, cut(q, dm.oq), cut(c, dm.ol)]

    local_copies = [
        pltpu.make_async_copy(src, dst, local.at[n])
        for n, (src, dst) in enumerate(
            ((up_own, up_piece(t)), (down_own, down_piece(t)), (wo_own, wo_piece(t)))
        )
    ]
    for copy in local_copies:
        copy.start()
    up_line = Line(sems, dm.z, up_piece, up_own)
    down_line = Line(sems, dm.z, down_piece, down_own)
    wo_line = Line(sems, dm.z, wo_piece, wo_own)

    def up_view(i, half):
        return upH.at[cut(lax.rem(i, 4), dm.uq), pl.ds(2 * dm.hf * half, 2 * dm.hf)]

    def down_view(i, half):
        return downH.at[pl.ds(2 * half, 2), cut(lax.rem(i, 4), dm.dq), :]

    def wo_view(i, half):
        return woF.at[pl.ds(2 * half, 2), cut(lax.rem(i, 4), dm.oq), cut(c, dm.ol)]

    up_plane = Plane(sems, 4, up_view, lambda half: up_view(b, half))
    down_plane = Plane(sems, 4, down_view, lambda half: down_view(b, half))
    wo_plane = Plane(sems, 4, wo_view, lambda half: wo_view(b, half))
    wo_pair = Swap(
        sems, "dp", dm.nc, lambda to: woF.at[:, :, cut(c, dm.ol)], lambda i: woF.at[:, :, cut(i, dm.ol)]
    )

    cot_swap = Swap(
        sems,
        "tensor",
        dm.z,
        lambda to: cot.at[:, :, cut(to, pt)],
        lambda i: cotT.at[:, cut(i, lw), :],
    )
    kv_planes = [
        Plane(
            sems,
            dm.nb,
            lambda i, half, r=r: kv.at[r, i, pl.ds(lw * half, lw), :],
            lambda half, r=r: kv.at[r, b, pl.ds(lw * half, lw), :],
        )
        for r in range(dm.rows)
    ]
    ctx_swaps = [
        Swap(
            sems,
            "tensor",
            dm.z,
            lambda to, r=r: ctxs.at[r, :, cut(to, pt)],
            lambda i, r=r: ctxT.at[r, cut(i, lw), :],
        )
        for r in range(dm.rows)
    ]

    for r in range(dm.rows):
        cotT[r, cut(t, lw), :] = cot[r, :, cut(t, pt)]
    for m in range(3):
        wT[pl.ds(lw * m, lw), :] = jnp.transpose(w[m])

    def project(r):
        y = dot(wT[...], xT[r], 1, 0)
        qT[r] = (y[:lw] + bcol[0][:, :1]).astype(bf16) * bf16(HEAD_DIM**-0.5)
        kv[r, b, 0:lw, :] = y[lw : 2 * lw].astype(bf16)
        kv[r, b, lw : 2 * lw, :] = (y[2 * lw :] + bcol[1][:, :1]).astype(bf16)
        xO[r] = xT[r, :, cut(t, pt)]
        for h in range(dm.heads):
            m_s[r, h] = jnp.full((8, dm.tok), MASKED, f32)
            l_s[r, h] = jnp.zeros((8, dm.tok), f32)
            acc[r, h] = jnp.zeros((HEAD_DIM, dm.tok), f32)

    def attend(r, block):
        bias = mask_bias(segg, r, block, b, dm.tok)
        for h in range(dm.heads):
            k = kv[r, block, pl.ds(HEAD_DIM * h, HEAD_DIM), :]
            v = kv[r, block, pl.ds(lw + HEAD_DIM * h, HEAD_DIM), :]
            s = dot(k, qT[r, pl.ds(HEAD_DIM * h, HEAD_DIM), :], 0, 0) + bias
            old = m_s[r, h, :1]
            new = jnp.maximum(old, jnp.max(s, 0, keepdims=True))
            p = jnp.exp(s - new)
            scale = jnp.exp(old - new)
            l_s[r, h, :1] = l_s[r, h, :1] * scale + jnp.sum(p, 0, keepdims=True)
            m_s[r, h, :1] = new
            acc[r, h] = acc[r, h] * scale + dot(v, p.astype(bf16), 1, 0)

    def others(r, first):
        def body(k):
            kv_planes[r].wait(k)
            attend(r, b ^ k)

        each(first, dm.nb, body)

    def finish(r):
        for h in range(dm.heads):
            denominator = l_s[r, h, :1]
            ctx = acc[r, h] / denominator
            ctxr[r, pl.ds(HEAD_DIM * h, HEAD_DIM), :] = ctx
            ctxs[r, pl.ds(HEAD_DIM * h, HEAD_DIM), :] = ctx.astype(bf16)
            lse[r, h : h + 1, :] = m_s[r, h, :1] + jnp.log(denominator)
        ctxT[r, cut(t, lw), :] = ctxs[r, :, cut(t, pt)]
        ctx_swaps[r].start()

    token_lines[0].step(1)
    token_lines[0].step(2)
    token_lines[1].start()
    token_lines[0].step(3)
    project(0)
    kv_planes[0].start()
    token_lines[1].step(1)
    seg_swap.wait_all()
    attend(0, b)
    token_lines[1].step(2)
    kv_planes[0].forward()
    wo_line.start()
    token_lines[1].step(3)
    up_line.start()
    project(1)
    kv_planes[1].start()
    wo_line.step(1)
    attend(1, b)
    wo_line.step(2)
    down_line.start()
    up_line.step(1)
    others(0, 1)
    finish(0)
    wo_line.step(3)
    for copy in local_copies:
        copy.wait()
    kv_planes[1].forward()
    wo_plane.start()
    up_line.step(2)
    down_line.step(1)
    cot_swap.start()
    up_line.step(3)
    up_plane.start()
    others(1, 1)
    finish(1)
    wo_plane.forward()
    down_line.step(2)
    wo_plane.wait_all()
    wo_pair.start()
    up_plane.forward()
    down_line.step(3)
    down_plane.start()
    down_plane.forward()
    up_plane.wait_all()
    down_plane.wait_all()
    wo_pair.wait_all()
    for swap in (*ctx_swaps, cot_swap, ub_swap):
        swap.wait_all()
    for transfer in (*token_lines, up_line, down_line, wo_line, up_plane, down_plane, wo_plane,
                     *kv_planes, *ctx_swaps, cot_swap, ub_swap, seg_swap, wo_pair):
        transfer.done()


def run_forward(dm, tok, seg, w, bcol, ub, cot, up, down, wo):
    shape = jax.ShapeDtypeStruct
    vmem, hbm = pl.BlockSpec(memory_space=pltpu.VMEM), pl.BlockSpec(memory_space=pl.ANY)
    outs = (
        (shape((dm.rows, dm.d, dm.tok), bf16), vmem),
        (shape((dm.rows, dm.d, dm.pt), bf16), vmem),
        (shape((dm.rows, dm.lw, dm.tok), bf16), vmem),
        (shape((dm.rows, dm.nb, 2 * dm.lw, dm.tok), bf16), vmem),
        (shape((dm.nb, 8, dm.tok), jnp.int32), vmem),
        (shape((dm.rows, dm.lw, dm.tok), f32), vmem),
        (shape((dm.rows, 8, dm.tok), f32), vmem),
        (shape((dm.rows, dm.d, dm.pt), bf16), vmem),
        (shape((dm.rows, dm.d, dm.pt), bf16), vmem),
        (shape((dm.z, 8, dm.hf), f32), vmem),
        (shape((dm.d, dm.hid), bf16), hbm),
        (shape((dm.z, dm.hf, dm.d), bf16), hbm),
        (shape((dm.z, dm.lw, dm.d), bf16), hbm),
    )
    stats = pltpu.VMEM((dm.rows, dm.heads, 8, dm.tok), f32)
    return pl.pallas_call(
        functools.partial(forward_kernel, dm),
        name="encoder_forward",
        out_shape=[o[0] for o in outs],
        in_specs=[vmem] * 6 + [hbm] * 3,
        out_specs=[o[1] for o in outs],
        scratch_shapes=[
            pltpu.VMEM((3 * dm.lw, dm.d), bf16),
            pltpu.VMEM((dm.rows, dm.lw, dm.tok), bf16),
            stats,
            stats,
            pltpu.VMEM((dm.rows, dm.heads, HEAD_DIM, dm.tok), f32),
            pltpu.VMEM((8, dm.hf), f32),
            pltpu.SemaphoreType.DMA((3,)),
            pltpu.SemaphoreType.DMA((160 + 10 * dm.nb,)),
        ],
        compiler_params=pltpu.CompilerParams(
            collective_id=0, has_side_effects=True, vmem_limit_bytes=VMEM_LIMIT
        ),
    )(tok, seg, w, bcol, ub, cot, up, down, wo)


def middle_kernel(
    dm, ctxT, xO, cotT, woF, upH, downH, ubH, vec,
    loT, doT, frT, dG, uG, oG, sv,
    hl, gp, act, bg, fgf, fs_s, fs_r, z1_s, z2_s, srg_s, hid_s, outT, cgT, og_s, og_r, sem_ref,
):
    t, c = lax.axis_index("tensor"), lax.axis_index("dp")
    sems = Sems(sem_ref)
    lw, pt, own, d = dm.lw, dm.pt, dm.own, dm.d
    mine, other = cut(c, own), cut(1 - c, own)
    enter(dm, blk=False)
    out_b, g1, s1, down_b, g2, s2 = (vec[n : n + 1, :] for n in range(6))

    def pair(src, dst):
        return Swap(sems, "dp", dm.nc, src, dst)

    hl_pair = pair(lambda to: hl.at[mine], lambda i: hl.at[cut(i, own)])
    feed_pair = pair(lambda to: fs_s.at[0], lambda i: fs_r.at[0])
    fg_pair = pair(lambda to: fgf.at[mine], lambda i: fgf.at[cut(i, own)])
    part_pair = pair(lambda to: fs_s.at[1], lambda i: fs_r.at[1])
    og_pair = pair(lambda to: og_s, lambda i: og_r)
    out_swaps = [
        Swap(sems, "tensor", dm.z,
             lambda to, r=r: outT.at[r, cut(to, lw), :],
             lambda i, r=r: loT.at[r, :, cut(i, pt)])
        for r in range(dm.rows)
    ]
    grad_swaps = [
        Swap(sems, "tensor", dm.z,
             lambda to, r=r: cgT.at[r, cut(to, lw), :],
             lambda i, r=r: doT.at[r, :, cut(i, pt)])
        for r in range(dm.rows)
    ]

    def stats(x):
        center = x - jnp.mean(x, -1, keepdims=True)
        inverse = lax.rsqrt(jnp.mean(center * center, -1, keepdims=True) + EPS)
        return center * inverse, inverse

    def norm_back(g, gain, z, inverse):
        e = g * gain
        return (e - jnp.mean(e, -1, keepdims=True) - z * jnp.mean(e * z, -1, keepdims=True)) * inverse

    def total(x):
        return jnp.sum(x, 0, keepdims=True)

    inverse1 = []
    for r in range(dm.rows):
        rows = pl.ds(pt * r, pt)
        attended = dot(ctxT[r], woF[...], 0, 0) + out_b
        z, inv = stats(jnp.transpose(xO[r].astype(f32)) + attended)
        inverse1.append(inv)
        z1_s[rows, :] = z
        hidden = z * g1 + s1
        hid_s[rows, :] = hidden
        hl[pl.ds(pl.multiple_of(own * c + pt * r, pt), pt), :] = hidden.astype(bf16)
    hl_pair.start()

    def expand(rows):
        for n in range(dm.z):
            cols = pl.ds(dm.hf * n, dm.hf)
            v = dot(hl[rows, :], upH[:, cols], 1, 0) + ubH[n, :1, :]
            phi = 0.5 + 0.5 * lax.erf(v * (0.5**0.5))
            act[rows, cols] = (v * phi).astype(bf16)
            gp[rows, cols] = phi + v * (jnp.exp(-0.5 * v * v) * 0.3989422804014327)

    expand(mine)
    hl_pair.wait_all()
    expand(other)
    fs_s[0] = dot(act[other, :], downH[...], 1, 0).astype(bf16)
    feed_pair.start()
    feed = dot(act[mine, :], downH[...], 1, 0) + down_b
    feed_pair.wait_all()
    z2, inverse2 = stats(hid_s[...] + (feed + fs_r[0].astype(f32)))
    out = z2 * g2 + s2
    g = jnp.concatenate([jnp.transpose(cotT[r].astype(f32)) for r in range(dm.rows)], 0)
    sv[...] = jnp.zeros_like(sv)
    sv[0:1, :] = total(g * z2)
    sv[1:2, :] = total(g)
    resid = norm_back(g, g2, z2, inverse2)
    srg_s[...] = resid
    low = resid.astype(bf16)
    fgf[mine, :] = low
    fg_pair.start()
    sv[2:3, :] = total(low.astype(f32))
    for r in range(dm.rows):
        outT[r] = jnp.transpose(out[pt * r : pt * (r + 1)]).astype(bf16)
        loT[r, :, cut(t, pt)] = outT[r, cut(t, lw), :]
        out_swaps[r].start()

    def contract(rows):
        for n in range(dm.z):
            cols = pl.ds(dm.hf * n, dm.hf)
            grad = dot(fgf[rows, :], downH[cols, :], 1, 1)
            bg[rows, cols] = (grad * gp[rows, cols]).astype(bf16)

    contract(mine)
    fg_pair.wait_all()
    contract(other)
    fs_s[1] = dot(bg[other, :], upH[...], 1, 1).astype(bf16)
    part_pair.start()
    part = dot(bg[mine, :], upH[...], 1, 1)
    part_pair.wait_all()
    hidden_grad = srg_s[...] + (part + fs_r[1].astype(f32))
    z1 = z1_s[...]
    sv[3:4, :] = total(hidden_grad * z1)
    sv[4:5, :] = total(hidden_grad)
    first = norm_back(hidden_grad, g1, z1, jnp.concatenate(inverse1, 0))
    low = first.astype(bf16)
    sv[5:6, :] = total(low.astype(f32))
    for r in range(dm.rows):
        cgT[r] = dot(woF[...], low[pt * r : pt * (r + 1)], 1, 1).astype(bf16)
        doT[r, :, cut(t, pt)] = cgT[r, cut(t, lw), :]
        grad_swaps[r].start()
        frT[r] = jnp.transpose(first[pt * r : pt * (r + 1)])

    out_grad = sum(dot(ctxT[r], low[pt * r : pt * (r + 1)], 1, 0) for r in range(dm.rows))
    oG[...] = jnp.where(c == 0, out_grad[:, : dm.ol], out_grad[:, dm.ol :]).astype(bf16)
    og_s[...] = jnp.where(c == 0, out_grad[:, dm.ol :], out_grad[:, : dm.ol]).astype(bf16)
    og_pair.start()
    for n in range(dm.z):
        cols = pl.ds(dm.hf * n, dm.hf)
        dG[cols, :] = dot(act[:, cols], fgf[...], 0, 0).astype(bf16)
        grad = bg[:, cols]
        uG[:, cols] = dot(hl[...], grad, 0, 0).astype(bf16)
        bias_sum = total(grad.astype(f32))
        row = 6 + 2 * c + n // 2
        sv[pl.ds(row, 1), pl.ds(dm.hf * (n % 2), dm.hf)] = bias_sum
    og_pair.wait_all()
    oG[...] = (oG[...].astype(f32) + og_r[...].astype(f32)).astype(bf16)
    for swap in (*out_swaps, *grad_swaps):
        swap.wait_all()
    for swap in (hl_pair, feed_pair, fg_pair, part_pair, og_pair, *out_swaps, *grad_swaps):
        swap.done()


def run_middle(dm, ctxT, xO, cotT, woF, upH, downH, ubH, vec):
    shape = jax.ShapeDtypeStruct
    vmem = pl.BlockSpec(memory_space=pltpu.VMEM)
    outs = (
        shape((dm.rows, dm.lw, dm.tok), bf16),
        shape((dm.rows, dm.lw, dm.tok), bf16),
        shape((dm.rows, dm.d, dm.pt), f32),
        shape((dm.hid, dm.d), bf16),
        shape((dm.d, dm.hid), bf16),
        shape((dm.d, dm.ol), bf16),
        shape((16, dm.d), f32),
    )
    both = 2 * dm.own
    return pl.pallas_call(
        functools.partial(middle_kernel, dm),
        name="feed_forward",
        out_shape=outs,
        in_specs=[vmem] * 8,
        out_specs=[vmem] * len(outs),
        scratch_shapes=[
            pltpu.VMEM((both, dm.d), bf16),
            pltpu.VMEM((both, dm.hid), f32),
            pltpu.VMEM((both, dm.hid), bf16),
            pltpu.VMEM((both, dm.hid), bf16),
            pltpu.VMEM((both, dm.d), bf16),
            pltpu.VMEM((2, dm.own, dm.d), bf16),
            pltpu.VMEM((2, dm.own, dm.d), bf16),
            pltpu.VMEM((dm.own, dm.d), f32),
            pltpu.VMEM((dm.own, dm.d), f32),
            pltpu.VMEM((dm.own, dm.d), f32),
            pltpu.VMEM((dm.own, dm.d), f32),
            pltpu.VMEM((dm.rows, dm.d, dm.pt), bf16),
            pltpu.VMEM((dm.rows, dm.d, dm.pt), bf16),
            pltpu.VMEM((dm.d, dm.ol), bf16),
            pltpu.VMEM((dm.d, dm.ol), bf16),
            pltpu.SemaphoreType.DMA((100,)),
        ],
        compiler_params=pltpu.CompilerParams(
            collective_id=1, has_side_effects=True, vmem_limit_bytes=VMEM_LIMIT
        ),
    )(ctxT, xO, cotT, woF, upH, downH, ubH, vec)


def backward_kernel(
    dm, qT, kv, segg, lse, ctxr, doT, xT, w, frT, uG, dG, oG, sv,
    tgT, wF, fu, fd, fo, svF, bvF,
    dkv_s, dkv_r, own_kv, dq_s, low_s, delta, tp_s, tp_r,
    ur, dr, orr, us, ds_, os_, u2, d2, o2, vp, vb, vz, vs, wS, wR, w1, wr, bv_s, bvp, bvb, w_acc, gu, gd, go, gw, kvc, local, sem_ref,
):
    t, b, c = lax.axis_index("tensor"), lax.axis_index("blk"), lax.axis_index("dp")
    q = lax.rem(b, 4)
    sems = Sems(sem_ref)
    lw, pt, rows = dm.lw, dm.pt, dm.rows
    enter(dm)

    quarter = lambda i: lax.rem(i, 4)
    def u_part(i, half):
        return uG.at[cut(quarter(i), dm.uq), pl.ds(dm.hid // 2 * half, dm.hid // 2)]

    def d_part(i, half):
        return dG.at[pl.ds(dm.z // 2 * half, dm.z // 2), cut(quarter(i), dm.dq), :]

    def o_part(i, half):
        return oG.at[pl.ds(dm.z // 2 * half, dm.z // 2), cut(quarter(i), dm.oq), :]

    first_stage = tuple(
        Fold(sems, part, lambda half, got=got: got.at[4 + half], lambda n, got=got: got.at[n])
        for part, got in ((u_part, ur), (d_part, dr), (o_part, orr))
    )
    second_stage = (
        Swap(sems, "tensor", dm.z, lambda to: us.at[:, cut(to, dm.hf)], lambda i: u2.at[i]),
        Swap(sems, "tensor", dm.z, lambda to: ds_.at[to], lambda i: d2.at[i]),
        Swap(sems, "tensor", dm.z, lambda to: os_.at[to], lambda i: o2.at[i]),
    )
    groups = dm.nb // 4
    mine_u = (cut(q, dm.uq), cut(c, dm.hf))
    mine_d = (pl.ds(pl.multiple_of(dm.hf * c + dm.dq * q, dm.dq), dm.dq), slice(None))
    mine_o = (cut(q, dm.oq), cut(c, dm.ol))
    group_stage = tuple(
        Swap(sems, "blk", groups, lambda to, ref=ref, at=at: ref.at[at], lambda i, got=got: got.at[i // 4], True, 4)
        for ref, at, got in ((fu, mine_u, gu), (fd, mine_d, gd), (fo, mine_o, go))
    )
    split_u, split_o = dm.uq // 2, 128

    def fu_view(i, half):
        return fu.at[pl.ds(pl.multiple_of(dm.uq * quarter(i) + split_u * half, split_u), split_u), cut(c, dm.hf)]

    def fd_view(i, half):
        start = pl.multiple_of(dm.hf * c + dm.dq * quarter(i), dm.dq)
        return fd.at[pl.ds(start, dm.dq), pl.ds(dm.d // 2 * half, dm.d // 2)]

    def fo_view(i, half):
        start = pl.multiple_of(dm.ol * c + split_o * half, 128)
        return fo.at[cut(quarter(i), dm.oq), pl.ds(start, dm.ol - split_o if half else split_o)]

    third_stage = tuple(
        Plane(sems, 4, view, lambda half, view=view: view(b, half)) for view in (fu_view, fd_view, fo_view)
    )
    last_stage = (
        Swap(sems, "dp", dm.nc, lambda to: fu.at[:, cut(c, dm.hf)], lambda i: fu.at[:, cut(i, dm.hf)]),
        Swap(sems, "dp", dm.nc, lambda to: fd.at[cut(c, dm.hf), :], lambda i: fd.at[cut(i, dm.hf), :]),
        Swap(sems, "dp", dm.nc, lambda to: fo.at[:, cut(c, dm.ol)], lambda i: fo.at[:, cut(i, dm.ol)]),
    )
    vec_pair = Swap(sems, "dp", dm.nc, lambda to: sv, lambda i: vp)
    vec_blk = Swap(sems, "blk", dm.nb, lambda to: vs.at[0], lambda i: vb.at[i], xor=True)
    vec_z = Swap(sems, "tensor", dm.z, lambda to: vs.at[1], lambda i: vz.at[i])
    bv_pair = Swap(sems, "dp", dm.nc, lambda to: bv_s.at[0], lambda i: bvp)
    bv_blk = Swap(sems, "blk", dm.nb, lambda to: bv_s.at[1], lambda i: bvb.at[i], xor=True)
    kv_swaps = [
        Swap(sems, "blk", dm.nb, lambda to, r=r: dkv_s.at[r, to], lambda i, r=r: dkv_r.at[r, i], xor=True)
        for r in range(rows)
    ]
    kv_folds = [
        Fold(
            sems,
            lambda i, half, r=r: dkv_s.at[r, i, pl.ds(lw * half, lw), :],
            lambda half, r=r: dkv_r.at[r, 2, pl.ds(lw * half, lw), :],
            lambda n, r=r: dkv_r.at[r, n // 2, pl.ds(lw * (n % 2), lw), :],
        )
        for r in range(rows)
    ]
    fold_kv = dm.nb == 4
    tok_swaps = [
        Swap(sems, "tensor", dm.z, lambda to, r=r: tp_s.at[r, cut(to, lw), :], lambda i, r=r: tp_r.at[r, i])
        for r in range(rows)
    ]
    half_w, wq_r, wq_l = dm.wr // 2, dm.wr // 4, dm.d // 2
    w_pair = Swap(sems, "dp", dm.nc, lambda to: wS.at[cut(to, half_w), :], lambda i: wR)

    def w_at(i):
        return lax.div(quarter(i), 2), lax.rem(i, 2)

    w_blk = Swap(
        sems, "blk", 4,
        lambda to: w1.at[cut(w_at(to)[0], wq_r), cut(w_at(to)[1], wq_l)],
        lambda i: wr.at[quarter(i)], xor=True,
    )
    w_split = 80

    def wf_view(i, half):
        start = pl.multiple_of(half_w * c + wq_r * w_at(i)[0] + w_split * half, 16)
        return wF.at[pl.ds(start, wq_r - w_split if half else w_split), cut(w_at(i)[1], wq_l)]

    start_r, start_l = w_at(b)
    w_mine = (pl.ds(pl.multiple_of(half_w * c + wq_r * start_r, 16), wq_r), cut(start_l, wq_l))
    w_group = Swap(sems, "blk", groups, lambda to: wF.at[w_mine], lambda i: gw.at[i // 4], True, 4)
    w_plane = Plane(sems, 4, wf_view, lambda half: wf_view(b, half))
    w_last = Swap(sems, "dp", dm.nc, lambda to: wF.at[cut(c, half_w), :], lambda i: wF.at[cut(i, half_w), :])

    vec_pair.start()

    def prepare(r):
        for h in range(dm.heads):
            feats = pl.ds(HEAD_DIM * h, HEAD_DIM)
            delta[r, h : h + 1, :] = jnp.sum(doT[r, feats, :].astype(f32) * ctxr[r, feats, :], 0, keepdims=True)
        dq_s[r] = jnp.zeros((lw, dm.tok), f32)

    def attend(r, block, keep):
        chunk = kv.at[r, block]
        if dm.nb > 4:
            load = pltpu.make_async_copy(chunk, kvc, local.at[3])
            load.start()
            load.wait()
            chunk = kvc
        bias = mask_bias(segg, r, block, b, dm.tok)
        for h in range(dm.heads):
            feats = pl.ds(HEAD_DIM * h, HEAD_DIM)
            more = pl.ds(lw + HEAD_DIM * h, HEAD_DIM)
            k, v = chunk[feats, :], chunk[more, :]
            qh, do = qT[r, feats, :], doT[r, feats, :]
            p = jnp.exp(dot(k, qh, 0, 0) + bias - lse[r, h : h + 1, :])
            ds = (p * (dot(v, do, 0, 0) - delta[r, h : h + 1, :])).astype(bf16)
            dq_s[r, feats, :] += dot(k, ds, 1, 0)
            dk, dv = dot(qh, ds, 1, 1), dot(do, p.astype(bf16), 1, 1)
            if keep:
                own_kv[r, feats, :] = dk
                own_kv[r, more, :] = dv
            else:
                dkv_s[r, block, feats, :] = dk.astype(bf16)
                dkv_s[r, block, more, :] = dv.astype(bf16)

    def attention(r):
        prepare(r)
        if fold_kv:
            fold = kv_folds[r]
            attend(r, b ^ 3, False)
            fold.across(0).start()
            fold.across(1).start()
            attend(r, b ^ 1, False)
            fold.near(0).start()
            attend(r, b ^ 2, False)
            fold.near(1).start()
            fold.fold(0)
            fold.fold(1)
        else:

            def body(k):
                attend(r, b ^ k, False)
                kv_swaps[r].start_one(k)

            each(1, dm.nb, body)
        attend(r, b, True)

    def project(r):
        if fold_kv:
            for half in (0, 1):
                kv_folds[r].wait(half)
                own_kv[r, pl.ds(lw * half, lw), :] += kv_folds[r].received(half)
        else:

            def add(k):
                kv_swaps[r].wait(k)
                load = pltpu.make_async_copy(dkv_r.at[r, b ^ k], kvc, local.at[3])
                load.start()
                load.wait()
                own_kv[r] += kvc[...].astype(f32)

            each(1, dm.nb, add)
        low_s[r, 0:lw, :] = (dq_s[r] * HEAD_DIM**-0.5).astype(bf16)
        low_s[r, lw:, :] = own_kv[r].astype(bf16)
        part = sum(dot(w[m], low_s[r, pl.ds(lw * m, lw), :], 1, 0) for m in range(3))
        tp_s[r] = part.astype(bf16)
        tp_s[r, :, cut(t, pt)] = (
            dot_sum(w, low_s.at[r, :, cut(t, pt)], lw) + frT[r]
        ).astype(bf16)
        tok_swaps[r].start()
        ones = jnp.ones((16, dm.tok), bf16)
        for n, m in ((0, 0), (1, 2)):
            sums = dot(ones, low_s[r, pl.ds(lw * m, lw), :], 1, 1)
            if r == 0:
                bv_s[0, n : n + 1, 0:lw] = sums[:1]
            else:
                bv_s[0, n : n + 1, 0:lw] += sums[:1]
        grads = dot(low_s[r], xT[r], 1, 1)
        if r == 0:
            w_acc[...] = grads
        else:
            w_acc[...] += grads

    def add_up(own, parts, n):
        total = own.astype(f32)
        for k in range(n):
            total = total + parts(k)
        return total

    def send_first(n):
        for half in (0, 1):
            first_stage[n].across(half).start()
        for half in (0, 1):
            first_stage[n].near(half).start()

    def fold_first(n):
        first_stage[n].fold(0)
        first_stage[n].fold(1)

    def reduce_first(n):
        stage, part = first_stage[n], (u_part, d_part, o_part)[n]
        for half in (0, 1):
            stage.wait(half)
            sums = (part(b, half)[...].astype(f32) + stage.received(half)).astype(bf16)
            if n == 0:
                us[:, pl.ds(dm.hid // 2 * half, dm.hid // 2)] = sums
            else:
                (ds_, os_)[n - 1][pl.ds(dm.z // 2 * half, dm.z // 2)] = sums
        second_stage[n].start()

    def group_sum(own, got):
        return add_up(own, lambda k: got[(b ^ (4 * (k + 1))) // 4].astype(f32), groups - 1)

    def others_sum(got, n, me):
        return lambda k: got[lax.rem(me + 1 + k, n)].astype(f32)

    def reduce_second(n):
        second_stage[n].wait_all()
        ref, at, got, group = ((fu, mine_u, u2, gu), (fd, mine_d, d2, gd), (fo, mine_o, o2, go))[n]
        own = (lambda: us[:, cut(t, dm.hf)], lambda: ds_[t], lambda: os_[t])[n]()
        ref[at] = add_up(own, others_sum(got, dm.z, t), dm.z - 1).astype(bf16)
        if groups > 1:
            swap = group_stage[n]
            swap.start()
            swap.wait_all()
            swap.done()
            ref[at] = group_sum(ref[at], group).astype(bf16)
        third_stage[n].start()

    attention(0)
    attention(1)
    send_first(0)
    project(0)
    send_first(1)
    send_first(2)
    project(1)
    fold_first(0)
    vec_pair.wait_all()
    vs[0] = sv[...] + vp[...]
    vec_blk.start()
    wS[...] = w_acc[...].astype(bf16)
    w_pair.start()
    bv_pair.start()
    fold_first(1)
    fold_first(2)
    w_pair.wait_all()
    w1[...] = (w_acc[cut(c, half_w), :] + wR[...].astype(f32)).astype(bf16)
    w_blk.start()
    bv_pair.wait_all()
    bv_s[1] = bv_s[0] + bvp[...]
    bv_blk.start()
    reduce_first(0)
    for r in range(rows):
        tok_swaps[r].wait_all()
        total = tp_s[r, cut(t, lw), :].astype(f32)
        for k in range(1, dm.z):
            total = total + tp_r[r, lax.rem(t + k, dm.z)].astype(f32)
        tgT[r] = total
    reduce_first(1)
    reduce_first(2)
    vec_blk.wait_all()
    vs[1] = vs[0]

    def add_vec(k):
        vs[1] += vb[b ^ k]

    each(1, dm.nb, add_vec)
    vec_z.start()
    w_blk.wait_all()
    mine = w1[cut(start_r, wq_r), cut(start_l, wq_l)]
    wF[w_mine] = add_up(mine, lambda k: wr[q ^ (k + 1)].astype(f32), 3).astype(bf16)
    if groups > 1:
        w_group.start()
        w_group.wait_all()
        w_group.done()
        wF[w_mine] = group_sum(wF[w_mine], gw).astype(bf16)
    w_plane.start()
    reduce_second(0)
    w_plane.forward()
    reduce_second(1)
    reduce_second(2)
    for plane in third_stage:
        plane.forward()
    vec_z.wait_all()
    svF[...] = add_up(vs[1], others_sum(vz, dm.z, t), dm.z - 1)
    bv_blk.wait_all()
    bvF[...] = bv_s[1]

    def add_bias(k):
        bvF[...] += bvb[b ^ k]

    each(1, dm.nb, add_bias)
    for plane, swap in zip((*third_stage, w_plane), (*last_stage, w_last), strict=True):
        plane.wait_all()
        swap.start()
    for swap in (*last_stage, w_last):
        swap.wait_all()
    for transfer in (*first_stage, *second_stage, *third_stage, *last_stage, vec_pair, vec_blk, vec_z, bv_pair,
                     bv_blk, *(kv_folds if fold_kv else kv_swaps), *tok_swaps, w_pair, w_blk, w_plane, w_last):
        transfer.done()


def dot_sum(w, low, lw):
    return sum(dot(w[m], low[pl.ds(lw * m, lw), :], 1, 0) for m in range(3))


def run_backward(dm, qT, kv, segg, lse, ctxr, doT, xT, w, frT, uG, dG, oG, sv):
    shape = jax.ShapeDtypeStruct
    vmem, hbm = pl.BlockSpec(memory_space=pltpu.VMEM), pl.BlockSpec(memory_space=pl.ANY)
    outs = (
        shape((dm.rows, dm.lw, dm.tok), f32),
        shape((dm.wr, dm.d), bf16),
        shape((dm.d, dm.ff), bf16),
        shape((dm.ff, dm.d), bf16),
        shape((dm.lw, dm.d), bf16),
        shape((16, dm.d), f32),
        shape((8, 256), f32),
    )
    rows, lw, tok, d = dm.rows, dm.lw, dm.tok, dm.d
    V = pltpu.VMEM
    kernel = functools.partial(backward_kernel, dm)
    if dm.nb != 4:
        outs += (shape((rows, dm.nb, 2 * lw, tok), bf16),)

        def kernel(*refs):
            backward_kernel(dm, *refs[:20], refs[21], refs[20], *refs[22:])

    return pl.pallas_call(
        kernel,
        name="encoder_backward",
        out_shape=outs,
        in_specs=[vmem, hbm if dm.nb > 4 else vmem] + [vmem] * 11,
        out_specs=[vmem] * 7 + [hbm] * (len(outs) - 7),
        scratch_shapes=[
            V((rows, dm.nb, 2 * lw, tok), bf16),
            *([V((rows, 3, 2 * lw, tok), bf16)] if dm.nb == 4 else []),
            V((rows, 2 * lw, tok), f32),
            V((rows, lw, tok), f32),
            V((rows, 3 * lw, tok), bf16),
            V((rows, 8, tok), f32),
            V((rows, d, tok), bf16),
            V((rows, dm.z, lw, tok), bf16),
            V((6, dm.uq, dm.hid // 2), bf16),
            V((6, dm.z // 2, dm.dq, d), bf16),
            V((6, dm.z // 2, dm.oq, dm.ol), bf16),
            V((dm.uq, dm.hid), bf16),
            V((dm.z, dm.dq, d), bf16),
            V((dm.z, dm.oq, dm.ol), bf16),
            V((dm.z, dm.uq, dm.hf), bf16),
            V((dm.z, dm.dq, d), bf16),
            V((dm.z, dm.oq, dm.ol), bf16),
            V((16, d), f32),
            V((dm.nb, 16, d), f32),
            V((dm.z, 16, d), f32),
            V((2, 16, d), f32),
            V((dm.wr, d), bf16),
            V((dm.wr // 2, d), bf16),
            V((dm.wr // 2, d), bf16),
            V((4, dm.wr // 4, d // 2), bf16),
            V((2, 8, 256), f32),
            V((8, 256), f32),
            V((dm.nb, 8, 256), f32),
            V((dm.wr, d), f32),
            V((dm.nb // 4, dm.uq, dm.hf), bf16),
            V((dm.nb // 4, dm.dq, d), bf16),
            V((dm.nb // 4, dm.oq, dm.ol), bf16),
            V((dm.nb // 4, dm.wr // 4, d // 2), bf16),
            V((2 * lw, tok), bf16),
            pltpu.SemaphoreType.DMA((4,)),
            pltpu.SemaphoreType.DMA((220 + 8 * dm.nb,)),
        ],
        compiler_params=pltpu.CompilerParams(
            collective_id=2, has_side_effects=True, vmem_limit_bytes=VMEM_LIMIT
        ),
    )(qT, kv, segg, lse, ctxr, doT, xT, w, frT, uG, dG, oG, sv)


def shards(
    mesh, tokens, segment_ids, input_weight, input_bias, output_weight, output_bias, first_gain, first_shift,
    up_weight, up_bias, down_weight, down_bias, second_gain, second_shift, cotangent,
):
    dm = Dims(mesh, *tokens.shape, up_weight.shape[1])
    tokT = jnp.transpose(tokens, (0, 2, 1))
    cotT = jnp.transpose(cotangent, (0, 2, 1))
    bcol = jnp.broadcast_to(input_bias[:, :, None], (2, dm.lw, 128))
    xT, xO, qT, kv, segg, ctxr, lse, ctxT, cotT, ubH, upH, downH, woF = run_forward(
        dm, tokT, segment_ids, input_weight, bcol, up_bias[None], cotT, up_weight, down_weight, output_weight
    )
    vec = jnp.stack(
        [output_bias, first_gain, first_shift, down_bias, second_gain, second_shift, output_bias, output_bias]
    )
    loT, doT, frT, dG, uG, oG, sv = run_middle(
        dm, ctxT, xO, cotT, woF.reshape(dm.d, dm.d), upH, downH.reshape(dm.hid, dm.d), ubH, vec
    )
    tgT, wF, fu, fd, fo, svF, bvF, *_ = run_backward(
        dm, qT, kv, segg, lse, ctxr, doT, xT, input_weight, frT, uG, dG.reshape(dm.z, dm.hf, dm.d),
        oG.reshape(dm.z, dm.lw, dm.ol), sv,
    )
    up_bias_grad = lax.dynamic_index_in_dim(
        svF[6:10].reshape(2, dm.z, dm.hf), lax.axis_index("tensor"), 1, False
    ).reshape(dm.ff)
    return (
        jnp.transpose(loT, (0, 2, 1)),
        jnp.transpose(tgT, (0, 2, 1)),
        jnp.transpose(wF.reshape(3, dm.lw, dm.d), (0, 2, 1)).astype(f32),
        bvF[:2, : dm.lw],
        fo.astype(f32),
        svF[5],
        svF[3],
        svF[4],
        fu.astype(f32),
        up_bias_grad,
        fd.astype(f32),
        svF[2],
        svF[0],
        svF[1],
    )


def solution(mesh):
    rows = P("dp", "blk", "tensor")
    placed = (
        rows, P("dp", "blk"), P(None, None, "tensor"), P(None, "tensor"), P("tensor", None), P(), P(), P(),
        P(None, "tensor"), P("tensor"), P("tensor", None), P(), P(), P(), rows,
    )
    results = (
        rows, rows, P(None, None, "tensor"), P(None, "tensor"), P("tensor", None), P(), P(), P(),
        P(None, "tensor"), P("tensor"), P("tensor", None), P(), P(), P(),
    )
    return jax.shard_map(
        functools.partial(shards, mesh), mesh=mesh, in_specs=placed, out_specs=results, check_vma=False
    )
```

```python
import functools

import jax
import jax.numpy as jnp
from jax import lax
from jax.experimental import pallas as pl
from jax.experimental.pallas import tpu as pltpu
from jax.sharding import PartitionSpec as P

HEAD_DIM = 64
EPS = 1e-12
MASKED = -1e30
MESH = pl.DeviceIdType.MESH
bf16 = jnp.bfloat16
f32 = jnp.float32
VMEM_LIMIT = 60 * 2**20


def dot(a, b, ca, cb):
    return lax.dot_general(a, b, (((ca,), (cb,)), ((), ())), preferred_element_type=f32)


def aligned(index, size):
    return pl.multiple_of(index * size, size)


def cut(index, size):
    return pl.ds(aligned(index, size), size)


class Refs:
    def __init__(self, names, refs):
        for name, ref in zip(names, refs, strict=True):
            setattr(self, name, ref)


class Sems:
    def __init__(self, ref=None):
        self.ref = ref
        self.used = 0

    def take(self, count):
        first = self.used
        self.used += count
        return first


class Swap:
    def __init__(self, sems, axis, n, src, dst, xor=False, stride=1):
        self.sems, self.axis, self.n, self.src, self.dst, self.xor = sems, axis, n, src, dst, xor
        self.stride = stride
        self.me = lax.axis_index(axis)
        self.send, self.recv = sems.take(n), sems.take(n)

    def to(self, k):
        return self.me ^ (k * self.stride) if self.xor else lax.rem(self.me + k, self.n)

    def source(self, k):
        return self.me ^ (k * self.stride) if self.xor else lax.rem(self.me + self.n - k, self.n)

    def copy(self, k, dst_index):
        return pltpu.make_async_remote_copy(
            self.src(self.to(k)),
            self.dst(dst_index),
            self.sems.ref.at[self.send + k],
            self.sems.ref.at[self.recv + k],
            device_id={self.axis: self.to(k)},
            device_id_type=MESH,
        )

    def start_one(self, k):
        self.copy(k, self.me).start()

    def start(self):
        each(1, self.n, self.start_one)

    def wait(self, k):
        self.copy(k, self.source(k)).wait_recv()

    def wait_all(self):
        each(1, self.n, self.wait)

    def done(self):
        each(1, self.n, lambda k: self.copy(k, self.me).wait_send())


def each(low, high, body):
    if high - low <= 4:
        for k in range(low, high):
            body(k)
    else:

        def step(k, carry):
            body(k)
            return carry

        lax.fori_loop(low, high, step, 0)


class Line:
    def __init__(self, sems, n, view, own):
        self.sems, self.n, self.view, self.own = sems, n, view, own
        self.t = lax.axis_index("tensor")
        self.recv, self.right, self.left = sems.take(n), sems.take(n), sems.take(n)

    def copy(self, chunk, right, k):
        return pltpu.make_async_remote_copy(
            self.own if k == 0 else self.view(chunk),
            self.view(chunk),
            self.sems.ref.at[(self.right if right else self.left) + k],
            self.sems.ref.at[self.recv + chunk],
            device_id={"tensor": self.t + 1 if right else self.t - 1},
            device_id_type=MESH,
        )

    def start(self):
        t, n = self.t, self.n
        pl.when(t < n - 1)(lambda: self.copy(t, True, 0).start())
        pl.when(t > 0)(lambda: self.copy(t, False, 0).start())

    def step(self, k):
        t, n = self.t, self.n

        @pl.when(t >= k)
        def _():
            self.copy(t - k, True, k).wait_recv()
            pl.when(t < n - 1)(lambda: self.copy(t - k, True, k).start())

        @pl.when(t + k < n)
        def _():
            self.copy(t + k, False, k).wait_recv()
            pl.when(t > 0)(lambda: self.copy(t + k, False, k).start())

    def done(self):
        t, n = self.t, self.n
        for k in range(n):
            pl.when((t >= k) & (t < n - 1))(lambda k=k: self.copy(t - k, True, k).wait_send())
            pl.when((t + k < n) & (t > 0))(lambda k=k: self.copy(t + k, False, k).wait_send())


class Plane:
    def __init__(self, sems, n, view, own):
        self.sems, self.n, self.view, self.own = sems, n, view, own
        self.b = lax.axis_index("blk")
        self.send, self.recv = sems.take(2 * n), sems.take(2 * n)

    def copy(self, k, half, origin, to, own):
        return pltpu.make_async_remote_copy(
            self.own(half) if own else self.view(origin, half),
            self.view(origin, half),
            self.sems.ref.at[self.send + 2 * k + half],
            self.sems.ref.at[self.recv + 2 * k + half],
            device_id={"blk": to},
            device_id_type=MESH,
        )

    def ours(self, k, half):
        return self.copy(k, half, self.b, self.b ^ k, True)

    def passed(self, half):
        origin, to = (self.b ^ 1, self.b ^ 2) if half == 0 else (self.b ^ 2, self.b ^ 1)
        return self.copy(3, half, origin, to, False)

    def start(self):
        if self.n == 4:
            for k, half in ((1, 0), (2, 1), (1, 1), (2, 0)):
                self.ours(k, half).start()
        else:

            def go(k):
                self.ours(k, 0).start()
                self.ours(k, 1).start()

            each(1, self.n, go)

    def landed(self, k, half):
        self.copy(k, half, self.b ^ k, self.b ^ k, True).wait_recv()

    def forward(self):
        if self.n == 4:
            self.landed(1, 0)
            self.passed(0).start()
            self.landed(2, 1)
            self.passed(1).start()

    def wait(self, k):
        if self.n != 4:
            self.landed(k, 0)
            self.landed(k, 1)
        elif k == 1:
            self.landed(1, 1)
        elif k == 2:
            self.landed(2, 0)
        else:
            self.landed(3, 0)
            self.landed(3, 1)

    def wait_all(self):
        each(1, self.n, self.wait)

    def done(self):
        if self.n == 4:
            for k, half in ((1, 0), (2, 1), (1, 1), (2, 0)):
                self.ours(k, half).wait_send()
            self.passed(0).wait_send()
            self.passed(1).wait_send()
        else:

            def go(k):
                self.ours(k, 0).wait_send()
                self.ours(k, 1).wait_send()

            each(1, self.n, go)


class Spread:
    def __init__(self, sems, n, view):
        self.sems, self.n, self.view = sems, n, view
        self.b, self.t = lax.axis_index("blk"), lax.axis_index("tensor")
        self.send, self.recv = sems.take(8 * n), sems.take(8 * n)

    def copy(self, s, k, half, origin, to):
        ref = self.view(s, origin, half)
        return pltpu.make_async_remote_copy(
            ref,
            ref,
            self.sems.ref.at[self.send + 8 * s + 2 * k + half],
            self.sems.ref.at[self.recv + 8 * s + 2 * k + half],
            device_id={"blk": to},
            device_id_type=MESH,
        )

    def ours(self, s):
        return [self.copy(s, k, half, self.b, self.b ^ k) for k, half in ((1, 0), (2, 1), (1, 1), (2, 0))]

    def passed(self, s, half):
        near, far = (1, 2) if half == 0 else (2, 1)
        return self.copy(s, 3, half, self.b ^ near, self.b ^ far)

    def landed(self, s, k, half):
        self.copy(s, k, half, self.b ^ k, self.b ^ k).wait_recv()

    def around(self, k, body):
        pl.when(self.t >= k)(lambda: body(self.t - k))
        pl.when(self.t + k < self.n)(lambda: body(self.t + k))

    def start(self, k):
        def body(s):
            for copy in self.ours(s):
                copy.start()

        self.around(k, body)

    def forward(self, k):
        def body(s):
            self.landed(s, 1, 0)
            self.passed(s, 0).start()
            self.landed(s, 2, 1)
            self.passed(s, 1).start()

        self.around(k, body)

    def wait_all(self):
        def body(s):
            self.landed(s, 1, 1)
            self.landed(s, 2, 0)
            self.landed(s, 3, 0)
            self.landed(s, 3, 1)

        for k in range(1, self.n):
            self.around(k, body)

    def done(self):
        def body(s):
            for copy in (*self.ours(s), self.passed(s, 0), self.passed(s, 1)):
                copy.wait_send()

        for k in range(1, self.n):
            self.around(k, body)


class Fold:
    def __init__(self, sems, part, relay, inbox):
        self.sems, self.part, self.relay, self.inbox = sems, part, relay, inbox
        self.b = lax.axis_index("blk")
        self.send, self.recv = sems.take(6), sems.take(6)

    def copy(self, n, src, dst, k):
        return pltpu.make_async_remote_copy(
            src,
            dst,
            self.sems.ref.at[self.send + n],
            self.sems.ref.at[self.recv + n],
            device_id={"blk": self.b ^ k},
            device_id_type=MESH,
        )

    def across(self, half):
        return self.copy(half, self.part(self.b ^ 3, half), self.relay(half), half + 1)

    def near(self, half):
        return self.copy(2 + half, self.part(self.b ^ (half + 1), half), self.inbox(half), half + 1)

    def folded(self, half):
        return self.copy(4 + half, self.relay(half), self.inbox(2 + half), 2 - half)

    def fold(self, half):
        self.across(half).wait_recv()
        part, relay = self.part(self.b ^ (2 - half), half), self.relay(half)
        relay[...] = (part[...].astype(f32) + relay[...].astype(f32)).astype(bf16)
        self.folded(half).start()

    def wait(self, half):
        self.near(half).wait_recv()
        self.folded(half).wait_recv()

    def received(self, half):
        return self.inbox(half)[...].astype(f32) + self.inbox(2 + half)[...].astype(f32)

    def done(self):
        for half in (0, 1):
            for transfer in (self.across, self.near, self.folded):
                transfer(half).wait_send()


class LineFold:
    def __init__(self, sems, n, part, relay):
        self.sems, self.n, self.part, self.relay = sems, n, part, relay
        self.t = lax.axis_index("tensor")
        self.send, self.recv = sems.take(n), sems.take(n + 1)

    def copy(self, j, right, fresh):
        to = self.t + 1 if right else self.t - 1
        slot = j if right else jnp.where(j == to, self.n, j)
        return pltpu.make_async_remote_copy(
            self.part(j) if fresh else self.relay(j),
            self.relay(slot),
            self.sems.ref.at[self.send + j],
            self.sems.ref.at[self.recv + slot],
            device_id={"tensor": to},
            device_id_type=MESH,
        )

    def landed(self, slot):
        pltpu.make_async_remote_copy(
            self.relay(slot),
            self.relay(slot),
            self.sems.ref.at[self.send],
            self.sems.ref.at[self.recv + slot],
            device_id={"tensor": lax.rem(self.t + 1, self.n)},
            device_id_type=MESH,
        ).wait_recv()

    def start(self):
        n = self.n

        @pl.when(self.t == 0)
        def _():
            for j in range(n - 1, 0, -1):
                self.copy(j, True, True).start()

        @pl.when(self.t == n - 1)
        def _():
            for j in range(n - 1):
                self.copy(j, False, True).start()

    def pass_on(self, j, right):
        self.landed(j)
        relay, part = self.relay(j), self.part(j)
        relay[...] = (relay[...].astype(f32) + part[...].astype(f32)).astype(bf16)
        self.copy(j, right, False).start()

    def step(self, m):
        back = self.n - 1 - self.t
        pl.when((self.t >= 1) & (self.t <= m) & (back >= 1))(lambda: self.pass_on(self.n - 1 + self.t - m, True))
        pl.when((back >= 1) & (back <= m) & (self.t >= 1))(lambda: self.pass_on(m - back, False))

    def finish(self, store):
        @pl.when(self.t > 0)
        def _():
            self.landed(self.t)
            store(self.relay(self.t))

        @pl.when(self.t < self.n - 1)
        def _():
            self.landed(self.n)
            store(self.relay(self.n))

    def done(self):
        for j in range(self.n):
            pl.when(self.t < j)(lambda j=j: self.copy(j, True, False).wait_send())
            pl.when(self.t > j)(lambda j=j: self.copy(j, False, False).wait_send())


class Dims:
    def __init__(self, mesh, rows, tok, width, ff):
        self.z, self.nb, self.nc = mesh.shape["tensor"], mesh.shape["blk"], mesh.shape["dp"]
        self.rows, self.tok, self.lw, self.ff = rows, tok, width, ff
        self.d = width * self.z
        self.heads = width // HEAD_DIM
        self.pt = tok // self.z
        self.own = rows * self.pt
        self.hf = ff // 2
        self.hid = self.hf * self.z
        self.uq, self.dq, self.oq, self.ol = self.d // 4, self.hf // 4, width // 4, self.d // 2
        self.wr = 3 * width


def enter(dm, dp=True, blk=True, tensor=True):
    barrier = pltpu.get_barrier_semaphore()
    count = 0
    for axis, n, wanted in (("dp", dm.nc, dp), ("blk", dm.nb, blk), ("tensor", dm.z, tensor)):
        if not wanted:
            continue
        me = lax.axis_index(axis)

        def greet(k, axis=axis, n=n, me=me):
            pl.semaphore_signal(barrier, inc=1, device_id={axis: lax.rem(me + k, n)}, device_id_type=MESH)

        each(1, n, greet)
        count += n - 1
    pl.semaphore_wait(barrier, count)


def mask_bias(segg, r, key_block, own_block, tok):
    key_row = segg[key_block, r : r + 1, :]
    column = jnp.transpose(jnp.broadcast_to(key_row.astype(f32), (128, tok)))
    wide = jnp.concatenate([column] * (tok // 128), axis=1)
    query_row = segg[own_block, r : r + 1, :].astype(f32)
    return jnp.where(wide == query_row, 0.0, MASKED)


def layer_kernel(dm, names, *refs):
    R = Refs(names, refs)
    t, b, c = lax.axis_index("tensor"), lax.axis_index("blk"), lax.axis_index("dp")
    q = lax.rem(b, 4)
    sems = Sems(R.sems)
    rows, lw, pt, own, d, tok, hf, z = dm.rows, dm.lw, dm.pt, dm.own, dm.d, dm.tok, dm.hf, dm.z
    small = dm.nb == 4
    mine, other = cut(c, own), cut(1 - c, own)
    quarter = lambda i: lax.rem(i, 4)
    half_d, half_z, half_h = d // 2, z // 2, dm.hid // 2
    split_u, split_o = dm.uq // 2, 128

    def z_swap(src, dst):
        return Swap(sems, "tensor", z, src, dst)

    def pair(src, dst):
        return Swap(sems, "dp", dm.nc, src, dst)

    token_lines = [
        Line(sems, z, lambda i, r=r: R.xT.at[r, cut(i, lw), :], R.xT.at[r, cut(t, lw), :]) for r in range(rows)
    ]
    seg_swap = Swap(sems, "blk", dm.nb, lambda to: R.segg.at[b], lambda i: R.segg.at[i], xor=True)
    ub_swap = z_swap(lambda to: R.ub8, lambda i: R.ubH.at[:, cut(i, hf)])
    up_own = R.up.at[cut(q, dm.uq), cut(c, hf)]
    down_own = R.down.at[pl.ds(pl.multiple_of(hf * c + dm.dq * q, dm.dq), dm.dq), :]
    wo_own = R.wo.at[:, cut(c, dm.ol)]

    def up_piece(i):
        return R.upH.at[cut(q, dm.uq), cut(i, hf)]

    def down_piece(i):
        return R.downH.at[i, cut(q, dm.dq), :]

    def wo_piece(i):
        return R.woF.at[i, :, cut(c, dm.ol)]

    up_line = Line(sems, z, up_piece, up_own)
    down_line = Line(sems, z, down_piece, down_own)
    wo_line = Line(sems, z, wo_piece, wo_own)

    def up_view(s, i, half):
        start = pl.multiple_of(dm.uq * quarter(i) + split_u * half, split_u)
        return R.upH.at[pl.ds(start, split_u), cut(s, hf)]

    def down_view(s, i, half):
        return R.downH.at[s, cut(quarter(i), dm.dq), pl.ds(half_d * half, half_d)]

    up_spread, down_spread = Spread(sems, z, up_view), Spread(sems, z, down_view)
    wo_pair = pair(lambda to: R.woF.at[:, :, cut(c, dm.ol)], lambda i: R.woF.at[:, :, cut(i, dm.ol)])
    cot_swap = z_swap(lambda to: R.cot.at[:, :, cut(to, pt)], lambda i: R.cotT.at[:, cut(i, lw), :])
    kv_planes = [
        Plane(
            sems,
            dm.nb,
            lambda i, half, r=r: R.kv.at[r, i, pl.ds(lw * half, lw), :],
            lambda half, r=r: R.kv.at[r, b, pl.ds(lw * half, lw), :],
        )
        for r in range(rows)
    ]
    ctx_swaps = [
        z_swap(lambda to, r=r: R.ctxs.at[r, :, cut(to, pt)], lambda i, r=r: R.ctxT.at[r, cut(i, lw), :])
        for r in range(rows)
    ]
    hl_pair = pair(lambda to: R.hl.at[mine], lambda i: R.hl.at[cut(i, own)])
    feed_pair = pair(lambda to: R.fs_s.at[0], lambda i: R.fs_r.at[0])
    fg_pair = pair(lambda to: R.fgf.at[mine], lambda i: R.fgf.at[cut(i, own)])
    part_pair = pair(lambda to: R.fs_s.at[1], lambda i: R.fs_r.at[1])
    og_pair = pair(lambda to: R.og_s, lambda i: R.og_r)
    out_swaps = [
        z_swap(lambda to, r=r: R.outT.at[r, cut(to, lw), :], lambda i, r=r: R.loT.at[r, :, cut(i, pt)])
        for r in range(rows)
    ]
    grad_swaps = [
        z_swap(lambda to, r=r: R.cgT.at[r, cut(to, lw), :], lambda i, r=r: R.doT.at[r, :, cut(i, pt)])
        for r in range(rows)
    ]

    def u_part(i, half):
        return R.uG.at[cut(quarter(i), dm.uq), pl.ds(half_h * half, half_h)]

    def d_part(i, half):
        return R.dG.at[pl.ds(half_z * half, half_z), cut(quarter(i), dm.dq), :]

    def o_part(i, half):
        return R.oG.at[pl.ds(half_z * half, half_z), cut(quarter(i), dm.oq), :]

    parts = (u_part, d_part, o_part)
    first_stage = tuple(
        Fold(sems, part, lambda half, got=got: got.at[4 + half], lambda n, got=got: got.at[n])
        for part, got in zip(parts, (R.ur, R.dr, R.orr), strict=True)
    )
    second_stage = (
        LineFold(sems, z, lambda j: R.uG.at[cut(q, dm.uq), cut(j, hf)], lambda j: R.u2.at[j]),
        LineFold(sems, z, lambda j: R.dG.at[j, cut(q, dm.dq), :], lambda j: R.d2.at[j]),
        LineFold(sems, z, lambda j: R.oG.at[j, cut(q, dm.oq), :], lambda j: R.o2.at[j]),
    )
    groups = dm.nb // 4
    piece_refs, group_refs = (R.uP, R.dP, R.oP), (R.gu, R.gd, R.go)
    group_stage = tuple(
        Swap(sems, "blk", groups, lambda to, ref=ref: ref, lambda i, got=got: got.at[i // 4], True, 4)
        for ref, got in zip(piece_refs, group_refs, strict=True)
    )

    def fu_view(i, half):
        return R.fu.at[pl.ds(pl.multiple_of(dm.uq * quarter(i) + split_u * half, split_u), split_u), cut(c, hf)]

    def fd_view(i, half):
        start = pl.multiple_of(hf * c + dm.dq * quarter(i), dm.dq)
        return R.fd.at[pl.ds(start, dm.dq), pl.ds(half_d * half, half_d)]

    def fo_view(i, half):
        start = pl.multiple_of(dm.ol * c + split_o * half, 128)
        return R.fo.at[cut(quarter(i), dm.oq), pl.ds(start, dm.ol - split_o if half else split_o)]

    piece_halves = (
        lambda half: R.uP.at[pl.ds(split_u * half, split_u), :],
        lambda half: R.dP.at[:, pl.ds(half_d * half, half_d)],
        lambda half: R.oP.at[:, pl.ds(split_o * half, dm.ol - split_o if half else split_o)],
    )
    third_stage = tuple(
        Plane(sems, 4, view, piece) for view, piece in zip((fu_view, fd_view, fo_view), piece_halves, strict=True)
    )
    place = (
        R.fu.at[cut(q, dm.uq), cut(c, hf)],
        R.fd.at[pl.ds(pl.multiple_of(hf * c + dm.dq * q, dm.dq), dm.dq), :],
        R.fo.at[cut(q, dm.oq), cut(c, dm.ol)],
    )
    place_copies = [
        pltpu.make_async_copy(src, dst, R.local.at[4 + n])
        for n, (src, dst) in enumerate(zip(piece_refs, place, strict=True))
    ]
    last_stage = (
        pair(lambda to: R.fu.at[:, cut(c, hf)], lambda i: R.fu.at[:, cut(i, hf)]),
        pair(lambda to: R.fd.at[cut(c, hf), :], lambda i: R.fd.at[cut(i, hf), :]),
        pair(lambda to: R.fo.at[:, cut(c, dm.ol)], lambda i: R.fo.at[:, cut(i, dm.ol)]),
    )
    vec_pair = pair(lambda to: R.sv, lambda i: R.vp)
    vec_blk = Swap(sems, "blk", dm.nb, lambda to: R.vs.at[0], lambda i: R.vb.at[i], xor=True)
    vec_z = z_swap(lambda to: R.vs.at[1], lambda i: R.vz.at[i])
    bv_pair = pair(lambda to: R.bv_s.at[0], lambda i: R.bvp)
    bv_blk = Swap(sems, "blk", dm.nb, lambda to: R.bv_s.at[1], lambda i: R.bvb.at[i], xor=True)
    if small:
        kv_folds = [
            Fold(
                sems,
                lambda i, half, r=r: R.kv.at[r, i, pl.ds(lw * half, lw), :],
                lambda half, r=r: R.dkv_r.at[r, 2, pl.ds(lw * half, lw), :],
                lambda n, r=r: R.dkv_r.at[r, n // 2, pl.ds(lw * (n % 2), lw), :],
            )
            for r in range(rows)
        ]
    else:
        kv_folds = [
            Swap(sems, "blk", dm.nb, lambda to, r=r: R.kv.at[r, to], lambda i, r=r: R.dkv_r.at[r, i], xor=True)
            for r in range(rows)
        ]
    tok_folds = [
        LineFold(sems, z, lambda j, r=r: R.tp_s.at[r, cut(j, lw), :], lambda j, r=r: R.tp_r.at[r, j])
        for r in range(rows)
    ]
    half_w, wq_r, wq_l = dm.wr // 2, dm.wr // 4, d // 2
    w_pair = pair(lambda to: R.wT.at[cut(to, half_w), :], lambda i: R.wR)

    def w_at(i):
        return lax.div(quarter(i), 2), lax.rem(i, 2)

    w_blk = Swap(
        sems, "blk", 4,
        lambda to: R.w1.at[cut(w_at(to)[0], wq_r), cut(w_at(to)[1], wq_l)],
        lambda i: R.wr.at[quarter(i)], xor=True,
    )
    w_split = 80

    def wf_view(i, half):
        start = pl.multiple_of(half_w * c + wq_r * w_at(i)[0] + w_split * half, 16)
        return R.wF.at[pl.ds(start, wq_r - w_split if half else w_split), cut(w_at(i)[1], wq_l)]

    start_r, start_l = w_at(b)
    w_group = Swap(sems, "blk", groups, lambda to: R.wP, lambda i: R.gw.at[i // 4], True, 4)
    w_plane = Plane(
        sems, 4, wf_view, lambda half: R.wP.at[pl.ds(w_split * half, wq_r - w_split if half else w_split), :]
    )
    w_place = pltpu.make_async_copy(
        R.wP,
        R.wF.at[pl.ds(pl.multiple_of(half_w * c + wq_r * start_r, 16), wq_r), cut(start_l, wq_l)],
        R.local.at[7],
    )
    w_last = pair(lambda to: R.wF.at[cut(c, half_w), :], lambda i: R.wF.at[cut(i, half_w), :])

    def sync(src, dst):
        copy = pltpu.make_async_copy(src, dst, R.local.at[3])
        copy.start()
        copy.wait()

    def chunk_of(r, block):
        if small:
            return R.kv.at[r, block]
        sync(R.kv.at[r, block], R.kvc)
        return R.kvc

    def project(r):
        y = dot(R.w[...].reshape(dm.wr, d), R.xT[r], 1, 0)
        R.qT[r] = (y[:lw] + R.bcol[0][:, :1]).astype(bf16) * bf16(HEAD_DIM**-0.5)
        chunk = R.kv.at[r, b] if small else R.kvc
        chunk[0:lw, :] = y[lw : 2 * lw].astype(bf16)
        chunk[lw : 2 * lw, :] = (y[2 * lw :] + R.bcol[1][:, :1]).astype(bf16)
        if not small:
            sync(R.kvc, R.kv.at[r, b])
        for h in range(dm.heads):
            R.m_s[r, h] = jnp.full((8, tok), MASKED, f32)
            R.l_s[r, h] = jnp.zeros((8, tok), f32)
            R.acc[r, h] = jnp.zeros((HEAD_DIM, tok), f32)
        kv_planes[r].start()

    def attend(r, block):
        bias = mask_bias(R.segg, r, block, b, tok)
        chunk = chunk_of(r, block)
        for h in range(dm.heads):
            k = chunk[pl.ds(HEAD_DIM * h, HEAD_DIM), :]
            v = chunk[pl.ds(lw + HEAD_DIM * h, HEAD_DIM), :]
            s = dot(k, R.qT[r, pl.ds(HEAD_DIM * h, HEAD_DIM), :], 0, 0) + bias
            old = R.m_s[r, h, :1]
            new = jnp.maximum(old, jnp.max(s, 0, keepdims=True))
            p = jnp.exp(s - new)
            scale = jnp.exp(old - new)
            R.l_s[r, h, :1] = R.l_s[r, h, :1] * scale + jnp.sum(p, 0, keepdims=True)
            R.m_s[r, h, :1] = new
            R.acc[r, h] = R.acc[r, h] * scale + dot(v, p.astype(bf16), 1, 0)

    def attend_near(r, k):
        if small:
            kv_planes[r].wait(k)
            attend(r, b ^ k)

    def attend_rest(r):
        if not small:

            def body(k):
                kv_planes[r].wait(k)
                attend(r, b ^ k)

            each(1, dm.nb, body)

    def finish(r):
        for h in range(dm.heads):
            denominator = R.l_s[r, h, :1]
            ctx = R.acc[r, h] / denominator
            R.ctxr[r, pl.ds(HEAD_DIM * h, HEAD_DIM), :] = ctx
            R.ctxs[r, pl.ds(HEAD_DIM * h, HEAD_DIM), :] = ctx.astype(bf16)
            R.lse[r, h : h + 1, :] = R.m_s[r, h, :1] + jnp.log(denominator)
        R.ctxT[r, cut(t, lw), :] = R.ctxs[r, :, cut(t, pt)]
        ctx_swaps[r].start()

    enter(dm)
    for r in range(rows):
        R.xT[r, cut(t, lw), :] = R.tok[r]
    token_lines[0].start()
    up_line.start()
    weight_copies = [
        pltpu.make_async_copy(src, dst, R.local.at[n])
        for n, (src, dst) in enumerate(
            (
                (R.up.at[:, cut(c, hf)], R.upH.at[:, cut(t, hf)]),
                (R.down.at[cut(c, hf), :], R.downH.at[t]),
                (wo_own, wo_piece(t)),
            )
        )
    ]
    for copy in weight_copies:
        copy.start()
    for r in range(rows):
        R.cotT[r, cut(t, lw), :] = R.cot[r, :, cut(t, pt)]
    for m in range(3):
        R.wN[m] = jnp.transpose(R.w[m])
    R.segg[b] = jnp.zeros((8, tok), jnp.int32)
    R.segg[b, 0:rows, :] = R.seg[...]
    seg_swap.start()
    for n in range(7):
        R.vec[n, :] = getattr(R, f"vec{n}")[...]
    for n in range(2):
        R.bcol[n] = jnp.transpose(jnp.broadcast_to(R.ib[n : n + 1, :], (128, lw)))
    R.ub8[...] = jnp.broadcast_to(R.vec[6:7, cut(c, hf)], (8, hf))
    R.ubH[:, cut(t, hf)] = R.ub8[...]
    ub_swap.start()

    token_lines[0].step(1)
    up_line.step(1)
    up_spread.start(1)
    token_lines[0].step(2)
    token_lines[1].start()
    up_line.step(2)
    up_spread.start(2)
    token_lines[0].step(3)
    project(0)
    up_line.step(3)
    up_spread.start(3)
    up_spread.forward(1)
    token_lines[1].step(1)
    wo_line.start()
    seg_swap.wait_all()
    attend(0, b)
    up_spread.forward(2)
    token_lines[1].step(2)
    down_line.start()
    kv_planes[0].forward()
    up_spread.forward(3)
    wo_line.step(1)
    token_lines[1].step(3)
    project(1)
    wo_line.step(2)
    down_line.step(1)
    down_spread.start(1)
    attend(1, b)
    wo_line.step(3)
    for copy in weight_copies:
        copy.wait()
    wo_pair.start()
    attend_near(0, 1)
    down_line.step(2)
    down_spread.start(2)
    attend_near(0, 2)
    down_line.step(3)
    down_spread.start(3)
    attend_near(0, 3)
    attend_rest(0)
    finish(0)
    kv_planes[1].forward()
    attend_near(1, 1)
    down_spread.forward(1)
    attend_near(1, 2)
    down_spread.forward(2)
    attend_near(1, 3)
    attend_rest(1)
    finish(1)
    cot_swap.start()
    down_spread.forward(3)

    out_b, g1, s1, down_b, g2, s2 = (R.vec[n : n + 1, :] for n in range(6))

    def stats(x):
        center = x - jnp.mean(x, -1, keepdims=True)
        inverse = lax.rsqrt(jnp.mean(center * center, -1, keepdims=True) + EPS)
        return center * inverse, inverse

    def norm_back(g, gain, zn, inverse):
        e = g * gain
        return (e - jnp.mean(e, -1, keepdims=True) - zn * jnp.mean(e * zn, -1, keepdims=True)) * inverse

    def total(x):
        return jnp.sum(x, 0, keepdims=True)

    blocks = dm.hid // tok

    inverse1 = []
    wo_pair.wait_all()
    for r in range(rows):
        ctx_swaps[r].wait_all()
        attended = dot(R.ctxT[r], R.woF[...].reshape(d, d), 0, 0) + out_b
        zn, inv = stats(jnp.transpose(R.xT[r, :, cut(t, pt)].astype(f32)) + attended)
        inverse1.append(inv)
        R.z1_s[pl.ds(pt * r, pt), :] = zn
        R.hl[pl.ds(pl.multiple_of(own * c + pt * r, pt), pt), :] = (zn * g1 + s1).astype(bf16)
    hl_pair.start()
    ub_swap.wait_all()

    def expand(core):
        part = cut(core, own)
        for n in range(blocks):
            cols = pl.ds(tok * n, tok)
            v = dot(R.hl[part, :], R.upH[:, cols], 1, 0) + R.ubH[:1, cols]
            phi = 0.5 + 0.5 * lax.erf(v * (0.5**0.5))
            R.act[part, cols] = (v * phi).astype(bf16)
            R.pool[cut(2 * n + core, own), :] = phi + v * (jnp.exp(-0.5 * v * v) * 0.3989422804014327)

    up_spread.wait_all()
    expand(c)
    hl_pair.wait_all()
    expand(1 - c)
    down_spread.wait_all()
    down_w = R.downH[...].reshape(dm.hid, d)
    R.fs_s[0] = dot(R.act[other, :], down_w, 1, 0).astype(bf16)
    feed_pair.start()
    feed = dot(R.act[mine, :], down_w, 1, 0) + down_b
    cot_swap.wait_all()
    g = jnp.concatenate([jnp.transpose(R.cotT[r].astype(f32)) for r in range(rows)], 0)
    feed_pair.wait_all()
    hidden = R.z1_s[...] * g1 + s1
    z2, inverse2 = stats(hidden + (feed + R.fs_r[0].astype(f32)))
    resid = norm_back(g, g2, z2, inverse2)
    R.srg_s[...] = resid
    low = resid.astype(bf16)
    R.fgf[mine, :] = low
    fg_pair.start()
    out = z2 * g2 + s2
    R.sv[...] = jnp.zeros_like(R.sv)
    R.sv[0:1, :] = total(g * z2)
    R.sv[1:2, :] = total(g)
    R.sv[2:3, :] = total(low.astype(f32))

    def contract(core):
        part = cut(core, own)
        for n in range(blocks):
            cols = pl.ds(tok * n, tok)
            grad = dot(R.fgf[part, :], R.downH[...].reshape(dm.hid, d)[tok * n : tok * (n + 1)], 1, 1)
            R.bg[part, cols] = (grad * R.pool[cut(2 * n + core, own), :]).astype(bf16)

    contract(c)
    fg_pair.wait_all()
    contract(1 - c)
    R.fs_s[1] = dot(R.bg[other, :], R.upH[...], 1, 1).astype(bf16)
    part_pair.start()
    part = dot(R.bg[mine, :], R.upH[...], 1, 1)
    for r in range(rows):
        R.outT[r] = jnp.transpose(out[pt * r : pt * (r + 1)]).astype(bf16)
        R.loT[r, :, cut(t, pt)] = R.outT[r, cut(t, lw), :]
        out_swaps[r].start()

    def send_first(n):
        for half in (0, 1):
            first_stage[n].across(half).start()
        for half in (0, 1):
            first_stage[n].near(half).start()

    for n in range(z):
        R.dG[n] = dot(R.act[:, pl.ds(hf * n, hf)], R.fgf[...], 0, 0).astype(bf16)
    send_first(1)
    part_pair.wait_all()
    hidden_grad = R.srg_s[...] + (part + R.fs_r[1].astype(f32))
    z1 = R.z1_s[...]
    first = norm_back(hidden_grad, g1, z1, jnp.concatenate(inverse1, 0))
    low = first.astype(bf16)
    for r in range(rows):
        R.cgT[r] = dot(R.woF[...].reshape(d, d), low[pt * r : pt * (r + 1)], 1, 1).astype(bf16)
        R.doT[r, :, cut(t, pt)] = R.cgT[r, cut(t, lw), :]
        grad_swaps[r].start()
        R.frT[r] = jnp.transpose(first[pt * r : pt * (r + 1)])
    R.sv[3:4, :] = total(hidden_grad * z1)
    R.sv[4:5, :] = total(hidden_grad)
    R.sv[5:6, :] = total(low.astype(f32))
    out_grad = sum(dot(R.ctxT[r], low[pt * r : pt * (r + 1)], 1, 0) for r in range(rows))
    left = out_grad[:, : dm.ol].reshape(z, lw, dm.ol)
    right = out_grad[:, dm.ol :].reshape(z, lw, dm.ol)
    R.oG[...] = jnp.where(c == 0, left, right).astype(bf16)
    R.og_s[...] = jnp.where(c == 0, right, left).astype(bf16)
    og_pair.start()
    for n in range(blocks):
        cols = pl.ds(tok * n, tok)
        R.uG[:, cols] = dot(R.hl[...], R.bg[:, cols], 0, 0).astype(bf16)
    for n in range(z):
        R.sv[pl.ds(6 + 2 * c + n // 2, 1), pl.ds(hf * (n % 2), hf)] = total(
            R.bg[:, pl.ds(hf * n, hf)].astype(f32)
        )
    vec_pair.start()
    first_stage[1].fold(0)
    first_stage[1].fold(1)
    og_pair.wait_all()
    R.oG[...] = (R.oG[...].astype(f32) + R.og_r[...].astype(f32)).astype(bf16)

    for line in (*token_lines, up_line, down_line, wo_line):
        line.done()
    for r in range(rows):
        kv_planes[r].done()

    def store_chunk(r, block):
        if not small:
            sync(R.kvc, R.kv.at[r, block])

    def own_kv(r, at, size):
        return R.pool.at[pl.ds(2 * lw * r + at, size), :]

    def dq_at(r, at, size):
        return R.pool.at[pl.ds(2 * lw * rows + lw * r + at, size), :]

    def prepare(r):
        grad_swaps[r].wait_all()
        for h in range(dm.heads):
            feats = pl.ds(HEAD_DIM * h, HEAD_DIM)
            R.delta[r, h : h + 1, :] = jnp.sum(R.doT[r, feats, :].astype(f32) * R.ctxr[r, feats, :], 0, keepdims=True)
        dq_at(r, 0, lw)[...] = jnp.zeros((lw, tok), f32)

    def attend_back(r, block, keep):
        bias = mask_bias(R.segg, r, block, b, tok)
        chunk = chunk_of(r, block)
        for h in range(dm.heads):
            feats = pl.ds(HEAD_DIM * h, HEAD_DIM)
            more = pl.ds(lw + HEAD_DIM * h, HEAD_DIM)
            k, v = chunk[feats, :], chunk[more, :]
            qh, do = R.qT[r, feats, :], R.doT[r, feats, :]
            p = jnp.exp(dot(k, qh, 0, 0) + bias - R.lse[r, h : h + 1, :])
            ds = (p * (dot(v, do, 0, 0) - R.delta[r, h : h + 1, :])).astype(bf16)
            dq_at(r, HEAD_DIM * h, HEAD_DIM)[...] += dot(k, ds, 1, 0)
            dk, dv = dot(qh, ds, 1, 1), dot(do, p.astype(bf16), 1, 1)
            if keep:
                own_kv(r, HEAD_DIM * h, HEAD_DIM)[...] = dk
                own_kv(r, lw + HEAD_DIM * h, HEAD_DIM)[...] = dv
            else:
                chunk[feats, :] = dk.astype(bf16)
                chunk[more, :] = dv.astype(bf16)
        if not keep:
            store_chunk(r, block)

    def back_far(r):
        prepare(r)
        if small:
            attend_back(r, b ^ 3, False)
            kv_folds[r].across(0).start()
            kv_folds[r].across(1).start()
        else:

            def body(k):
                attend_back(r, b ^ k, False)
                kv_folds[r].start_one(k)

            each(1, dm.nb, body)

    def back_near(r, half):
        if small:
            attend_back(r, b ^ (half + 1), False)
            kv_folds[r].near(half).start()

    def fold_kv(r):
        if small:
            kv_folds[r].fold(0)
            kv_folds[r].fold(1)

    def project_back(r):
        if small:
            for half in (0, 1):
                kv_folds[r].wait(half)
                own_kv(r, lw * half, lw)[...] += kv_folds[r].received(half)
        else:

            def add(k):
                kv_folds[r].wait(k)
                sync(R.dkv_r.at[r, b ^ k], R.kvc)
                own_kv(r, 0, 2 * lw)[...] += R.kvc[...].astype(f32)

            each(1, dm.nb, add)
        R.low_s[r, 0:lw, :] = (dq_at(r, 0, lw)[...] * HEAD_DIM**-0.5).astype(bf16)
        R.low_s[r, lw:, :] = own_kv(r, 0, 2 * lw)[...].astype(bf16)
        R.tp_s[r] = back_through(R.wN, R.low_s[r], lw).astype(bf16)
        R.tp_s[r, :, cut(t, pt)] = (back_through(R.wN, R.low_s[r, :, cut(t, pt)], lw) + R.frT[r]).astype(bf16)
        tok_folds[r].start()

    def weight_grads(r):
        ones = jnp.ones((16, tok), bf16)
        for n, m in ((0, 0), (1, 2)):
            sums = dot(ones, R.low_s[r, pl.ds(lw * m, lw), :], 1, 1)
            if r == 0:
                R.bv_s[0, n : n + 1, 0:lw] = sums[:1]
            else:
                R.bv_s[0, n : n + 1, 0:lw] += sums[:1]
        grads = dot(R.low_s[r], R.xT[r], 1, 1)
        if r == 0:
            R.w_acc[...] = grads
        else:
            R.w_acc[...] += grads

    def add_up(first, parts, n):
        result = first.astype(f32)
        for k in range(n):
            result = result + parts(k)
        return result

    def fold_first(n):
        first_stage[n].fold(0)
        first_stage[n].fold(1)

    def reduce_first(n):
        for half in (0, 1):
            first_stage[n].wait(half)
            part = parts[n](b, half)
            part[...] = (part[...].astype(f32) + first_stage[n].received(half)).astype(bf16)
        second_stage[n].start()

    def group_sum(ref, got):
        ref[...] = add_up(ref[...], lambda k: got[(b ^ (4 * (k + 1))) // 4].astype(f32), groups - 1).astype(bf16)

    def across_groups(swap, ref, got):
        if groups > 1:
            swap.start()
            swap.wait_all()
            swap.done()
            group_sum(ref, got)

    def others_sum(got):
        return lambda k: got[lax.rem(t + 1 + k, z)].astype(f32)

    def reduce_second(n):
        own = (
            lambda: R.uG[cut(q, dm.uq), cut(t, hf)],
            lambda: R.dG[t, cut(q, dm.dq), :],
            lambda: R.oG[t, cut(q, dm.oq), :],
        )[n]
        sums = (R.u_f, R.d_f, R.o_f)[n]
        sums[...] = own().astype(f32)

        def add(ref):
            sums[...] += ref[...].astype(f32)

        second_stage[n].finish(add)
        piece_refs[n][...] = sums[...].astype(bf16)
        across_groups(group_stage[n], piece_refs[n], group_refs[n])
        place_copies[n].start()
        third_stage[n].start()

    def tokens_out(r):
        R.tgT[r] = R.tp_s[r, cut(t, lw), :].astype(f32)

        def add(ref):
            R.tgT[r] += ref[...].astype(f32)

        tok_folds[r].finish(add)

    def add_vec(k):
        R.vs[1] += R.vb[b ^ k]

    def add_bias(k):
        R.bvF[...] += R.bvb[b ^ k]

    back_far(0)
    back_near(0, 0)
    back_near(0, 1)
    attend_back(0, b, True)
    vec_pair.wait_all()
    R.vs[0] = R.sv[...] + R.vp[...]
    vec_blk.start()
    back_far(1)
    fold_kv(0)
    reduce_first(1)
    back_near(1, 0)
    back_near(1, 1)
    second_stage[1].step(1)
    attend_back(1, b, True)
    send_first(0)
    fold_kv(1)
    second_stage[1].step(2)
    project_back(0)
    vec_blk.wait_all()
    R.vs[1] = R.vs[0]
    each(1, dm.nb, add_vec)
    vec_z.start()
    weight_grads(0)
    tok_folds[0].step(1)
    reduce_second(1)
    fold_first(0)
    project_back(1)
    send_first(2)
    tok_folds[0].step(2)
    weight_grads(1)
    R.wT[...] = R.w_acc[...].astype(bf16)
    w_pair.start()
    bv_pair.start()
    tok_folds[1].step(1)
    third_stage[1].forward()
    w_pair.wait_all()
    R.w1[...] = (R.w_acc[cut(c, half_w), :] + R.wR[...].astype(f32)).astype(bf16)
    w_blk.start()
    bv_pair.wait_all()
    R.bv_s[1] = R.bv_s[0] + R.bvp[...]
    bv_blk.start()
    fold_first(2)
    tokens_out(0)
    tok_folds[1].step(2)
    reduce_first(0)
    reduce_first(2)
    w_blk.wait_all()
    R.wP[...] = add_up(
        R.w1[cut(start_r, wq_r), cut(start_l, wq_l)], lambda k: R.wr[q ^ (k + 1)].astype(f32), 3
    ).astype(bf16)
    across_groups(w_group, R.wP, R.gw)
    w_place.start()
    w_plane.start()
    second_stage[0].step(1)
    second_stage[2].step(1)
    tokens_out(1)
    w_plane.forward()
    second_stage[0].step(2)
    second_stage[2].step(2)
    vec_z.wait_all()
    R.svF[...] = add_up(R.vs[1], others_sum(R.vz), z - 1)
    bv_blk.wait_all()
    R.bvF[...] = R.bv_s[1]
    each(1, dm.nb, add_bias)
    reduce_second(0)
    reduce_second(2)
    third_stage[0].forward()
    third_stage[2].forward()
    order = (
        (third_stage[1], place_copies[1], last_stage[1]),
        (w_plane, w_place, w_last),
        (third_stage[0], place_copies[0], last_stage[0]),
        (third_stage[2], place_copies[2], last_stage[2]),
    )
    for gather, copy, swap in order:
        copy.wait()
        gather.wait_all()
        swap.start()
    for _, _, swap in order:
        swap.wait_all()
    for swap in out_swaps:
        swap.wait_all()
    for transfer in (
        up_spread, down_spread, *ctx_swaps, cot_swap, ub_swap, seg_swap, wo_pair,
        hl_pair, feed_pair, fg_pair, part_pair, og_pair, *out_swaps, *grad_swaps,
        *first_stage, *second_stage, *third_stage, *last_stage, vec_pair, vec_blk, vec_z, bv_pair, bv_blk,
        *kv_folds, *tok_folds, w_pair, w_blk, w_plane, w_last,
    ):
        transfer.done()


def back_through(w, low, lw):
    return sum(dot(w[m], low[lw * m : lw * (m + 1)], 1, 0) for m in range(3))


def run_layer(dm, *inputs):
    shape = jax.ShapeDtypeStruct
    vmem, hbm = pl.BlockSpec(memory_space=pltpu.VMEM), pl.BlockSpec(memory_space=pl.ANY)
    V, rows, lw, tok, d, pt, own, z = pltpu.VMEM, dm.rows, dm.lw, dm.tok, dm.d, dm.pt, dm.own, dm.z
    small = dm.nb == 4
    both, half_h, half_z = 2 * own, dm.hid // 2, z // 2
    vectors = [f"vec{n}" for n in range(7)]
    in_names = ["tok", "seg", "w", "ib", "cot", *vectors, "up", "down", "wo"]
    outs = {
        "loT": ((rows, lw, tok), bf16, vmem),
        "tgT": ((rows, lw, tok), f32, vmem),
        "wF": ((dm.wr, d), bf16, hbm),
        "fu": ((d, dm.ff), bf16, hbm),
        "fd": ((dm.ff, d), bf16, hbm),
        "fo": ((lw, d), bf16, hbm),
        "svF": ((16, d), f32, vmem),
        "bvF": ((8, 256), f32, vmem),
    }
    kv, received = ((rows, dm.nb, 2 * lw, tok), bf16), ((rows, 3 if small else dm.nb, 2 * lw, tok), bf16)
    if not small:
        outs["kv"], outs["dkv_r"] = (*kv, hbm), (*received, hbm)
    scratch = {
        "xT": V((rows, d, tok), bf16),
        "wT": V((dm.wr, d), bf16),
        "wN": V((3, d, lw), bf16),
        "bcol": V((2, lw, 128), f32),
        "vec": V((8, d), f32),
        "qT": V((rows, lw, tok), bf16),
        "segg": V((dm.nb, 8, tok), jnp.int32),
        "m_s": V((rows, dm.heads, 8, tok), f32),
        "l_s": V((rows, dm.heads, 8, tok), f32),
        "acc": V((rows, dm.heads, HEAD_DIM, tok), f32),
        "ctxr": V((rows, lw, tok), f32),
        "ctxs": V((rows, lw, tok), bf16),
        "ctxT": V((rows, d, pt), bf16),
        "cotT": V((rows, d, pt), bf16),
        "lse": V((rows, 8, tok), f32),
        "ub8": V((8, dm.hf), f32),
        "ubH": V((8, dm.hid), f32),
        "upH": V((d, dm.hid), bf16),
        "downH": V((z, dm.hf, d), bf16),
        "woF": V((z, lw, d), bf16),
        "hl": V((both, d), bf16),
        "act": V((both, dm.hid), bf16),
        "bg": V((both, dm.hid), bf16),
        "pool": V((dm.hid // tok * both, tok), f32),
        "fgf": V((both, d), bf16),
        "fs_s": V((2, own, d), bf16),
        "fs_r": V((2, own, d), bf16),
        "z1_s": V((own, d), f32),
        "srg_s": V((own, d), f32),
        "outT": V((rows, d, pt), bf16),
        "cgT": V((rows, d, pt), bf16),
        "og_s": V((z, lw, dm.ol), bf16),
        "og_r": V((z, lw, dm.ol), bf16),
        "doT": V((rows, lw, tok), bf16),
        "frT": V((rows, d, pt), f32),
        "dG": V((z, dm.hf, d), bf16),
        "uG": V((d, dm.hid), bf16),
        "oG": V((z, lw, dm.ol), bf16),
        "sv": V((16, d), f32),
        "low_s": V((rows, 3 * lw, tok), bf16),
        "delta": V((rows, 8, tok), f32),
        "tp_s": V((rows, d, tok), bf16),
        "tp_r": V((rows, z + 1, lw, tok), bf16),
        "ur": V((6, dm.uq, half_h), bf16),
        "dr": V((6, half_z, dm.dq, d), bf16),
        "orr": V((6, half_z, dm.oq, dm.ol), bf16),
        "u2": V((z + 1, dm.uq, dm.hf), bf16),
        "d2": V((z + 1, dm.dq, d), bf16),
        "o2": V((z + 1, dm.oq, dm.ol), bf16),
        "u_f": V((dm.uq, dm.hf), f32),
        "d_f": V((dm.dq, d), f32),
        "o_f": V((dm.oq, dm.ol), f32),
        "uP": V((dm.uq, dm.hf), bf16),
        "dP": V((dm.dq, d), bf16),
        "oP": V((dm.oq, dm.ol), bf16),
        "wP": V((dm.wr // 4, d // 2), bf16),
        "vp": V((16, d), f32),
        "vb": V((dm.nb, 16, d), f32),
        "vz": V((z, 16, d), f32),
        "vs": V((2, 16, d), f32),
        "wR": V((dm.wr // 2, d), bf16),
        "w1": V((dm.wr // 2, d), bf16),
        "wr": V((4, dm.wr // 4, d // 2), bf16),
        "bv_s": V((2, 8, 256), f32),
        "bvp": V((8, 256), f32),
        "bvb": V((dm.nb, 8, 256), f32),
        "w_acc": V((dm.wr, d), f32),
        "gu": V((dm.nb // 4, dm.uq, dm.hf), bf16),
        "gd": V((dm.nb // 4, dm.dq, d), bf16),
        "go": V((dm.nb // 4, dm.oq, dm.ol), bf16),
        "gw": V((dm.nb // 4, dm.wr // 4, d // 2), bf16),
        "kvc": V((2 * lw, tok), bf16),
        "local": pltpu.SemaphoreType.DMA((8,)),
        "sems": pltpu.SemaphoreType.DMA((540 + 24 * dm.nb,)),
    }
    if small:
        scratch["kv"], scratch["dkv_r"] = V(*kv), V(*received)
    names = (*in_names, *outs, *scratch)
    return pl.pallas_call(
        functools.partial(layer_kernel, dm, names),
        name="encoder_layer",
        out_shape=[shape(s, dtype) for s, dtype, _ in outs.values()],
        in_specs=[vmem] * 12 + [hbm] * 3,
        out_specs=[spec for _, _, spec in outs.values()],
        scratch_shapes=list(scratch.values()),
        compiler_params=pltpu.CompilerParams(
            collective_id=0, has_side_effects=True, vmem_limit_bytes=VMEM_LIMIT
        ),
    )(*inputs)


def shards(
    mesh, tokens, segment_ids, input_weight, input_bias, output_weight, output_bias, first_gain, first_shift,
    up_weight, up_bias, down_weight, down_bias, second_gain, second_shift, cotangent,
):
    dm = Dims(mesh, *tokens.shape, up_weight.shape[1])
    tokT = jnp.transpose(tokens, (0, 2, 1))
    cotT = jnp.transpose(cotangent, (0, 2, 1))
    loT, tgT, wF, fu, fd, fo, svF, bvF, *_ = run_layer(
        dm, tokT, segment_ids, jnp.transpose(input_weight, (0, 2, 1)), input_bias, cotT,
        output_bias, first_gain, first_shift, down_bias, second_gain, second_shift, up_bias,
        up_weight, down_weight, output_weight,
    )
    low = write_outputs(dm, loT, tgT, wF, fu, fd, fo, svF, bvF)
    layer_output, tokens_grad, w_grad, out_w, up_w, down_w, bias, ub, *vectors = low
    second_gain_g, second_shift_g, down_b, first_gain_g, first_shift_g, out_b = vectors
    return (
        jnp.transpose(layer_output, (0, 2, 1)),
        jnp.transpose(tokens_grad, (0, 2, 1)),
        jnp.transpose(w_grad, (0, 2, 1)),
        bias,
        out_w,
        out_b,
        first_gain_g,
        first_shift_g,
        up_w,
        ub,
        down_w,
        down_b,
        second_gain_g,
        second_shift_g,
    )


def output_kernel(dm, loT, tgT, wF, fu, fd, fo, svF, bvF, lo, tg, w_o, fo_o, fu_o, fd_o, bias, ub, *vectors):
    lo[...] = loT[...]
    tg[...] = tgT[...]
    w_o[...] = wF[...].reshape(3, dm.lw, dm.d).astype(f32)
    fu_o[...] = fu[...].astype(f32)
    fd_o[...] = fd[...].astype(f32)
    fo_o[...] = fo[...].astype(f32)
    bias[...] = bvF[0:2, 0 : dm.lw]
    for n, ref in enumerate(vectors):
        ref[...] = svF[n, :]
    t = lax.axis_index("tensor")
    for half in range(2):
        row = svF[pl.ds(6 + 2 * half + lax.div(t, 2), 1), cut(lax.rem(t, 2), dm.hf)]
        ub[pl.ds(dm.hf * half, dm.hf)] = row.reshape(dm.hf)


def write_outputs(dm, *inputs):
    shape = jax.ShapeDtypeStruct
    vmem = pl.BlockSpec(memory_space=pltpu.VMEM)
    outs = [
        shape((dm.rows, dm.lw, dm.tok), bf16),
        shape((dm.rows, dm.lw, dm.tok), f32),
        shape((3, dm.lw, dm.d), f32),
        shape((dm.lw, dm.d), f32),
        shape((dm.d, dm.ff), f32),
        shape((dm.ff, dm.d), f32),
        shape((2, dm.lw), f32),
        shape((dm.ff,), f32),
        *[shape((dm.d,), f32)] * 6,
    ]
    return pl.pallas_call(
        functools.partial(output_kernel, dm),
        name="write_outputs",
        out_shape=outs,
        in_specs=[vmem] * len(inputs),
        out_specs=[vmem] * len(outs),
        compiler_params=pltpu.CompilerParams(vmem_limit_bytes=VMEM_LIMIT),
    )(*inputs)


def solution(mesh):
    rows = P("dp", "blk", "tensor")
    placed = (
        rows, P("dp", "blk"), P(None, None, "tensor"), P(None, "tensor"), P("tensor", None), P(), P(), P(),
        P(None, "tensor"), P("tensor"), P("tensor", None), P(), P(), P(), rows,
    )
    results = (
        rows, rows, P(None, None, "tensor"), P(None, "tensor"), P("tensor", None), P(), P(), P(),
        P(None, "tensor"), P("tensor"), P("tensor", None), P(), P(), P(),
    )
    return jax.shard_map(
        functools.partial(shards, mesh), mesh=mesh, in_specs=placed, out_specs=results, check_vma=False
    )
```

```python
import functools

import jax
import jax.numpy as jnp
from jax import lax
from jax.experimental import pallas as pl
from jax.experimental.pallas import tpu as pltpu
from jax.sharding import PartitionSpec as P

HEAD_DIM = 64
EPS = 1e-12
MASKED = -1e30
MESH = pl.DeviceIdType.MESH
bf16 = jnp.bfloat16
f32 = jnp.float32
VMEM_LIMIT = 60 * 2**20


def dot(a, b, ca, cb):
    return lax.dot_general(a, b, (((ca,), (cb,)), ((), ())), preferred_element_type=f32)


def aligned(index, size):
    return pl.multiple_of(index * size, size)


def cut(index, size):
    return pl.ds(aligned(index, size), size)


class Refs:
    def __init__(self, names, refs):
        for name, ref in zip(names, refs, strict=True):
            setattr(self, name, ref)


class Sems:
    def __init__(self, ref=None):
        self.ref = ref
        self.used = 0

    def take(self, count):
        first = self.used
        self.used += count
        return first


class Swap:
    def __init__(self, sems, axis, n, src, dst, xor=False, stride=1):
        self.sems, self.axis, self.n, self.src, self.dst, self.xor = sems, axis, n, src, dst, xor
        self.stride = stride
        self.me = lax.axis_index(axis)
        self.send, self.recv = sems.take(n), sems.take(n)

    def to(self, k):
        return self.me ^ (k * self.stride) if self.xor else lax.rem(self.me + k, self.n)

    def source(self, k):
        return self.me ^ (k * self.stride) if self.xor else lax.rem(self.me + self.n - k, self.n)

    def copy(self, k, dst_index):
        return pltpu.make_async_remote_copy(
            self.src(self.to(k)),
            self.dst(dst_index),
            self.sems.ref.at[self.send + k],
            self.sems.ref.at[self.recv + k],
            device_id={self.axis: self.to(k)},
            device_id_type=MESH,
        )

    def start_one(self, k):
        self.copy(k, self.me).start()

    def start(self):
        each(1, self.n, self.start_one)

    def wait(self, k):
        self.copy(k, self.source(k)).wait_recv()

    def wait_all(self):
        each(1, self.n, self.wait)

    def done(self):
        each(1, self.n, lambda k: self.copy(k, self.me).wait_send())


def each(low, high, body):
    if high - low <= 4:
        for k in range(low, high):
            body(k)
    else:

        def step(k, carry):
            body(k)
            return carry

        lax.fori_loop(low, high, step, 0)


class Line:
    def __init__(self, sems, n, view, own):
        self.sems, self.n, self.view, self.own = sems, n, view, own
        self.t = lax.axis_index("tensor")
        self.recv, self.right, self.left = sems.take(n), sems.take(n), sems.take(n)

    def copy(self, chunk, right, k):
        return pltpu.make_async_remote_copy(
            self.own if k == 0 else self.view(chunk),
            self.view(chunk),
            self.sems.ref.at[(self.right if right else self.left) + k],
            self.sems.ref.at[self.recv + chunk],
            device_id={"tensor": self.t + 1 if right else self.t - 1},
            device_id_type=MESH,
        )

    def start(self):
        t, n = self.t, self.n
        pl.when(t < n - 1)(lambda: self.copy(t, True, 0).start())
        pl.when(t > 0)(lambda: self.copy(t, False, 0).start())

    def step(self, k):
        t, n = self.t, self.n

        @pl.when(t >= k)
        def _():
            self.copy(t - k, True, k).wait_recv()
            pl.when(t < n - 1)(lambda: self.copy(t - k, True, k).start())

        @pl.when(t + k < n)
        def _():
            self.copy(t + k, False, k).wait_recv()
            pl.when(t > 0)(lambda: self.copy(t + k, False, k).start())

    def done(self):
        t, n = self.t, self.n
        for k in range(n):
            pl.when((t >= k) & (t < n - 1))(lambda k=k: self.copy(t - k, True, k).wait_send())
            pl.when((t + k < n) & (t > 0))(lambda k=k: self.copy(t + k, False, k).wait_send())


class Plane:
    def __init__(self, sems, n, view, own):
        self.sems, self.n, self.view, self.own = sems, n, view, own
        self.b = lax.axis_index("blk")
        self.send, self.recv = sems.take(2 * n), sems.take(2 * n)

    def copy(self, k, half, origin, to, own):
        return pltpu.make_async_remote_copy(
            self.own(half) if own else self.view(origin, half),
            self.view(origin, half),
            self.sems.ref.at[self.send + 2 * k + half],
            self.sems.ref.at[self.recv + 2 * k + half],
            device_id={"blk": to},
            device_id_type=MESH,
        )

    def ours(self, k, half):
        return self.copy(k, half, self.b, self.b ^ k, True)

    def passed(self, half):
        origin, to = (self.b ^ 1, self.b ^ 2) if half == 0 else (self.b ^ 2, self.b ^ 1)
        return self.copy(3, half, origin, to, False)

    def start(self):
        if self.n == 4:
            for k, half in ((1, 0), (2, 1), (1, 1), (2, 0)):
                self.ours(k, half).start()
        else:

            def go(k):
                self.ours(k, 0).start()
                self.ours(k, 1).start()

            each(1, self.n, go)

    def landed(self, k, half):
        self.copy(k, half, self.b ^ k, self.b ^ k, True).wait_recv()

    def forward(self):
        if self.n == 4:
            self.landed(1, 0)
            self.passed(0).start()
            self.landed(2, 1)
            self.passed(1).start()

    def wait(self, k):
        if self.n != 4:
            self.landed(k, 0)
            self.landed(k, 1)
        elif k == 1:
            self.landed(1, 1)
        elif k == 2:
            self.landed(2, 0)
        else:
            self.landed(3, 0)
            self.landed(3, 1)

    def wait_all(self):
        each(1, self.n, self.wait)

    def done(self):
        if self.n == 4:
            for k, half in ((1, 0), (2, 1), (1, 1), (2, 0)):
                self.ours(k, half).wait_send()
            self.passed(0).wait_send()
            self.passed(1).wait_send()
        else:

            def go(k):
                self.ours(k, 0).wait_send()
                self.ours(k, 1).wait_send()

            each(1, self.n, go)


class Spread:
    def __init__(self, sems, n, view):
        self.sems, self.n, self.view = sems, n, view
        self.b, self.t = lax.axis_index("blk"), lax.axis_index("tensor")
        self.send, self.recv = sems.take(8 * n), sems.take(8 * n)

    def copy(self, s, k, half, origin, to):
        ref = self.view(s, origin, half)
        return pltpu.make_async_remote_copy(
            ref,
            ref,
            self.sems.ref.at[self.send + 8 * s + 2 * k + half],
            self.sems.ref.at[self.recv + 8 * s + 2 * k + half],
            device_id={"blk": to},
            device_id_type=MESH,
        )

    def ours(self, s):
        return [self.copy(s, k, half, self.b, self.b ^ k) for k, half in ((1, 0), (2, 1), (1, 1), (2, 0))]

    def passed(self, s, half):
        near, far = (1, 2) if half == 0 else (2, 1)
        return self.copy(s, 3, half, self.b ^ near, self.b ^ far)

    def landed(self, s, k, half):
        self.copy(s, k, half, self.b ^ k, self.b ^ k).wait_recv()

    def around(self, k, body):
        pl.when(self.t >= k)(lambda: body(self.t - k))
        pl.when(self.t + k < self.n)(lambda: body(self.t + k))

    def start(self, k):
        def body(s):
            for copy in self.ours(s):
                copy.start()

        self.around(k, body)

    def forward(self, k):
        def body(s):
            self.landed(s, 1, 0)
            self.passed(s, 0).start()
            self.landed(s, 2, 1)
            self.passed(s, 1).start()

        self.around(k, body)

    def wait_all(self):
        def body(s):
            self.landed(s, 1, 1)
            self.landed(s, 2, 0)
            self.landed(s, 3, 0)
            self.landed(s, 3, 1)

        for k in range(1, self.n):
            self.around(k, body)

    def done(self):
        def body(s):
            for copy in (*self.ours(s), self.passed(s, 0), self.passed(s, 1)):
                copy.wait_send()

        for k in range(1, self.n):
            self.around(k, body)


class Fold:
    def __init__(self, sems, part, relay, inbox):
        self.sems, self.part, self.relay, self.inbox = sems, part, relay, inbox
        self.b = lax.axis_index("blk")
        self.send, self.recv = sems.take(6), sems.take(6)

    def copy(self, n, src, dst, k):
        return pltpu.make_async_remote_copy(
            src,
            dst,
            self.sems.ref.at[self.send + n],
            self.sems.ref.at[self.recv + n],
            device_id={"blk": self.b ^ k},
            device_id_type=MESH,
        )

    def across(self, half):
        return self.copy(half, self.part(self.b ^ 3, half), self.relay(half), half + 1)

    def near(self, half):
        return self.copy(2 + half, self.part(self.b ^ (half + 1), half), self.inbox(half), half + 1)

    def folded(self, half):
        return self.copy(4 + half, self.relay(half), self.inbox(2 + half), 2 - half)

    def fold(self, half):
        self.across(half).wait_recv()
        part, relay = self.part(self.b ^ (2 - half), half), self.relay(half)
        relay[...] = (part[...].astype(f32) + relay[...].astype(f32)).astype(bf16)
        self.folded(half).start()

    def wait(self, half):
        self.near(half).wait_recv()
        self.folded(half).wait_recv()

    def received(self, half):
        return self.inbox(half)[...].astype(f32) + self.inbox(2 + half)[...].astype(f32)

    def done(self):
        for half in (0, 1):
            for transfer in (self.across, self.near, self.folded):
                transfer(half).wait_send()


class LineFold:
    def __init__(self, sems, n, part, relay):
        self.sems, self.n, self.part, self.relay = sems, n, part, relay
        self.t = lax.axis_index("tensor")
        self.send, self.recv = sems.take(n), sems.take(n + 1)

    def copy(self, j, right, fresh):
        to = self.t + 1 if right else self.t - 1
        slot = j if right else jnp.where(j == to, self.n, j)
        return pltpu.make_async_remote_copy(
            self.part(j) if fresh else self.relay(j),
            self.relay(slot),
            self.sems.ref.at[self.send + j],
            self.sems.ref.at[self.recv + slot],
            device_id={"tensor": to},
            device_id_type=MESH,
        )

    def landed(self, slot):
        pltpu.make_async_remote_copy(
            self.relay(slot),
            self.relay(slot),
            self.sems.ref.at[self.send],
            self.sems.ref.at[self.recv + slot],
            device_id={"tensor": lax.rem(self.t + 1, self.n)},
            device_id_type=MESH,
        ).wait_recv()

    def start(self):
        n = self.n

        @pl.when(self.t == 0)
        def _():
            for j in range(n - 1, 0, -1):
                self.copy(j, True, True).start()

        @pl.when(self.t == n - 1)
        def _():
            for j in range(n - 1):
                self.copy(j, False, True).start()

    def pass_on(self, j, right):
        self.landed(j)
        relay, part = self.relay(j), self.part(j)
        relay[...] = (relay[...].astype(f32) + part[...].astype(f32)).astype(bf16)
        self.copy(j, right, False).start()

    def step(self, m):
        back = self.n - 1 - self.t
        pl.when((self.t >= 1) & (self.t <= m) & (back >= 1))(lambda: self.pass_on(self.n - 1 + self.t - m, True))
        pl.when((back >= 1) & (back <= m) & (self.t >= 1))(lambda: self.pass_on(m - back, False))

    def finish(self, store):
        @pl.when(self.t > 0)
        def _():
            self.landed(self.t)
            store(self.relay(self.t))

        @pl.when(self.t < self.n - 1)
        def _():
            self.landed(self.n)
            store(self.relay(self.n))

    def done(self):
        for j in range(self.n):
            pl.when(self.t < j)(lambda j=j: self.copy(j, True, False).wait_send())
            pl.when(self.t > j)(lambda j=j: self.copy(j, False, False).wait_send())


class Dims:
    def __init__(self, mesh, rows, tok, width, ff):
        self.z, self.nb, self.nc = mesh.shape["tensor"], mesh.shape["blk"], mesh.shape["dp"]
        self.rows, self.tok, self.lw, self.ff = rows, tok, width, ff
        self.d = width * self.z
        self.heads = width // HEAD_DIM
        self.pt = tok // self.z
        self.own = rows * self.pt
        self.hf = ff // 2
        self.hid = self.hf * self.z
        self.uq, self.dq, self.oq, self.ol = self.d // 4, self.hf // 4, width // 4, self.d // 2
        self.wr = 3 * width


def enter(dm, dp=True, blk=True, tensor=True):
    barrier = pltpu.get_barrier_semaphore()
    count = 0
    for axis, n, wanted in (("dp", dm.nc, dp), ("blk", dm.nb, blk), ("tensor", dm.z, tensor)):
        if not wanted:
            continue
        me = lax.axis_index(axis)

        def greet(k, axis=axis, n=n, me=me):
            pl.semaphore_signal(barrier, inc=1, device_id={axis: lax.rem(me + k, n)}, device_id_type=MESH)

        each(1, n, greet)
        count += n - 1
    pl.semaphore_wait(barrier, count)


def mask_bias(segg, r, key_block, own_block, tok):
    key_row = segg[key_block, r : r + 1, :]
    column = jnp.transpose(jnp.broadcast_to(key_row.astype(f32), (128, tok)))
    wide = jnp.concatenate([column] * (tok // 128), axis=1)
    query_row = segg[own_block, r : r + 1, :].astype(f32)
    return jnp.where(wide == query_row, 0.0, MASKED)


def layer_kernel(dm, names, *refs):
    R = Refs(names, refs)
    t, b, c = lax.axis_index("tensor"), lax.axis_index("blk"), lax.axis_index("dp")
    q = lax.rem(b, 4)
    sems = Sems(R.sems)
    rows, lw, pt, own, d, tok, hf, z = dm.rows, dm.lw, dm.pt, dm.own, dm.d, dm.tok, dm.hf, dm.z
    small = dm.nb == 4
    mine, other = cut(c, own), cut(1 - c, own)
    quarter = lambda i: lax.rem(i, 4)
    half_d, half_z, half_h = d // 2, z // 2, dm.hid // 2
    split_u, split_o = dm.uq // 2, 128

    def z_swap(src, dst):
        return Swap(sems, "tensor", z, src, dst)

    def pair(src, dst):
        return Swap(sems, "dp", dm.nc, src, dst)

    token_lines = [
        Line(sems, z, lambda i, r=r: R.xT.at[r, cut(i, lw), :], R.xT.at[r, cut(t, lw), :]) for r in range(rows)
    ]
    seg_swap = Swap(sems, "blk", dm.nb, lambda to: R.segg.at[b], lambda i: R.segg.at[i], xor=True)
    ub_swap = z_swap(lambda to: R.ub8, lambda i: R.ubH.at[:, cut(i, hf)])
    up_own = R.up.at[cut(q, dm.uq), cut(c, hf)]
    down_own = R.down.at[pl.ds(pl.multiple_of(hf * c + dm.dq * q, dm.dq), dm.dq), :]
    wo_own = R.wo.at[:, cut(c, dm.ol)]

    def up_piece(i):
        return R.upH.at[cut(q, dm.uq), cut(i, hf)]

    def down_piece(i):
        return R.downH.at[i, cut(q, dm.dq), :]

    def wo_piece(i):
        return R.woF.at[i, :, cut(c, dm.ol)]

    up_line = Line(sems, z, up_piece, up_own)
    down_line = Line(sems, z, down_piece, down_own)
    wo_line = Line(sems, z, wo_piece, wo_own)

    def up_view(s, i, half):
        start = pl.multiple_of(dm.uq * quarter(i) + split_u * half, split_u)
        return R.upH.at[pl.ds(start, split_u), cut(s, hf)]

    def down_view(s, i, half):
        return R.downH.at[s, cut(quarter(i), dm.dq), pl.ds(half_d * half, half_d)]

    up_spread, down_spread = Spread(sems, z, up_view), Spread(sems, z, down_view)
    wo_pair = pair(lambda to: R.woF.at[:, :, cut(c, dm.ol)], lambda i: R.woF.at[:, :, cut(i, dm.ol)])
    cot_swap = z_swap(lambda to: R.cot.at[:, :, cut(to, pt)], lambda i: R.cotT.at[:, cut(i, lw), :])
    kv_planes = [
        Plane(
            sems,
            dm.nb,
            lambda i, half, r=r: R.kv.at[r, i, pl.ds(lw * half, lw), :],
            lambda half, r=r: R.kv.at[r, b, pl.ds(lw * half, lw), :],
        )
        for r in range(rows)
    ]
    ctx_swaps = [
        z_swap(lambda to, r=r: R.ctxs.at[r, :, cut(to, pt)], lambda i, r=r: R.ctxT.at[r, cut(i, lw), :])
        for r in range(rows)
    ]
    hl_pair = pair(lambda to: R.hl.at[mine], lambda i: R.hl.at[cut(i, own)])
    feed_pair = pair(lambda to: R.fs_s.at[0], lambda i: R.fs_r.at[0])
    fg_pair = pair(lambda to: R.fgf.at[mine], lambda i: R.fgf.at[cut(i, own)])
    part_pair = pair(lambda to: R.fs_s.at[1], lambda i: R.fs_r.at[1])
    og_pair = pair(lambda to: R.og_s, lambda i: R.og_r)
    out_swaps = [
        z_swap(lambda to, r=r: R.outT.at[r, cut(to, lw), :], lambda i, r=r: R.loT.at[r, :, cut(i, pt)])
        for r in range(rows)
    ]
    grad_swaps = [
        z_swap(lambda to, r=r: R.cgT.at[r, cut(to, lw), :], lambda i, r=r: R.doT.at[r, :, cut(i, pt)])
        for r in range(rows)
    ]

    def u_part(i, half):
        return R.uG.at[cut(quarter(i), dm.uq), pl.ds(half_h * half, half_h)]

    def d_part(i, half):
        return R.dG.at[pl.ds(half_z * half, half_z), cut(quarter(i), dm.dq), :]

    def o_part(i, half):
        return R.oG.at[pl.ds(half_z * half, half_z), cut(quarter(i), dm.oq), :]

    parts = (u_part, d_part, o_part)
    first_stage = tuple(
        Fold(sems, part, lambda half, got=got: got.at[4 + half], lambda n, got=got: got.at[n])
        for part, got in zip(parts, (R.ur, R.dr, R.orr), strict=True)
    )
    second_stage = (
        LineFold(sems, z, lambda j: R.uG.at[cut(q, dm.uq), cut(j, hf)], lambda j: R.u2.at[j]),
        LineFold(sems, z, lambda j: R.dG.at[j, cut(q, dm.dq), :], lambda j: R.d2.at[j]),
        LineFold(sems, z, lambda j: R.oG.at[j, cut(q, dm.oq), :], lambda j: R.o2.at[j]),
    )
    groups = dm.nb // 4
    piece_refs, group_refs = (R.uP, R.dP, R.oP), (R.gu, R.gd, R.go)
    group_stage = tuple(
        Swap(sems, "blk", groups, lambda to, ref=ref: ref, lambda i, got=got: got.at[i // 4], True, 4)
        for ref, got in zip(piece_refs, group_refs, strict=True)
    )

    def fu_view(i, half):
        return R.fu.at[pl.ds(pl.multiple_of(dm.uq * quarter(i) + split_u * half, split_u), split_u), cut(c, hf)]

    def fd_view(i, half):
        start = pl.multiple_of(hf * c + dm.dq * quarter(i), dm.dq)
        return R.fd.at[pl.ds(start, dm.dq), pl.ds(half_d * half, half_d)]

    def fo_view(i, half):
        start = pl.multiple_of(dm.ol * c + split_o * half, 128)
        return R.fo.at[cut(quarter(i), dm.oq), pl.ds(start, dm.ol - split_o if half else split_o)]

    piece_halves = (
        lambda half: R.uP.at[pl.ds(split_u * half, split_u), :],
        lambda half: R.dP.at[:, pl.ds(half_d * half, half_d)],
        lambda half: R.oP.at[:, pl.ds(split_o * half, dm.ol - split_o if half else split_o)],
    )
    third_stage = tuple(
        Plane(sems, 4, view, piece) for view, piece in zip((fu_view, fd_view, fo_view), piece_halves, strict=True)
    )
    place = (
        R.fu.at[cut(q, dm.uq), cut(c, hf)],
        R.fd.at[pl.ds(pl.multiple_of(hf * c + dm.dq * q, dm.dq), dm.dq), :],
        R.fo.at[cut(q, dm.oq), cut(c, dm.ol)],
    )
    place_copies = [
        pltpu.make_async_copy(src, dst, R.local.at[4 + n])
        for n, (src, dst) in enumerate(zip(piece_refs, place, strict=True))
    ]
    last_stage = (
        pair(lambda to: R.fu.at[:, cut(c, hf)], lambda i: R.fu.at[:, cut(i, hf)]),
        pair(lambda to: R.fd.at[cut(c, hf), :], lambda i: R.fd.at[cut(i, hf), :]),
        pair(lambda to: R.fo.at[:, cut(c, dm.ol)], lambda i: R.fo.at[:, cut(i, dm.ol)]),
    )
    vec_pair = pair(lambda to: R.sv, lambda i: R.vp)
    vec_blk = Swap(sems, "blk", dm.nb, lambda to: R.vs.at[0], lambda i: R.vb.at[i], xor=True)
    vec_z = z_swap(lambda to: R.vs.at[1], lambda i: R.vz.at[i])
    bv_pair = pair(lambda to: R.bv_s.at[0], lambda i: R.bvp)
    bv_blk = Swap(sems, "blk", dm.nb, lambda to: R.bv_s.at[1], lambda i: R.bvb.at[i], xor=True)
    if small:
        kv_folds = [
            Fold(
                sems,
                lambda i, half, r=r: R.kv.at[r, i, pl.ds(lw * half, lw), :],
                lambda half, r=r: R.dkv_r.at[r, 2, pl.ds(lw * half, lw), :],
                lambda n, r=r: R.dkv_r.at[r, n // 2, pl.ds(lw * (n % 2), lw), :],
            )
            for r in range(rows)
        ]
    else:
        kv_folds = [
            Swap(sems, "blk", dm.nb, lambda to, r=r: R.kv.at[r, to], lambda i, r=r: R.dkv_r.at[r, i], xor=True)
            for r in range(rows)
        ]
    tok_folds = [
        LineFold(sems, z, lambda j, r=r: R.tp_s.at[r, cut(j, lw), :], lambda j, r=r: R.tp_r.at[r, j])
        for r in range(rows)
    ]
    half_w, wq_r, wq_l = dm.wr // 2, dm.wr // 4, d // 2
    w_pair = pair(lambda to: R.wT.at[cut(to, half_w), :], lambda i: R.wR)

    def w_at(i):
        return lax.div(quarter(i), 2), lax.rem(i, 2)

    w_blk = Swap(
        sems, "blk", 4,
        lambda to: R.w1.at[cut(w_at(to)[0], wq_r), cut(w_at(to)[1], wq_l)],
        lambda i: R.wr.at[quarter(i)], xor=True,
    )
    w_split = 80

    def wf_view(i, half):
        start = pl.multiple_of(half_w * c + wq_r * w_at(i)[0] + w_split * half, 16)
        return R.wF.at[pl.ds(start, wq_r - w_split if half else w_split), cut(w_at(i)[1], wq_l)]

    start_r, start_l = w_at(b)
    w_group = Swap(sems, "blk", groups, lambda to: R.wP, lambda i: R.gw.at[i // 4], True, 4)
    w_plane = Plane(
        sems, 4, wf_view, lambda half: R.wP.at[pl.ds(w_split * half, wq_r - w_split if half else w_split), :]
    )
    w_place = pltpu.make_async_copy(
        R.wP,
        R.wF.at[pl.ds(pl.multiple_of(half_w * c + wq_r * start_r, 16), wq_r), cut(start_l, wq_l)],
        R.local.at[7],
    )
    w_last = pair(lambda to: R.wF.at[cut(c, half_w), :], lambda i: R.wF.at[cut(i, half_w), :])

    def sync(src, dst):
        copy = pltpu.make_async_copy(src, dst, R.local.at[3])
        copy.start()
        copy.wait()

    def chunk_of(r, block):
        if small:
            return R.kv.at[r, block]
        sync(R.kv.at[r, block], R.kvc)
        return R.kvc

    def project(r):
        y = dot(R.w[...].reshape(dm.wr, d), R.xT[r], 1, 0)
        R.qT[r] = (y[:lw] + R.bcol[0][:, :1]).astype(bf16) * bf16(HEAD_DIM**-0.5)
        chunk = R.kv.at[r, b] if small else R.kvc
        chunk[0:lw, :] = y[lw : 2 * lw].astype(bf16)
        chunk[lw : 2 * lw, :] = (y[2 * lw :] + R.bcol[1][:, :1]).astype(bf16)
        if not small:
            sync(R.kvc, R.kv.at[r, b])
        for h in range(dm.heads):
            R.m_s[r, h] = jnp.full((8, tok), MASKED, f32)
            R.l_s[r, h] = jnp.zeros((8, tok), f32)
            R.acc[r, h] = jnp.zeros((HEAD_DIM, tok), f32)
        kv_planes[r].start()

    def attend(r, block):
        bias = mask_bias(R.segg, r, block, b, tok)
        chunk = chunk_of(r, block)
        for h in range(dm.heads):
            k = chunk[pl.ds(HEAD_DIM * h, HEAD_DIM), :]
            v = chunk[pl.ds(lw + HEAD_DIM * h, HEAD_DIM), :]
            s = dot(k, R.qT[r, pl.ds(HEAD_DIM * h, HEAD_DIM), :], 0, 0) + bias
            old = R.m_s[r, h, :1]
            new = jnp.maximum(old, jnp.max(s, 0, keepdims=True))
            p = jnp.exp(s - new)
            scale = jnp.exp(old - new)
            R.l_s[r, h, :1] = R.l_s[r, h, :1] * scale + jnp.sum(p, 0, keepdims=True)
            R.m_s[r, h, :1] = new
            R.acc[r, h] = R.acc[r, h] * scale + dot(v, p.astype(bf16), 1, 0)

    def attend_near(r, k):
        if small:
            kv_planes[r].wait(k)
            attend(r, b ^ k)

    def attend_rest(r):
        if not small:

            def body(k):
                kv_planes[r].wait(k)
                attend(r, b ^ k)

            each(1, dm.nb, body)

    def finish(r):
        for h in range(dm.heads):
            denominator = R.l_s[r, h, :1]
            ctx = R.acc[r, h] / denominator
            R.ctxr[r, pl.ds(HEAD_DIM * h, HEAD_DIM), :] = ctx
            R.ctxs[r, pl.ds(HEAD_DIM * h, HEAD_DIM), :] = ctx.astype(bf16)
            R.lse[r, h : h + 1, :] = R.m_s[r, h, :1] + jnp.log(denominator)
        R.ctxT[r, cut(t, lw), :] = R.ctxs[r, :, cut(t, pt)]
        ctx_swaps[r].start()

    enter(dm)
    for r in range(rows):
        R.xT[r, cut(t, lw), :] = R.tok[r]
    token_lines[0].start()
    up_line.start()
    weight_copies = [
        pltpu.make_async_copy(src, dst, R.local.at[n])
        for n, (src, dst) in enumerate(
            (
                (R.up.at[:, cut(c, hf)], R.upH.at[:, cut(t, hf)]),
                (R.down.at[cut(c, hf), :], R.downH.at[t]),
                (wo_own, wo_piece(t)),
            )
        )
    ]
    for copy in weight_copies:
        copy.start()
    for r in range(rows):
        R.cotT[r, cut(t, lw), :] = R.cot[r, :, cut(t, pt)]
    for m in range(3):
        R.wN[m] = jnp.transpose(R.w[m])
    R.segg[b] = jnp.zeros((8, tok), jnp.int32)
    R.segg[b, 0:rows, :] = R.seg[...]
    seg_swap.start()
    for n in range(7):
        R.vec[n, :] = getattr(R, f"vec{n}")[...]
    for n in range(2):
        R.bcol[n] = jnp.transpose(jnp.broadcast_to(R.ib[n : n + 1, :], (128, lw)))
    R.ub8[...] = jnp.broadcast_to(R.vec[6:7, cut(c, hf)], (8, hf))
    R.ubH[:, cut(t, hf)] = R.ub8[...]
    ub_swap.start()

    token_lines[0].step(1)
    up_line.step(1)
    up_spread.start(1)
    token_lines[0].step(2)
    token_lines[1].start()
    up_line.step(2)
    up_spread.start(2)
    token_lines[0].step(3)
    project(0)
    up_line.step(3)
    up_spread.start(3)
    up_spread.forward(1)
    token_lines[1].step(1)
    wo_line.start()
    seg_swap.wait_all()
    attend(0, b)
    up_spread.forward(2)
    token_lines[1].step(2)
    down_line.start()
    kv_planes[0].forward()
    up_spread.forward(3)
    wo_line.step(1)
    token_lines[1].step(3)
    project(1)
    wo_line.step(2)
    down_line.step(1)
    down_spread.start(1)
    attend(1, b)
    wo_line.step(3)
    for copy in weight_copies:
        copy.wait()
    wo_pair.start()
    attend_near(0, 1)
    down_line.step(2)
    down_spread.start(2)
    attend_near(0, 2)
    down_line.step(3)
    down_spread.start(3)
    attend_near(0, 3)
    attend_rest(0)
    finish(0)
    kv_planes[1].forward()
    attend_near(1, 1)
    down_spread.forward(1)
    attend_near(1, 2)
    down_spread.forward(2)
    attend_near(1, 3)
    attend_rest(1)
    finish(1)
    cot_swap.start()
    down_spread.forward(3)

    out_b, g1, s1, down_b, g2, s2 = (R.vec[n : n + 1, :] for n in range(6))

    def stats(x):
        center = x - jnp.mean(x, -1, keepdims=True)
        inverse = lax.rsqrt(jnp.mean(center * center, -1, keepdims=True) + EPS)
        return center * inverse, inverse

    def norm_back(g, gain, zn, inverse):
        e = g * gain
        return (e - jnp.mean(e, -1, keepdims=True) - zn * jnp.mean(e * zn, -1, keepdims=True)) * inverse

    def total(x):
        return jnp.sum(x, 0, keepdims=True)

    blocks = dm.hid // tok

    inverse1 = []
    wo_pair.wait_all()
    for r in range(rows):
        ctx_swaps[r].wait_all()
        attended = dot(R.ctxT[r], R.woF[...].reshape(d, d), 0, 0) + out_b
        zn, inv = stats(jnp.transpose(R.xT[r, :, cut(t, pt)].astype(f32)) + attended)
        inverse1.append(inv)
        R.z1_s[pl.ds(pt * r, pt), :] = zn
        R.hl[pl.ds(pl.multiple_of(own * c + pt * r, pt), pt), :] = (zn * g1 + s1).astype(bf16)
    hl_pair.start()
    ub_swap.wait_all()

    def expand(core):
        part = cut(core, own)
        for n in range(blocks):
            cols = pl.ds(tok * n, tok)
            v = dot(R.hl[part, :], R.upH[:, cols], 1, 0) + R.ubH[:1, cols]
            phi = 0.5 + 0.5 * lax.erf(v * (0.5**0.5))
            R.act[part, cols] = (v * phi).astype(bf16)
            R.pool[cut(2 * n + core, own), :] = phi + v * (jnp.exp(-0.5 * v * v) * 0.3989422804014327)

    up_spread.wait_all()
    expand(c)
    hl_pair.wait_all()
    expand(1 - c)
    down_spread.wait_all()
    down_w = R.downH[...].reshape(dm.hid, d)
    R.fs_s[0] = dot(R.act[other, :], down_w, 1, 0).astype(bf16)
    feed_pair.start()
    feed = dot(R.act[mine, :], down_w, 1, 0) + down_b
    cot_swap.wait_all()
    g = jnp.concatenate([jnp.transpose(R.cotT[r].astype(f32)) for r in range(rows)], 0)
    feed_pair.wait_all()
    hidden = R.z1_s[...] * g1 + s1
    z2, inverse2 = stats(hidden + (feed + R.fs_r[0].astype(f32)))
    resid = norm_back(g, g2, z2, inverse2)
    R.srg_s[...] = resid
    low = resid.astype(bf16)
    R.fgf[mine, :] = low
    fg_pair.start()
    out = z2 * g2 + s2
    R.sv[...] = jnp.zeros_like(R.sv)
    R.sv[0:1, :] = total(g * z2)
    R.sv[1:2, :] = total(g)
    R.sv[2:3, :] = total(low.astype(f32))

    def contract(core):
        part = cut(core, own)
        for n in range(blocks):
            cols = pl.ds(tok * n, tok)
            grad = dot(R.fgf[part, :], R.downH[...].reshape(dm.hid, d)[tok * n : tok * (n + 1)], 1, 1)
            R.bg[part, cols] = (grad * R.pool[cut(2 * n + core, own), :]).astype(bf16)

    def send_first(n):
        for half in (0, 1):
            first_stage[n].across(half).start()
        for half in (0, 1):
            first_stage[n].near(half).start()

    contract(c)
    fg_pair.wait_all()
    for n in range(z):
        R.dG[n] = dot(R.act[:, pl.ds(hf * n, hf)], R.fgf[...], 0, 0).astype(bf16)
    send_first(1)
    contract(1 - c)
    R.fs_s[1] = dot(R.bg[other, :], R.upH[...], 1, 1).astype(bf16)
    part_pair.start()
    part = dot(R.bg[mine, :], R.upH[...], 1, 1)
    for n in range(blocks):
        cols = pl.ds(tok * n, tok)
        R.uG[:, cols] = dot(R.hl[...], R.bg[:, cols], 0, 0).astype(bf16)
    part_pair.wait_all()
    hidden_grad = R.srg_s[...] + (part + R.fs_r[1].astype(f32))
    z1 = R.z1_s[...]
    first = norm_back(hidden_grad, g1, z1, jnp.concatenate(inverse1, 0))
    low = first.astype(bf16)
    for r in range(rows):
        R.cgT[r] = dot(R.woF[...].reshape(d, d), low[pt * r : pt * (r + 1)], 1, 1).astype(bf16)
        R.doT[r, :, cut(t, pt)] = R.cgT[r, cut(t, lw), :]
        grad_swaps[r].start()
        R.frT[r] = jnp.transpose(first[pt * r : pt * (r + 1)])
    first_stage[1].fold(0)
    first_stage[1].fold(1)
    out_grad = sum(dot(R.ctxT[r], low[pt * r : pt * (r + 1)], 1, 0) for r in range(rows))
    left = out_grad[:, : dm.ol].reshape(z, lw, dm.ol)
    right = out_grad[:, dm.ol :].reshape(z, lw, dm.ol)
    R.oG[...] = jnp.where(c == 0, left, right).astype(bf16)
    R.og_s[...] = jnp.where(c == 0, right, left).astype(bf16)
    og_pair.start()
    R.sv[3:4, :] = total(hidden_grad * z1)
    R.sv[4:5, :] = total(hidden_grad)
    R.sv[5:6, :] = total(low.astype(f32))
    for n in range(z):
        R.sv[pl.ds(6 + 2 * c + n // 2, 1), pl.ds(hf * (n % 2), hf)] = total(
            R.bg[:, pl.ds(hf * n, hf)].astype(f32)
        )
    vec_pair.start()
    for r in range(rows):
        R.outT[r] = jnp.transpose(out[pt * r : pt * (r + 1)]).astype(bf16)
        R.loT[r, :, cut(t, pt)] = R.outT[r, cut(t, lw), :]
        out_swaps[r].start()
    og_pair.wait_all()
    R.oG[...] = (R.oG[...].astype(f32) + R.og_r[...].astype(f32)).astype(bf16)

    for line in (*token_lines, up_line, down_line, wo_line):
        line.done()
    for r in range(rows):
        kv_planes[r].done()

    def store_chunk(r, block):
        if not small:
            sync(R.kvc, R.kv.at[r, block])

    def own_kv(r, at, size):
        return R.pool.at[pl.ds(2 * lw * r + at, size), :]

    def dq_at(r, at, size):
        return R.pool.at[pl.ds(2 * lw * rows + lw * r + at, size), :]

    def prepare(r):
        grad_swaps[r].wait_all()
        for h in range(dm.heads):
            feats = pl.ds(HEAD_DIM * h, HEAD_DIM)
            R.delta[r, h : h + 1, :] = jnp.sum(R.doT[r, feats, :].astype(f32) * R.ctxr[r, feats, :], 0, keepdims=True)
        dq_at(r, 0, lw)[...] = jnp.zeros((lw, tok), f32)

    def attend_back(r, block, keep):
        bias = mask_bias(R.segg, r, block, b, tok)
        chunk = chunk_of(r, block)
        for h in range(dm.heads):
            feats = pl.ds(HEAD_DIM * h, HEAD_DIM)
            more = pl.ds(lw + HEAD_DIM * h, HEAD_DIM)
            k, v = chunk[feats, :], chunk[more, :]
            qh, do = R.qT[r, feats, :], R.doT[r, feats, :]
            p = jnp.exp(dot(k, qh, 0, 0) + bias - R.lse[r, h : h + 1, :])
            ds = (p * (dot(v, do, 0, 0) - R.delta[r, h : h + 1, :])).astype(bf16)
            dq_at(r, HEAD_DIM * h, HEAD_DIM)[...] += dot(k, ds, 1, 0)
            dk, dv = dot(qh, ds, 1, 1), dot(do, p.astype(bf16), 1, 1)
            if keep:
                own_kv(r, HEAD_DIM * h, HEAD_DIM)[...] = dk
                own_kv(r, lw + HEAD_DIM * h, HEAD_DIM)[...] = dv
            else:
                chunk[feats, :] = dk.astype(bf16)
                chunk[more, :] = dv.astype(bf16)
        if not keep:
            store_chunk(r, block)

    def back_far(r):
        prepare(r)
        if small:
            attend_back(r, b ^ 3, False)
            kv_folds[r].across(0).start()
            kv_folds[r].across(1).start()
        else:

            def body(k):
                attend_back(r, b ^ k, False)
                kv_folds[r].start_one(k)

            each(1, dm.nb, body)

    def back_near(r, half):
        if small:
            attend_back(r, b ^ (half + 1), False)
            kv_folds[r].near(half).start()

    def fold_kv(r):
        if small:
            kv_folds[r].fold(0)
            kv_folds[r].fold(1)

    def project_back(r):
        if small:
            for half in (0, 1):
                kv_folds[r].wait(half)
                own_kv(r, lw * half, lw)[...] += kv_folds[r].received(half)
        else:

            def add(k):
                kv_folds[r].wait(k)
                sync(R.dkv_r.at[r, b ^ k], R.kvc)
                own_kv(r, 0, 2 * lw)[...] += R.kvc[...].astype(f32)

            each(1, dm.nb, add)
        R.low_s[r, 0:lw, :] = (dq_at(r, 0, lw)[...] * HEAD_DIM**-0.5).astype(bf16)
        R.low_s[r, lw:, :] = own_kv(r, 0, 2 * lw)[...].astype(bf16)
        R.tp_s[r] = back_through(R.wN, R.low_s[r], lw).astype(bf16)
        R.tp_s[r, :, cut(t, pt)] = (back_through(R.wN, R.low_s[r, :, cut(t, pt)], lw) + R.frT[r]).astype(bf16)
        tok_folds[r].start()

    def weight_grads(r):
        ones = jnp.ones((16, tok), bf16)
        for n, m in ((0, 0), (1, 2)):
            sums = dot(ones, R.low_s[r, pl.ds(lw * m, lw), :], 1, 1)
            if r == 0:
                R.bv_s[0, n : n + 1, 0:lw] = sums[:1]
            else:
                R.bv_s[0, n : n + 1, 0:lw] += sums[:1]
        grads = dot(R.low_s[r], R.xT[r], 1, 1)
        if r == 0:
            R.w_acc[...] = grads
        else:
            R.w_acc[...] += grads

    def add_up(first, parts, n):
        result = first.astype(f32)
        for k in range(n):
            result = result + parts(k)
        return result

    def fold_first(n):
        first_stage[n].fold(0)
        first_stage[n].fold(1)

    def reduce_first(n):
        for half in (0, 1):
            first_stage[n].wait(half)
            part = parts[n](b, half)
            part[...] = (part[...].astype(f32) + first_stage[n].received(half)).astype(bf16)
        second_stage[n].start()

    def group_sum(ref, got):
        ref[...] = add_up(ref[...], lambda k: got[(b ^ (4 * (k + 1))) // 4].astype(f32), groups - 1).astype(bf16)

    def across_groups(swap, ref, got):
        if groups > 1:
            swap.start()
            swap.wait_all()
            swap.done()
            group_sum(ref, got)

    def others_sum(got):
        return lambda k: got[lax.rem(t + 1 + k, z)].astype(f32)

    def reduce_second(n):
        own = (
            lambda: R.uG[cut(q, dm.uq), cut(t, hf)],
            lambda: R.dG[t, cut(q, dm.dq), :],
            lambda: R.oG[t, cut(q, dm.oq), :],
        )[n]
        sums = (R.u_f, R.d_f, R.o_f)[n]
        sums[...] = own().astype(f32)

        def add(ref):
            sums[...] += ref[...].astype(f32)

        second_stage[n].finish(add)
        piece_refs[n][...] = sums[...].astype(bf16)
        across_groups(group_stage[n], piece_refs[n], group_refs[n])
        place_copies[n].start()
        third_stage[n].start()

    def tokens_out(r):
        R.tgT[r] = R.tp_s[r, cut(t, lw), :].astype(f32)

        def add(ref):
            R.tgT[r] += ref[...].astype(f32)

        tok_folds[r].finish(add)

    def add_vec(k):
        R.vs[1] += R.vb[b ^ k]

    def add_bias(k):
        R.bvF[...] += R.bvb[b ^ k]

    back_far(0)
    back_near(0, 0)
    back_near(0, 1)
    attend_back(0, b, True)
    vec_pair.wait_all()
    R.vs[0] = R.sv[...] + R.vp[...]
    vec_blk.start()
    back_far(1)
    fold_kv(0)
    reduce_first(1)
    back_near(1, 0)
    back_near(1, 1)
    second_stage[1].step(1)
    attend_back(1, b, True)
    send_first(0)
    fold_kv(1)
    second_stage[1].step(2)
    project_back(0)
    vec_blk.wait_all()
    R.vs[1] = R.vs[0]
    each(1, dm.nb, add_vec)
    vec_z.start()
    weight_grads(0)
    tok_folds[0].step(1)
    reduce_second(1)
    fold_first(0)
    project_back(1)
    send_first(2)
    tok_folds[0].step(2)
    weight_grads(1)
    R.wT[...] = R.w_acc[...].astype(bf16)
    w_pair.start()
    bv_pair.start()
    tok_folds[1].step(1)
    third_stage[1].forward()
    w_pair.wait_all()
    R.w1[...] = (R.w_acc[cut(c, half_w), :] + R.wR[...].astype(f32)).astype(bf16)
    w_blk.start()
    bv_pair.wait_all()
    R.bv_s[1] = R.bv_s[0] + R.bvp[...]
    bv_blk.start()
    fold_first(2)
    tokens_out(0)
    tok_folds[1].step(2)
    reduce_first(0)
    reduce_first(2)
    w_blk.wait_all()
    R.wP[...] = add_up(
        R.w1[cut(start_r, wq_r), cut(start_l, wq_l)], lambda k: R.wr[q ^ (k + 1)].astype(f32), 3
    ).astype(bf16)
    across_groups(w_group, R.wP, R.gw)
    w_place.start()
    w_plane.start()
    second_stage[0].step(1)
    second_stage[2].step(1)
    tokens_out(1)
    w_plane.forward()
    second_stage[0].step(2)
    second_stage[2].step(2)
    vec_z.wait_all()
    R.svF[...] = add_up(R.vs[1], others_sum(R.vz), z - 1)
    bv_blk.wait_all()
    R.bvF[...] = R.bv_s[1]
    each(1, dm.nb, add_bias)
    reduce_second(0)
    reduce_second(2)
    third_stage[0].forward()
    third_stage[2].forward()
    order = (
        (third_stage[1], place_copies[1], last_stage[1]),
        (w_plane, w_place, w_last),
        (third_stage[0], place_copies[0], last_stage[0]),
        (third_stage[2], place_copies[2], last_stage[2]),
    )
    for gather, copy, swap in order:
        copy.wait()
        gather.wait_all()
        swap.start()
    for _, _, swap in order:
        swap.wait_all()
    for swap in out_swaps:
        swap.wait_all()
    for transfer in (
        up_spread, down_spread, *ctx_swaps, cot_swap, ub_swap, seg_swap, wo_pair,
        hl_pair, feed_pair, fg_pair, part_pair, og_pair, *out_swaps, *grad_swaps,
        *first_stage, *second_stage, *third_stage, *last_stage, vec_pair, vec_blk, vec_z, bv_pair, bv_blk,
        *kv_folds, *tok_folds, w_pair, w_blk, w_plane, w_last,
    ):
        transfer.done()


def back_through(w, low, lw):
    return sum(dot(w[m], low[lw * m : lw * (m + 1)], 1, 0) for m in range(3))


def run_layer(dm, *inputs):
    shape = jax.ShapeDtypeStruct
    vmem, hbm = pl.BlockSpec(memory_space=pltpu.VMEM), pl.BlockSpec(memory_space=pl.ANY)
    V, rows, lw, tok, d, pt, own, z = pltpu.VMEM, dm.rows, dm.lw, dm.tok, dm.d, dm.pt, dm.own, dm.z
    small = dm.nb == 4
    both, half_h, half_z = 2 * own, dm.hid // 2, z // 2
    vectors = [f"vec{n}" for n in range(7)]
    in_names = ["tok", "seg", "w", "ib", "cot", *vectors, "up", "down", "wo"]
    outs = {
        "loT": ((rows, lw, tok), bf16, vmem),
        "tgT": ((rows, lw, tok), f32, vmem),
        "wF": ((dm.wr, d), bf16, hbm),
        "fu": ((d, dm.ff), bf16, hbm),
        "fd": ((dm.ff, d), bf16, hbm),
        "fo": ((lw, d), bf16, hbm),
        "svF": ((16, d), f32, vmem),
        "bvF": ((8, 256), f32, vmem),
    }
    kv, received = ((rows, dm.nb, 2 * lw, tok), bf16), ((rows, 3 if small else dm.nb, 2 * lw, tok), bf16)
    if not small:
        outs["kv"], outs["dkv_r"] = (*kv, hbm), (*received, hbm)
    scratch = {
        "xT": V((rows, d, tok), bf16),
        "wT": V((dm.wr, d), bf16),
        "wN": V((3, d, lw), bf16),
        "bcol": V((2, lw, 128), f32),
        "vec": V((8, d), f32),
        "qT": V((rows, lw, tok), bf16),
        "segg": V((dm.nb, 8, tok), jnp.int32),
        "m_s": V((rows, dm.heads, 8, tok), f32),
        "l_s": V((rows, dm.heads, 8, tok), f32),
        "acc": V((rows, dm.heads, HEAD_DIM, tok), f32),
        "ctxr": V((rows, lw, tok), f32),
        "ctxs": V((rows, lw, tok), bf16),
        "ctxT": V((rows, d, pt), bf16),
        "cotT": V((rows, d, pt), bf16),
        "lse": V((rows, 8, tok), f32),
        "ub8": V((8, dm.hf), f32),
        "ubH": V((8, dm.hid), f32),
        "upH": V((d, dm.hid), bf16),
        "downH": V((z, dm.hf, d), bf16),
        "woF": V((z, lw, d), bf16),
        "hl": V((both, d), bf16),
        "act": V((both, dm.hid), bf16),
        "bg": V((both, dm.hid), bf16),
        "pool": V((dm.hid // tok * both, tok), f32),
        "fgf": V((both, d), bf16),
        "fs_s": V((2, own, d), bf16),
        "fs_r": V((2, own, d), bf16),
        "z1_s": V((own, d), f32),
        "srg_s": V((own, d), f32),
        "outT": V((rows, d, pt), bf16),
        "cgT": V((rows, d, pt), bf16),
        "og_s": V((z, lw, dm.ol), bf16),
        "og_r": V((z, lw, dm.ol), bf16),
        "doT": V((rows, lw, tok), bf16),
        "frT": V((rows, d, pt), f32),
        "dG": V((z, dm.hf, d), bf16),
        "uG": V((d, dm.hid), bf16),
        "oG": V((z, lw, dm.ol), bf16),
        "sv": V((16, d), f32),
        "low_s": V((rows, 3 * lw, tok), bf16),
        "delta": V((rows, 8, tok), f32),
        "tp_s": V((rows, d, tok), bf16),
        "tp_r": V((rows, z + 1, lw, tok), bf16),
        "ur": V((6, dm.uq, half_h), bf16),
        "dr": V((6, half_z, dm.dq, d), bf16),
        "orr": V((6, half_z, dm.oq, dm.ol), bf16),
        "u2": V((z + 1, dm.uq, dm.hf), bf16),
        "d2": V((z + 1, dm.dq, d), bf16),
        "o2": V((z + 1, dm.oq, dm.ol), bf16),
        "u_f": V((dm.uq, dm.hf), f32),
        "d_f": V((dm.dq, d), f32),
        "o_f": V((dm.oq, dm.ol), f32),
        "uP": V((dm.uq, dm.hf), bf16),
        "dP": V((dm.dq, d), bf16),
        "oP": V((dm.oq, dm.ol), bf16),
        "wP": V((dm.wr // 4, d // 2), bf16),
        "vp": V((16, d), f32),
        "vb": V((dm.nb, 16, d), f32),
        "vz": V((z, 16, d), f32),
        "vs": V((2, 16, d), f32),
        "wR": V((dm.wr // 2, d), bf16),
        "w1": V((dm.wr // 2, d), bf16),
        "wr": V((4, dm.wr // 4, d // 2), bf16),
        "bv_s": V((2, 8, 256), f32),
        "bvp": V((8, 256), f32),
        "bvb": V((dm.nb, 8, 256), f32),
        "w_acc": V((dm.wr, d), f32),
        "gu": V((dm.nb // 4, dm.uq, dm.hf), bf16),
        "gd": V((dm.nb // 4, dm.dq, d), bf16),
        "go": V((dm.nb // 4, dm.oq, dm.ol), bf16),
        "gw": V((dm.nb // 4, dm.wr // 4, d // 2), bf16),
        "kvc": V((2 * lw, tok), bf16),
        "local": pltpu.SemaphoreType.DMA((8,)),
        "sems": pltpu.SemaphoreType.DMA((540 + 24 * dm.nb,)),
    }
    if small:
        scratch["kv"], scratch["dkv_r"] = V(*kv), V(*received)
    names = (*in_names, *outs, *scratch)
    return pl.pallas_call(
        functools.partial(layer_kernel, dm, names),
        name="encoder_layer",
        out_shape=[shape(s, dtype) for s, dtype, _ in outs.values()],
        in_specs=[vmem] * 12 + [hbm] * 3,
        out_specs=[spec for _, _, spec in outs.values()],
        scratch_shapes=list(scratch.values()),
        compiler_params=pltpu.CompilerParams(
            collective_id=0, has_side_effects=True, vmem_limit_bytes=VMEM_LIMIT
        ),
    )(*inputs)


def shards(
    mesh, tokens, segment_ids, input_weight, input_bias, output_weight, output_bias, first_gain, first_shift,
    up_weight, up_bias, down_weight, down_bias, second_gain, second_shift, cotangent,
):
    dm = Dims(mesh, *tokens.shape, up_weight.shape[1])
    tokT = jnp.transpose(tokens, (0, 2, 1))
    cotT = jnp.transpose(cotangent, (0, 2, 1))
    loT, tgT, wF, fu, fd, fo, svF, bvF, *_ = run_layer(
        dm, tokT, segment_ids, jnp.transpose(input_weight, (0, 2, 1)), input_bias, cotT,
        output_bias, first_gain, first_shift, down_bias, second_gain, second_shift, up_bias,
        up_weight, down_weight, output_weight,
    )
    low = write_outputs(dm, loT, tgT, wF, fu, fd, fo, svF, bvF)
    layer_output, tokens_grad, w_grad, out_w, up_w, down_w, bias, ub, *vectors = low
    second_gain_g, second_shift_g, down_b, first_gain_g, first_shift_g, out_b = vectors
    return (
        jnp.transpose(layer_output, (0, 2, 1)),
        jnp.transpose(tokens_grad, (0, 2, 1)),
        jnp.transpose(w_grad, (0, 2, 1)),
        bias,
        out_w,
        out_b,
        first_gain_g,
        first_shift_g,
        up_w,
        ub,
        down_w,
        down_b,
        second_gain_g,
        second_shift_g,
    )


def output_kernel(dm, loT, tgT, wF, fu, fd, fo, svF, bvF, lo, tg, w_o, fo_o, fu_o, fd_o, bias, ub, *vectors):
    lo[...] = loT[...]
    tg[...] = tgT[...]
    w_o[...] = wF[...].reshape(3, dm.lw, dm.d).astype(f32)
    fu_o[...] = fu[...].astype(f32)
    fd_o[...] = fd[...].astype(f32)
    fo_o[...] = fo[...].astype(f32)
    bias[...] = bvF[0:2, 0 : dm.lw]
    for n, ref in enumerate(vectors):
        ref[...] = svF[n, :]
    t = lax.axis_index("tensor")
    for half in range(2):
        row = svF[pl.ds(6 + 2 * half + lax.div(t, 2), 1), cut(lax.rem(t, 2), dm.hf)]
        ub[pl.ds(dm.hf * half, dm.hf)] = row.reshape(dm.hf)


def write_outputs(dm, *inputs):
    shape = jax.ShapeDtypeStruct
    vmem = pl.BlockSpec(memory_space=pltpu.VMEM)
    outs = [
        shape((dm.rows, dm.lw, dm.tok), bf16),
        shape((dm.rows, dm.lw, dm.tok), f32),
        shape((3, dm.lw, dm.d), f32),
        shape((dm.lw, dm.d), f32),
        shape((dm.d, dm.ff), f32),
        shape((dm.ff, dm.d), f32),
        shape((2, dm.lw), f32),
        shape((dm.ff,), f32),
        *[shape((dm.d,), f32)] * 6,
    ]
    return pl.pallas_call(
        functools.partial(output_kernel, dm),
        name="write_outputs",
        out_shape=outs,
        in_specs=[vmem] * len(inputs),
        out_specs=[vmem] * len(outs),
        compiler_params=pltpu.CompilerParams(vmem_limit_bytes=VMEM_LIMIT),
    )(*inputs)


def solution(mesh):
    rows = P("dp", "blk", "tensor")
    placed = (
        rows, P("dp", "blk"), P(None, None, "tensor"), P(None, "tensor"), P("tensor", None), P(), P(), P(),
        P(None, "tensor"), P("tensor"), P("tensor", None), P(), P(), P(), rows,
    )
    results = (
        rows, rows, P(None, None, "tensor"), P(None, "tensor"), P("tensor", None), P(), P(), P(),
        P(None, "tensor"), P("tensor"), P("tensor", None), P(), P(), P(),
    )
    return jax.shard_map(
        functools.partial(shards, mesh), mesh=mesh, in_specs=placed, out_specs=results, check_vma=False
    )
```

```python
import functools

import jax
import jax.numpy as jnp
from jax import lax
from jax.experimental import pallas as pl
from jax.experimental.pallas import tpu as pltpu
from jax.sharding import PartitionSpec as P

HEAD_DIM = 64
EPS = 1e-12
MASKED = -1e30
MESH = pl.DeviceIdType.MESH
bf16 = jnp.bfloat16
f32 = jnp.float32
VMEM_LIMIT = 60 * 2**20


def dot(a, b, ca, cb):
    return lax.dot_general(a, b, (((ca,), (cb,)), ((), ())), preferred_element_type=f32)


def aligned(index, size):
    return pl.multiple_of(index * size, size)


def cut(index, size):
    return pl.ds(aligned(index, size), size)


class Refs:
    def __init__(self, names, refs):
        for name, ref in zip(names, refs, strict=True):
            setattr(self, name, ref)


class Sems:
    def __init__(self, ref=None):
        self.ref = ref
        self.used = 0

    def take(self, count):
        first = self.used
        self.used += count
        return first


class Swap:
    def __init__(self, sems, axis, n, src, dst, xor=False, stride=1):
        self.sems, self.axis, self.n, self.src, self.dst, self.xor = sems, axis, n, src, dst, xor
        self.stride = stride
        self.me = lax.axis_index(axis)
        self.send, self.recv = sems.take(n), sems.take(n)

    def to(self, k):
        return self.me ^ (k * self.stride) if self.xor else lax.rem(self.me + k, self.n)

    def source(self, k):
        return self.me ^ (k * self.stride) if self.xor else lax.rem(self.me + self.n - k, self.n)

    def copy(self, k, dst_index):
        return pltpu.make_async_remote_copy(
            self.src(self.to(k)),
            self.dst(dst_index),
            self.sems.ref.at[self.send + k],
            self.sems.ref.at[self.recv + k],
            device_id={self.axis: self.to(k)},
            device_id_type=MESH,
        )

    def start_one(self, k):
        self.copy(k, self.me).start()

    def start(self):
        each(1, self.n, self.start_one)

    def wait(self, k):
        self.copy(k, self.source(k)).wait_recv()

    def wait_all(self):
        each(1, self.n, self.wait)

    def done(self):
        each(1, self.n, lambda k: self.copy(k, self.me).wait_send())


def each(low, high, body):
    if high - low <= 4:
        for k in range(low, high):
            body(k)
    else:

        def step(k, carry):
            body(k)
            return carry

        lax.fori_loop(low, high, step, 0)


class Line:
    def __init__(self, sems, n, view, own):
        self.sems, self.n, self.view, self.own = sems, n, view, own
        self.t = lax.axis_index("tensor")
        self.recv, self.right, self.left = sems.take(n), sems.take(n), sems.take(n)

    def copy(self, chunk, right, k):
        return pltpu.make_async_remote_copy(
            self.own if k == 0 else self.view(chunk),
            self.view(chunk),
            self.sems.ref.at[(self.right if right else self.left) + k],
            self.sems.ref.at[self.recv + chunk],
            device_id={"tensor": self.t + 1 if right else self.t - 1},
            device_id_type=MESH,
        )

    def start(self):
        t, n = self.t, self.n
        pl.when(t < n - 1)(lambda: self.copy(t, True, 0).start())
        pl.when(t > 0)(lambda: self.copy(t, False, 0).start())

    def step(self, k):
        t, n = self.t, self.n

        @pl.when(t >= k)
        def _():
            self.copy(t - k, True, k).wait_recv()
            pl.when(t < n - 1)(lambda: self.copy(t - k, True, k).start())

        @pl.when(t + k < n)
        def _():
            self.copy(t + k, False, k).wait_recv()
            pl.when(t > 0)(lambda: self.copy(t + k, False, k).start())

    def done(self):
        t, n = self.t, self.n
        for k in range(n):
            pl.when((t >= k) & (t < n - 1))(lambda k=k: self.copy(t - k, True, k).wait_send())
            pl.when((t + k < n) & (t > 0))(lambda k=k: self.copy(t + k, False, k).wait_send())


class Plane:
    def __init__(self, sems, n, view, own):
        self.sems, self.n, self.view, self.own = sems, n, view, own
        self.b = lax.axis_index("blk")
        self.send, self.recv = sems.take(2 * n), sems.take(2 * n)

    def copy(self, k, half, origin, to, own):
        return pltpu.make_async_remote_copy(
            self.own(half) if own else self.view(origin, half),
            self.view(origin, half),
            self.sems.ref.at[self.send + 2 * k + half],
            self.sems.ref.at[self.recv + 2 * k + half],
            device_id={"blk": to},
            device_id_type=MESH,
        )

    def ours(self, k, half):
        return self.copy(k, half, self.b, self.b ^ k, True)

    def passed(self, half):
        origin, to = (self.b ^ 1, self.b ^ 2) if half == 0 else (self.b ^ 2, self.b ^ 1)
        return self.copy(3, half, origin, to, False)

    def start(self):
        if self.n == 4:
            for k, half in ((1, 0), (2, 1), (1, 1), (2, 0)):
                self.ours(k, half).start()
        else:

            def go(k):
                self.ours(k, 0).start()
                self.ours(k, 1).start()

            each(1, self.n, go)

    def landed(self, k, half):
        self.copy(k, half, self.b ^ k, self.b ^ k, True).wait_recv()

    def forward(self):
        if self.n == 4:
            self.landed(1, 0)
            self.passed(0).start()
            self.landed(2, 1)
            self.passed(1).start()

    def wait(self, k):
        if self.n != 4:
            self.landed(k, 0)
            self.landed(k, 1)
        elif k == 1:
            self.landed(1, 1)
        elif k == 2:
            self.landed(2, 0)
        else:
            self.landed(3, 0)
            self.landed(3, 1)

    def wait_all(self):
        each(1, self.n, self.wait)

    def done(self):
        if self.n == 4:
            for k, half in ((1, 0), (2, 1), (1, 1), (2, 0)):
                self.ours(k, half).wait_send()
            self.passed(0).wait_send()
            self.passed(1).wait_send()
        else:

            def go(k):
                self.ours(k, 0).wait_send()
                self.ours(k, 1).wait_send()

            each(1, self.n, go)


class Spread:
    def __init__(self, sems, n, view):
        self.sems, self.n, self.view = sems, n, view
        self.b, self.t = lax.axis_index("blk"), lax.axis_index("tensor")
        self.send, self.recv = sems.take(8 * n), sems.take(8 * n)

    def copy(self, s, k, half, origin, to):
        ref = self.view(s, origin, half)
        return pltpu.make_async_remote_copy(
            ref,
            ref,
            self.sems.ref.at[self.send + 8 * s + 2 * k + half],
            self.sems.ref.at[self.recv + 8 * s + 2 * k + half],
            device_id={"blk": to},
            device_id_type=MESH,
        )

    def ours(self, s):
        return [self.copy(s, k, half, self.b, self.b ^ k) for k, half in ((1, 0), (2, 1), (1, 1), (2, 0))]

    def passed(self, s, half):
        near, far = (1, 2) if half == 0 else (2, 1)
        return self.copy(s, 3, half, self.b ^ near, self.b ^ far)

    def landed(self, s, k, half):
        self.copy(s, k, half, self.b ^ k, self.b ^ k).wait_recv()

    def around(self, k, body):
        pl.when(self.t >= k)(lambda: body(self.t - k))
        pl.when(self.t + k < self.n)(lambda: body(self.t + k))

    def start(self, k):
        def body(s):
            for copy in self.ours(s):
                copy.start()

        self.around(k, body)

    def forward(self, k):
        def body(s):
            self.landed(s, 1, 0)
            self.passed(s, 0).start()
            self.landed(s, 2, 1)
            self.passed(s, 1).start()

        self.around(k, body)

    def wait_all(self):
        def body(s):
            self.landed(s, 1, 1)
            self.landed(s, 2, 0)
            self.landed(s, 3, 0)
            self.landed(s, 3, 1)

        for k in range(1, self.n):
            self.around(k, body)

    def done(self):
        def body(s):
            for copy in (*self.ours(s), self.passed(s, 0), self.passed(s, 1)):
                copy.wait_send()

        for k in range(1, self.n):
            self.around(k, body)


class Fold:
    def __init__(self, sems, part, relay, inbox):
        self.sems, self.part, self.relay, self.inbox = sems, part, relay, inbox
        self.b = lax.axis_index("blk")
        self.send, self.recv = sems.take(6), sems.take(6)

    def copy(self, n, src, dst, k):
        return pltpu.make_async_remote_copy(
            src,
            dst,
            self.sems.ref.at[self.send + n],
            self.sems.ref.at[self.recv + n],
            device_id={"blk": self.b ^ k},
            device_id_type=MESH,
        )

    def across(self, half):
        return self.copy(half, self.part(self.b ^ 3, half), self.relay(half), half + 1)

    def near(self, half):
        return self.copy(2 + half, self.part(self.b ^ (half + 1), half), self.inbox(half), half + 1)

    def folded(self, half):
        return self.copy(4 + half, self.relay(half), self.inbox(2 + half), 2 - half)

    def fold(self, half):
        self.across(half).wait_recv()
        part, relay = self.part(self.b ^ (2 - half), half), self.relay(half)
        relay[...] = (part[...].astype(f32) + relay[...].astype(f32)).astype(bf16)
        self.folded(half).start()

    def wait(self, half):
        self.near(half).wait_recv()
        self.folded(half).wait_recv()

    def received(self, half):
        return self.inbox(half)[...].astype(f32) + self.inbox(2 + half)[...].astype(f32)

    def done(self):
        for half in (0, 1):
            for transfer in (self.across, self.near, self.folded):
                transfer(half).wait_send()


class LineFold:
    def __init__(self, sems, n, part, relay):
        self.sems, self.n, self.part, self.relay = sems, n, part, relay
        self.t = lax.axis_index("tensor")
        self.send, self.recv = sems.take(n), sems.take(n + 1)

    def copy(self, j, right, fresh):
        to = self.t + 1 if right else self.t - 1
        slot = j if right else jnp.where(j == to, self.n, j)
        return pltpu.make_async_remote_copy(
            self.part(j) if fresh else self.relay(j),
            self.relay(slot),
            self.sems.ref.at[self.send + j],
            self.sems.ref.at[self.recv + slot],
            device_id={"tensor": to},
            device_id_type=MESH,
        )

    def landed(self, slot):
        pltpu.make_async_remote_copy(
            self.relay(slot),
            self.relay(slot),
            self.sems.ref.at[self.send],
            self.sems.ref.at[self.recv + slot],
            device_id={"tensor": lax.rem(self.t + 1, self.n)},
            device_id_type=MESH,
        ).wait_recv()

    def start(self):
        n = self.n

        @pl.when(self.t == 0)
        def _():
            for j in range(n - 1, 0, -1):
                self.copy(j, True, True).start()

        @pl.when(self.t == n - 1)
        def _():
            for j in range(n - 1):
                self.copy(j, False, True).start()

    def pass_on(self, j, right):
        self.landed(j)
        relay, part = self.relay(j), self.part(j)
        relay[...] = (relay[...].astype(f32) + part[...].astype(f32)).astype(bf16)
        self.copy(j, right, False).start()

    def step(self, m):
        back = self.n - 1 - self.t
        pl.when((self.t >= 1) & (self.t <= m) & (back >= 1))(lambda: self.pass_on(self.n - 1 + self.t - m, True))
        pl.when((back >= 1) & (back <= m) & (self.t >= 1))(lambda: self.pass_on(m - back, False))

    def finish(self, store):
        @pl.when(self.t > 0)
        def _():
            self.landed(self.t)
            store(self.relay(self.t))

        @pl.when(self.t < self.n - 1)
        def _():
            self.landed(self.n)
            store(self.relay(self.n))

    def done(self):
        for j in range(self.n):
            pl.when(self.t < j)(lambda j=j: self.copy(j, True, False).wait_send())
            pl.when(self.t > j)(lambda j=j: self.copy(j, False, False).wait_send())


class Dims:
    def __init__(self, mesh, rows, tok, width, ff):
        self.z, self.nb, self.nc = mesh.shape["tensor"], mesh.shape["blk"], mesh.shape["dp"]
        self.rows, self.tok, self.lw, self.ff = rows, tok, width, ff
        self.d = width * self.z
        self.heads = width // HEAD_DIM
        self.pt = tok // self.z
        self.own = rows * self.pt
        self.hf = ff // 2
        self.hid = self.hf * self.z
        self.uq, self.dq, self.oq, self.ol = self.d // 4, self.hf // 4, width // 4, self.d // 2
        self.wr = 3 * width


def enter(dm, dp=True, blk=True, tensor=True):
    barrier = pltpu.get_barrier_semaphore()
    count = 0
    for axis, n, wanted in (("dp", dm.nc, dp), ("blk", dm.nb, blk), ("tensor", dm.z, tensor)):
        if not wanted:
            continue
        me = lax.axis_index(axis)

        def greet(k, axis=axis, n=n, me=me):
            pl.semaphore_signal(barrier, inc=1, device_id={axis: lax.rem(me + k, n)}, device_id_type=MESH)

        each(1, n, greet)
        count += n - 1
    pl.semaphore_wait(barrier, count)


def mask_bias(segg, r, key_block, own_block, tok):
    key_row = segg[key_block, r : r + 1, :]
    column = jnp.transpose(jnp.broadcast_to(key_row.astype(f32), (128, tok)))
    wide = jnp.concatenate([column] * (tok // 128), axis=1)
    query_row = segg[own_block, r : r + 1, :].astype(f32)
    return jnp.where(wide == query_row, 0.0, MASKED)


def layer_kernel(dm, names, *refs):
    R = Refs(names, refs)
    t, b, c = lax.axis_index("tensor"), lax.axis_index("blk"), lax.axis_index("dp")
    q = lax.rem(b, 4)
    sems = Sems(R.sems)
    rows, lw, pt, own, d, tok, hf, z = dm.rows, dm.lw, dm.pt, dm.own, dm.d, dm.tok, dm.hf, dm.z
    small = dm.nb == 4
    mine, other = cut(c, own), cut(1 - c, own)
    quarter = lambda i: lax.rem(i, 4)
    half_d, half_z, half_h = d // 2, z // 2, dm.hid // 2
    split_u, split_o = dm.uq // 2, 128

    def z_swap(src, dst):
        return Swap(sems, "tensor", z, src, dst)

    def pair(src, dst):
        return Swap(sems, "dp", dm.nc, src, dst)

    token_lines = [
        Line(sems, z, lambda i, r=r: R.xT.at[r, cut(i, lw), :], R.xT.at[r, cut(t, lw), :]) for r in range(rows)
    ]
    seg_swap = Swap(sems, "blk", dm.nb, lambda to: R.segg.at[b], lambda i: R.segg.at[i], xor=True)
    ub_swap = z_swap(lambda to: R.ub8, lambda i: R.ubH.at[:, cut(i, hf)])
    up_own = R.up.at[cut(q, dm.uq), cut(c, hf)]
    down_own = R.down.at[pl.ds(pl.multiple_of(hf * c + dm.dq * q, dm.dq), dm.dq), :]
    wo_own = R.wo.at[:, cut(c, dm.ol)]

    def up_piece(i):
        return R.upH.at[cut(q, dm.uq), cut(i, hf)]

    def down_piece(i):
        return R.downH.at[i, cut(q, dm.dq), :]

    def wo_piece(i):
        return R.woF.at[i, :, cut(c, dm.ol)]

    up_line = Line(sems, z, up_piece, up_own)
    down_line = Line(sems, z, down_piece, down_own)
    wo_line = Line(sems, z, wo_piece, wo_own)

    def up_view(s, i, half):
        start = pl.multiple_of(dm.uq * quarter(i) + split_u * half, split_u)
        return R.upH.at[pl.ds(start, split_u), cut(s, hf)]

    def down_view(s, i, half):
        return R.downH.at[s, cut(quarter(i), dm.dq), pl.ds(half_d * half, half_d)]

    up_spread, down_spread = Spread(sems, z, up_view), Spread(sems, z, down_view)
    wo_pair = pair(lambda to: R.woF.at[:, :, cut(c, dm.ol)], lambda i: R.woF.at[:, :, cut(i, dm.ol)])
    cot_swap = z_swap(lambda to: R.cot.at[:, :, cut(to, pt)], lambda i: R.cotT.at[:, cut(i, lw), :])
    kv_planes = [
        Plane(
            sems,
            dm.nb,
            lambda i, half, r=r: R.kv.at[r, i, pl.ds(lw * half, lw), :],
            lambda half, r=r: R.kv.at[r, b, pl.ds(lw * half, lw), :],
        )
        for r in range(rows)
    ]
    ctx_swaps = [
        z_swap(lambda to, r=r: R.ctxs.at[r, :, cut(to, pt)], lambda i, r=r: R.ctxT.at[r, cut(i, lw), :])
        for r in range(rows)
    ]
    hl_pair = pair(lambda to: R.hl.at[mine], lambda i: R.hl.at[cut(i, own)])
    feed_pair = pair(lambda to: R.fs_s.at[0], lambda i: R.fs_r.at[0])
    fg_pair = pair(lambda to: R.fgf.at[mine], lambda i: R.fgf.at[cut(i, own)])
    part_pair = pair(lambda to: R.fs_s.at[1], lambda i: R.fs_r.at[1])
    og_pair = pair(lambda to: R.og_s, lambda i: R.og_r)
    out_swaps = [
        z_swap(lambda to, r=r: R.outT.at[r, cut(to, lw), :], lambda i, r=r: R.loT.at[r, :, cut(i, pt)])
        for r in range(rows)
    ]
    grad_swaps = [
        z_swap(lambda to, r=r: R.cgT.at[r, cut(to, lw), :], lambda i, r=r: R.doT.at[r, :, cut(i, pt)])
        for r in range(rows)
    ]

    def u_part(i, half):
        return R.uG.at[cut(quarter(i), dm.uq), pl.ds(half_h * half, half_h)]

    def d_part(i, half):
        return R.dG.at[pl.ds(half_z * half, half_z), cut(quarter(i), dm.dq), :]

    def o_part(i, half):
        return R.oG.at[pl.ds(half_z * half, half_z), cut(quarter(i), dm.oq), :]

    parts = (u_part, d_part, o_part)
    first_stage = tuple(
        Fold(sems, part, lambda half, got=got: got.at[4 + half], lambda n, got=got: got.at[n])
        for part, got in zip(parts, (R.ur, R.dr, R.orr), strict=True)
    )
    second_stage = (
        LineFold(sems, z, lambda j: R.uG.at[cut(q, dm.uq), cut(j, hf)], lambda j: R.u2.at[j]),
        LineFold(sems, z, lambda j: R.dG.at[j, cut(q, dm.dq), :], lambda j: R.d2.at[j]),
        LineFold(sems, z, lambda j: R.oG.at[j, cut(q, dm.oq), :], lambda j: R.o2.at[j]),
    )
    groups = dm.nb // 4
    piece_refs, group_refs = (R.uP, R.dP, R.oP), (R.gu, R.gd, R.go)
    group_stage = tuple(
        Swap(sems, "blk", groups, lambda to, ref=ref: ref, lambda i, got=got: got.at[i // 4], True, 4)
        for ref, got in zip(piece_refs, group_refs, strict=True)
    )

    def fu_view(i, half):
        return R.fu.at[pl.ds(pl.multiple_of(dm.uq * quarter(i) + split_u * half, split_u), split_u), cut(c, hf)]

    def fd_view(i, half):
        start = pl.multiple_of(hf * c + dm.dq * quarter(i), dm.dq)
        return R.fd.at[pl.ds(start, dm.dq), pl.ds(half_d * half, half_d)]

    def fo_view(i, half):
        start = pl.multiple_of(dm.ol * c + split_o * half, 128)
        return R.fo.at[cut(quarter(i), dm.oq), pl.ds(start, dm.ol - split_o if half else split_o)]

    piece_halves = (
        lambda half: R.uP.at[pl.ds(split_u * half, split_u), :],
        lambda half: R.dP.at[:, pl.ds(half_d * half, half_d)],
        lambda half: R.oP.at[:, pl.ds(split_o * half, dm.ol - split_o if half else split_o)],
    )
    third_stage = tuple(
        Plane(sems, 4, view, piece) for view, piece in zip((fu_view, fd_view, fo_view), piece_halves, strict=True)
    )
    place = (
        R.fu.at[cut(q, dm.uq), cut(c, hf)],
        R.fd.at[pl.ds(pl.multiple_of(hf * c + dm.dq * q, dm.dq), dm.dq), :],
        R.fo.at[cut(q, dm.oq), cut(c, dm.ol)],
    )
    place_copies = [
        pltpu.make_async_copy(src, dst, R.local.at[4 + n])
        for n, (src, dst) in enumerate(zip(piece_refs, place, strict=True))
    ]
    last_stage = (
        pair(lambda to: R.fu.at[:, cut(c, hf)], lambda i: R.fu.at[:, cut(i, hf)]),
        pair(lambda to: R.fd.at[cut(c, hf), :], lambda i: R.fd.at[cut(i, hf), :]),
        pair(lambda to: R.fo.at[:, cut(c, dm.ol)], lambda i: R.fo.at[:, cut(i, dm.ol)]),
    )
    vec_pair = pair(lambda to: R.sv, lambda i: R.vp)
    vec_blk = Swap(sems, "blk", dm.nb, lambda to: R.vs.at[0], lambda i: R.vb.at[i], xor=True)
    vec_z = z_swap(lambda to: R.vs.at[1], lambda i: R.vz.at[i])
    bv_pair = pair(lambda to: R.bv_s.at[0], lambda i: R.bvp)
    bv_blk = Swap(sems, "blk", dm.nb, lambda to: R.bv_s.at[1], lambda i: R.bvb.at[i], xor=True)
    if small:
        kv_folds = [
            Fold(
                sems,
                lambda i, half, r=r: R.kv.at[r, i, pl.ds(lw * half, lw), :],
                lambda half, r=r: R.dkv_r.at[r, 2, pl.ds(lw * half, lw), :],
                lambda n, r=r: R.dkv_r.at[r, n // 2, pl.ds(lw * (n % 2), lw), :],
            )
            for r in range(rows)
        ]
    else:
        kv_folds = [
            Swap(sems, "blk", dm.nb, lambda to, r=r: R.kv.at[r, to], lambda i, r=r: R.dkv_r.at[r, i], xor=True)
            for r in range(rows)
        ]
    tok_folds = [
        LineFold(sems, z, lambda j, r=r: R.tp_s.at[r, cut(j, lw), :], lambda j, r=r: R.tp_r.at[r, j])
        for r in range(rows)
    ]
    half_w, wq_r, wq_l = dm.wr // 2, dm.wr // 4, d // 2
    w_pair = pair(lambda to: R.wT.at[cut(to, half_w), :], lambda i: R.wR)

    def w_at(i):
        return lax.div(quarter(i), 2), lax.rem(i, 2)

    w_blk = Swap(
        sems, "blk", 4,
        lambda to: R.w1.at[cut(w_at(to)[0], wq_r), cut(w_at(to)[1], wq_l)],
        lambda i: R.wr.at[quarter(i)], xor=True,
    )
    w_split = 80

    def wf_view(i, half):
        start = pl.multiple_of(half_w * c + wq_r * w_at(i)[0] + w_split * half, 16)
        return R.wF.at[pl.ds(start, wq_r - w_split if half else w_split), cut(w_at(i)[1], wq_l)]

    start_r, start_l = w_at(b)
    w_group = Swap(sems, "blk", groups, lambda to: R.wP, lambda i: R.gw.at[i // 4], True, 4)
    w_plane = Plane(
        sems, 4, wf_view, lambda half: R.wP.at[pl.ds(w_split * half, wq_r - w_split if half else w_split), :]
    )
    w_place = pltpu.make_async_copy(
        R.wP,
        R.wF.at[pl.ds(pl.multiple_of(half_w * c + wq_r * start_r, 16), wq_r), cut(start_l, wq_l)],
        R.local.at[7],
    )
    w_last = pair(lambda to: R.wF.at[cut(c, half_w), :], lambda i: R.wF.at[cut(i, half_w), :])

    def sync(src, dst):
        copy = pltpu.make_async_copy(src, dst, R.local.at[3])
        copy.start()
        copy.wait()

    def chunk_of(r, block):
        if small:
            return R.kv.at[r, block]
        sync(R.kv.at[r, block], R.kvc)
        return R.kvc

    def project(r):
        y = dot(R.w[...].reshape(dm.wr, d), R.xT[r], 1, 0)
        R.qT[r] = (y[:lw] + R.bcol[0][:, :1]).astype(bf16) * bf16(HEAD_DIM**-0.5)
        chunk = R.kv.at[r, b] if small else R.kvc
        chunk[0:lw, :] = y[lw : 2 * lw].astype(bf16)
        chunk[lw : 2 * lw, :] = (y[2 * lw :] + R.bcol[1][:, :1]).astype(bf16)
        if not small:
            sync(R.kvc, R.kv.at[r, b])
        for h in range(dm.heads):
            R.m_s[r, h] = jnp.full((8, tok), MASKED, f32)
            R.l_s[r, h] = jnp.zeros((8, tok), f32)
            R.acc[r, h] = jnp.zeros((HEAD_DIM, tok), f32)
        kv_planes[r].start()

    def attend(r, block):
        bias = mask_bias(R.segg, r, block, b, tok)
        chunk = chunk_of(r, block)
        for h in range(dm.heads):
            k = chunk[pl.ds(HEAD_DIM * h, HEAD_DIM), :]
            v = chunk[pl.ds(lw + HEAD_DIM * h, HEAD_DIM), :]
            s = dot(k, R.qT[r, pl.ds(HEAD_DIM * h, HEAD_DIM), :], 0, 0) + bias
            old = R.m_s[r, h, :1]
            new = jnp.maximum(old, jnp.max(s, 0, keepdims=True))
            p = jnp.exp(s - new)
            scale = jnp.exp(old - new)
            R.l_s[r, h, :1] = R.l_s[r, h, :1] * scale + jnp.sum(p, 0, keepdims=True)
            R.m_s[r, h, :1] = new
            R.acc[r, h] = R.acc[r, h] * scale + dot(v, p.astype(bf16), 1, 0)

    def attend_near(r, k):
        if small:
            kv_planes[r].wait(k)
            attend(r, b ^ k)

    def attend_rest(r):
        if not small:

            def body(k):
                kv_planes[r].wait(k)
                attend(r, b ^ k)

            each(1, dm.nb, body)

    def finish(r):
        for h in range(dm.heads):
            denominator = R.l_s[r, h, :1]
            ctx = R.acc[r, h] / denominator
            R.ctxr[r, pl.ds(HEAD_DIM * h, HEAD_DIM), :] = ctx
            R.ctxs[r, pl.ds(HEAD_DIM * h, HEAD_DIM), :] = ctx.astype(bf16)
            R.lse[r, h : h + 1, :] = R.m_s[r, h, :1] + jnp.log(denominator)
        R.ctxT[r, cut(t, lw), :] = R.ctxs[r, :, cut(t, pt)]
        ctx_swaps[r].start()

    enter(dm)
    for r in range(rows):
        R.xT[r, cut(t, lw), :] = R.tok[r]
    token_lines[0].start()
    up_line.start()
    weight_copies = [
        pltpu.make_async_copy(src, dst, R.local.at[n])
        for n, (src, dst) in enumerate(
            (
                (R.up.at[:, cut(c, hf)], R.upH.at[:, cut(t, hf)]),
                (R.down.at[cut(c, hf), :], R.downH.at[t]),
                (wo_own, wo_piece(t)),
            )
        )
    ]
    for copy in weight_copies:
        copy.start()
    for r in range(rows):
        R.cotT[r, cut(t, lw), :] = R.cot[r, :, cut(t, pt)]
    for m in range(3):
        R.wN[m] = jnp.transpose(R.w[m])
    R.segg[b] = jnp.zeros((8, tok), jnp.int32)
    R.segg[b, 0:rows, :] = R.seg[...]
    seg_swap.start()
    for n in range(7):
        R.vec[n, :] = getattr(R, f"vec{n}")[...]
    for n in range(2):
        R.bcol[n] = jnp.transpose(jnp.broadcast_to(R.ib[n : n + 1, :], (128, lw)))
    R.ub8[...] = jnp.broadcast_to(R.vec[6:7, cut(c, hf)], (8, hf))
    R.ubH[:, cut(t, hf)] = R.ub8[...]
    ub_swap.start()

    token_lines[0].step(1)
    up_line.step(1)
    up_spread.start(1)
    token_lines[0].step(2)
    token_lines[1].start()
    up_line.step(2)
    up_spread.start(2)
    token_lines[0].step(3)
    project(0)
    up_line.step(3)
    up_spread.start(3)
    up_spread.forward(1)
    token_lines[1].step(1)
    wo_line.start()
    seg_swap.wait_all()
    attend(0, b)
    up_spread.forward(2)
    token_lines[1].step(2)
    down_line.start()
    kv_planes[0].forward()
    up_spread.forward(3)
    wo_line.step(1)
    token_lines[1].step(3)
    project(1)
    wo_line.step(2)
    down_line.step(1)
    down_spread.start(1)
    attend(1, b)
    wo_line.step(3)
    for copy in weight_copies:
        copy.wait()
    wo_pair.start()
    attend_near(0, 1)
    down_line.step(2)
    down_spread.start(2)
    attend_near(0, 2)
    down_line.step(3)
    down_spread.start(3)
    attend_near(0, 3)
    attend_rest(0)
    finish(0)
    kv_planes[1].forward()
    attend_near(1, 1)
    down_spread.forward(1)
    attend_near(1, 2)
    down_spread.forward(2)
    attend_near(1, 3)
    attend_rest(1)
    finish(1)
    cot_swap.start()
    down_spread.forward(3)

    out_b, g1, s1, down_b, g2, s2 = (R.vec[n : n + 1, :] for n in range(6))

    def stats(x):
        center = x - jnp.mean(x, -1, keepdims=True)
        inverse = lax.rsqrt(jnp.mean(center * center, -1, keepdims=True) + EPS)
        return center * inverse, inverse

    def norm_back(g, gain, zn, inverse):
        e = g * gain
        return (e - jnp.mean(e, -1, keepdims=True) - zn * jnp.mean(e * zn, -1, keepdims=True)) * inverse

    def total(x):
        return jnp.sum(x, 0, keepdims=True)

    blocks = dm.hid // tok

    inverse1 = []
    wo_pair.wait_all()
    for r in range(rows):
        ctx_swaps[r].wait_all()
        attended = dot(R.ctxT[r], R.woF[...].reshape(d, d), 0, 0) + out_b
        zn, inv = stats(jnp.transpose(R.xT[r, :, cut(t, pt)].astype(f32)) + attended)
        inverse1.append(inv)
        R.z1_s[pl.ds(pt * r, pt), :] = zn
        R.hl[pl.ds(pl.multiple_of(own * c + pt * r, pt), pt), :] = (zn * g1 + s1).astype(bf16)
    hl_pair.start()
    ub_swap.wait_all()

    def expand(core):
        part = cut(core, own)
        for n in range(blocks):
            cols = pl.ds(tok * n, tok)
            v = dot(R.hl[part, :], R.upH[:, cols], 1, 0) + R.ubH[:1, cols]
            phi = 0.5 + 0.5 * lax.erf(v * (0.5**0.5))
            R.act[part, cols] = (v * phi).astype(bf16)
            R.pool[cut(2 * n + core, own), :] = phi + v * (jnp.exp(-0.5 * v * v) * 0.3989422804014327)

    up_spread.wait_all()
    expand(c)
    hl_pair.wait_all()
    expand(1 - c)
    down_spread.wait_all()
    down_w = R.downH[...].reshape(dm.hid, d)
    R.fs_s[0] = dot(R.act[other, :], down_w, 1, 0).astype(bf16)
    feed_pair.start()
    feed = dot(R.act[mine, :], down_w, 1, 0) + down_b
    cot_swap.wait_all()
    g = jnp.concatenate([jnp.transpose(R.cotT[r].astype(f32)) for r in range(rows)], 0)
    feed_pair.wait_all()
    hidden = R.z1_s[...] * g1 + s1
    z2, inverse2 = stats(hidden + (feed + R.fs_r[0].astype(f32)))
    resid = norm_back(g, g2, z2, inverse2)
    R.srg_s[...] = resid
    low = resid.astype(bf16)
    R.fgf[mine, :] = low
    fg_pair.start()
    out = z2 * g2 + s2
    R.sv[...] = jnp.zeros_like(R.sv)
    R.sv[0:1, :] = total(g * z2)
    R.sv[1:2, :] = total(g)
    R.sv[2:3, :] = total(low.astype(f32))

    def contract(core):
        part = cut(core, own)
        for n in range(blocks):
            cols = pl.ds(tok * n, tok)
            grad = dot(R.fgf[part, :], R.downH[...].reshape(dm.hid, d)[tok * n : tok * (n + 1)], 1, 1)
            R.bg[part, cols] = (grad * R.pool[cut(2 * n + core, own), :]).astype(bf16)

    def send_first(n):
        for half in (0, 1):
            first_stage[n].across(half).start()
        for half in (0, 1):
            first_stage[n].near(half).start()

    contract(c)
    fg_pair.wait_all()
    for n in range(z):
        R.dG[n] = dot(R.act[:, pl.ds(hf * n, hf)], R.fgf[...], 0, 0).astype(bf16)
    send_first(1)
    contract(1 - c)
    R.fs_s[1] = dot(R.bg[other, :], R.upH[...], 1, 1).astype(bf16)
    part_pair.start()
    part = dot(R.bg[mine, :], R.upH[...], 1, 1)
    for n in range(blocks):
        cols = pl.ds(tok * n, tok)
        R.uG[:, cols] = dot(R.hl[...], R.bg[:, cols], 0, 0).astype(bf16)
    part_pair.wait_all()
    hidden_grad = R.srg_s[...] + (part + R.fs_r[1].astype(f32))
    z1 = R.z1_s[...]
    first = norm_back(hidden_grad, g1, z1, jnp.concatenate(inverse1, 0))
    low = first.astype(bf16)
    for r in range(rows):
        R.cgT[r] = dot(R.woF[...].reshape(d, d), low[pt * r : pt * (r + 1)], 1, 1).astype(bf16)
        R.doT[r, :, cut(t, pt)] = R.cgT[r, cut(t, lw), :]
        grad_swaps[r].start()
        R.frT[r] = jnp.transpose(first[pt * r : pt * (r + 1)])
    first_stage[1].fold(0)
    first_stage[1].fold(1)
    out_grad = sum(dot(R.ctxT[r], low[pt * r : pt * (r + 1)], 1, 0) for r in range(rows))
    left = out_grad[:, : dm.ol].reshape(z, lw, dm.ol)
    right = out_grad[:, dm.ol :].reshape(z, lw, dm.ol)
    R.oG[...] = jnp.where(c == 0, left, right).astype(bf16)
    R.og_s[...] = jnp.where(c == 0, right, left).astype(bf16)
    og_pair.start()
    R.sv[3:4, :] = total(hidden_grad * z1)
    R.sv[4:5, :] = total(hidden_grad)
    R.sv[5:6, :] = total(low.astype(f32))
    for n in range(z):
        R.sv[pl.ds(6 + 2 * c + n // 2, 1), pl.ds(hf * (n % 2), hf)] = total(
            R.bg[:, pl.ds(hf * n, hf)].astype(f32)
        )
    vec_pair.start()
    for r in range(rows):
        R.outT[r] = jnp.transpose(out[pt * r : pt * (r + 1)]).astype(bf16)
        R.loT[r, :, cut(t, pt)] = R.outT[r, cut(t, lw), :]
        out_swaps[r].start()
    og_pair.wait_all()
    R.oG[...] = (R.oG[...].astype(f32) + R.og_r[...].astype(f32)).astype(bf16)

    for line in (*token_lines, up_line, down_line, wo_line):
        line.done()
    for r in range(rows):
        kv_planes[r].done()

    def store_chunk(r, block):
        if not small:
            sync(R.kvc, R.kv.at[r, block])

    def own_kv(r, at, size):
        return R.pool.at[pl.ds(2 * lw * r + at, size), :]

    def dq_at(r, at, size):
        return R.pool.at[pl.ds(2 * lw * rows + lw * r + at, size), :]

    def prepare(r):
        grad_swaps[r].wait_all()
        for h in range(dm.heads):
            feats = pl.ds(HEAD_DIM * h, HEAD_DIM)
            R.delta[r, h : h + 1, :] = jnp.sum(R.doT[r, feats, :].astype(f32) * R.ctxr[r, feats, :], 0, keepdims=True)
        dq_at(r, 0, lw)[...] = jnp.zeros((lw, tok), f32)

    def attend_back(r, block, keep):
        bias = mask_bias(R.segg, r, block, b, tok)
        chunk = chunk_of(r, block)
        for h in range(dm.heads):
            feats = pl.ds(HEAD_DIM * h, HEAD_DIM)
            more = pl.ds(lw + HEAD_DIM * h, HEAD_DIM)
            k, v = chunk[feats, :], chunk[more, :]
            qh, do = R.qT[r, feats, :], R.doT[r, feats, :]
            p = jnp.exp(dot(k, qh, 0, 0) + bias - R.lse[r, h : h + 1, :])
            ds = (p * (dot(v, do, 0, 0) - R.delta[r, h : h + 1, :])).astype(bf16)
            dq_at(r, HEAD_DIM * h, HEAD_DIM)[...] += dot(k, ds, 1, 0)
            dk, dv = dot(qh, ds, 1, 1), dot(do, p.astype(bf16), 1, 1)
            if keep:
                own_kv(r, HEAD_DIM * h, HEAD_DIM)[...] = dk
                own_kv(r, lw + HEAD_DIM * h, HEAD_DIM)[...] = dv
            else:
                chunk[feats, :] = dk.astype(bf16)
                chunk[more, :] = dv.astype(bf16)
        if not keep:
            store_chunk(r, block)

    def back_far(r):
        prepare(r)
        if small:
            attend_back(r, b ^ 3, False)
            kv_folds[r].across(0).start()
            kv_folds[r].across(1).start()
        else:

            def body(k):
                attend_back(r, b ^ k, False)
                kv_folds[r].start_one(k)

            each(1, dm.nb, body)

    def back_near(r, half):
        if small:
            attend_back(r, b ^ (half + 1), False)
            kv_folds[r].near(half).start()

    def fold_kv(r):
        if small:
            kv_folds[r].fold(0)
            kv_folds[r].fold(1)

    def project_back(r):
        if small:
            for half in (0, 1):
                kv_folds[r].wait(half)
                own_kv(r, lw * half, lw)[...] += kv_folds[r].received(half)
        else:

            def add(k):
                kv_folds[r].wait(k)
                sync(R.dkv_r.at[r, b ^ k], R.kvc)
                own_kv(r, 0, 2 * lw)[...] += R.kvc[...].astype(f32)

            each(1, dm.nb, add)
        R.low_s[r, 0:lw, :] = (dq_at(r, 0, lw)[...] * HEAD_DIM**-0.5).astype(bf16)
        R.low_s[r, lw:, :] = own_kv(r, 0, 2 * lw)[...].astype(bf16)
        R.tp_s[r] = back_through(R.wN, R.low_s[r], lw).astype(bf16)
        R.tp_s[r, :, cut(t, pt)] = (back_through(R.wN, R.low_s[r, :, cut(t, pt)], lw) + R.frT[r]).astype(bf16)
        tok_folds[r].start()

    def weight_grads(r):
        ones = jnp.ones((16, tok), bf16)
        for n, m in ((0, 0), (1, 2)):
            sums = dot(ones, R.low_s[r, pl.ds(lw * m, lw), :], 1, 1)
            if r == 0:
                R.bv_s[0, n : n + 1, 0:lw] = sums[:1]
            else:
                R.bv_s[0, n : n + 1, 0:lw] += sums[:1]
        grads = dot(R.low_s[r], R.xT[r], 1, 1)
        if r == 0:
            R.w_acc[...] = grads
        else:
            R.w_acc[...] += grads

    def add_up(first, parts, n):
        result = first.astype(f32)
        for k in range(n):
            result = result + parts(k)
        return result

    def fold_first(n):
        first_stage[n].fold(0)
        first_stage[n].fold(1)

    def reduce_first(n):
        for half in (0, 1):
            first_stage[n].wait(half)
            part = parts[n](b, half)
            part[...] = (part[...].astype(f32) + first_stage[n].received(half)).astype(bf16)
        second_stage[n].start()

    def group_sum(ref, got):
        ref[...] = add_up(ref[...], lambda k: got[(b ^ (4 * (k + 1))) // 4].astype(f32), groups - 1).astype(bf16)

    def across_groups(swap, ref, got):
        if groups > 1:
            swap.start()
            swap.wait_all()
            swap.done()
            group_sum(ref, got)

    def others_sum(got):
        return lambda k: got[lax.rem(t + 1 + k, z)].astype(f32)

    def reduce_second(n):
        own = (
            lambda: R.uG[cut(q, dm.uq), cut(t, hf)],
            lambda: R.dG[t, cut(q, dm.dq), :],
            lambda: R.oG[t, cut(q, dm.oq), :],
        )[n]
        sums = (R.u_f, R.d_f, R.o_f)[n]
        sums[...] = own().astype(f32)

        def add(ref):
            sums[...] += ref[...].astype(f32)

        second_stage[n].finish(add)
        piece_refs[n][...] = sums[...].astype(bf16)
        across_groups(group_stage[n], piece_refs[n], group_refs[n])
        place_copies[n].start()
        third_stage[n].start()

    def tokens_out(r):
        R.tgT[r] = R.tp_s[r, cut(t, lw), :].astype(f32)

        def add(ref):
            R.tgT[r] += ref[...].astype(f32)

        tok_folds[r].finish(add)

    def add_vec(k):
        R.vs[1] += R.vb[b ^ k]

    def add_bias(k):
        R.bvF[...] += R.bvb[b ^ k]

    back_far(0)
    back_near(0, 0)
    back_near(0, 1)
    attend_back(0, b, True)
    vec_pair.wait_all()
    R.vs[0] = R.sv[...] + R.vp[...]
    vec_blk.start()
    back_far(1)
    fold_kv(0)
    reduce_first(1)
    back_near(1, 0)
    back_near(1, 1)
    second_stage[1].step(1)
    send_first(0)
    attend_back(1, b, True)
    fold_kv(1)
    send_first(2)
    second_stage[1].step(2)
    project_back(0)
    vec_blk.wait_all()
    R.vs[1] = R.vs[0]
    each(1, dm.nb, add_vec)
    vec_z.start()
    weight_grads(0)
    tok_folds[0].step(1)
    reduce_second(1)
    fold_first(0)
    project_back(1)
    tok_folds[0].step(2)
    weight_grads(1)
    R.wT[...] = R.w_acc[...].astype(bf16)
    w_pair.start()
    bv_pair.start()
    tok_folds[1].step(1)
    third_stage[1].forward()
    w_pair.wait_all()
    R.w1[...] = (R.w_acc[cut(c, half_w), :] + R.wR[...].astype(f32)).astype(bf16)
    w_blk.start()
    bv_pair.wait_all()
    R.bv_s[1] = R.bv_s[0] + R.bvp[...]
    bv_blk.start()
    fold_first(2)
    tokens_out(0)
    tok_folds[1].step(2)
    reduce_first(0)
    reduce_first(2)
    w_blk.wait_all()
    R.wP[...] = add_up(
        R.w1[cut(start_r, wq_r), cut(start_l, wq_l)], lambda k: R.wr[q ^ (k + 1)].astype(f32), 3
    ).astype(bf16)
    across_groups(w_group, R.wP, R.gw)
    w_place.start()
    w_plane.start()
    second_stage[0].step(1)
    second_stage[2].step(1)
    tokens_out(1)
    w_plane.forward()
    second_stage[0].step(2)
    second_stage[2].step(2)
    vec_z.wait_all()
    R.svF[...] = add_up(R.vs[1], others_sum(R.vz), z - 1)
    bv_blk.wait_all()
    R.bvF[...] = R.bv_s[1]
    each(1, dm.nb, add_bias)
    reduce_second(0)
    reduce_second(2)
    third_stage[0].forward()
    third_stage[2].forward()
    order = (
        (third_stage[1], place_copies[1], last_stage[1]),
        (w_plane, w_place, w_last),
        (third_stage[0], place_copies[0], last_stage[0]),
        (third_stage[2], place_copies[2], last_stage[2]),
    )
    for gather, copy, swap in order:
        copy.wait()
        gather.wait_all()
        swap.start()
    for _, _, swap in order:
        swap.wait_all()
    for swap in out_swaps:
        swap.wait_all()
    for transfer in (
        up_spread, down_spread, *ctx_swaps, cot_swap, ub_swap, seg_swap, wo_pair,
        hl_pair, feed_pair, fg_pair, part_pair, og_pair, *out_swaps, *grad_swaps,
        *first_stage, *second_stage, *third_stage, *last_stage, vec_pair, vec_blk, vec_z, bv_pair, bv_blk,
        *kv_folds, *tok_folds, w_pair, w_blk, w_plane, w_last,
    ):
        transfer.done()


def back_through(w, low, lw):
    return sum(dot(w[m], low[lw * m : lw * (m + 1)], 1, 0) for m in range(3))


def run_layer(dm, *inputs):
    shape = jax.ShapeDtypeStruct
    vmem, hbm = pl.BlockSpec(memory_space=pltpu.VMEM), pl.BlockSpec(memory_space=pl.ANY)
    V, rows, lw, tok, d, pt, own, z = pltpu.VMEM, dm.rows, dm.lw, dm.tok, dm.d, dm.pt, dm.own, dm.z
    small = dm.nb == 4
    both, half_h, half_z = 2 * own, dm.hid // 2, z // 2
    vectors = [f"vec{n}" for n in range(7)]
    in_names = ["tok", "seg", "w", "ib", "cot", *vectors, "up", "down", "wo"]
    outs = {
        "loT": ((rows, lw, tok), bf16, vmem),
        "tgT": ((rows, lw, tok), f32, vmem),
        "wF": ((dm.wr, d), bf16, hbm),
        "fu": ((d, dm.ff), bf16, hbm),
        "fd": ((dm.ff, d), bf16, hbm),
        "fo": ((lw, d), bf16, hbm),
        "svF": ((16, d), f32, vmem),
        "bvF": ((8, 256), f32, vmem),
    }
    kv, received = ((rows, dm.nb, 2 * lw, tok), bf16), ((rows, 3 if small else dm.nb, 2 * lw, tok), bf16)
    if not small:
        outs["kv"], outs["dkv_r"] = (*kv, hbm), (*received, hbm)
    scratch = {
        "xT": V((rows, d, tok), bf16),
        "wT": V((dm.wr, d), bf16),
        "wN": V((3, d, lw), bf16),
        "bcol": V((2, lw, 128), f32),
        "vec": V((8, d), f32),
        "qT": V((rows, lw, tok), bf16),
        "segg": V((dm.nb, 8, tok), jnp.int32),
        "m_s": V((rows, dm.heads, 8, tok), f32),
        "l_s": V((rows, dm.heads, 8, tok), f32),
        "acc": V((rows, dm.heads, HEAD_DIM, tok), f32),
        "ctxr": V((rows, lw, tok), f32),
        "ctxs": V((rows, lw, tok), bf16),
        "ctxT": V((rows, d, pt), bf16),
        "cotT": V((rows, d, pt), bf16),
        "lse": V((rows, 8, tok), f32),
        "ub8": V((8, dm.hf), f32),
        "ubH": V((8, dm.hid), f32),
        "upH": V((d, dm.hid), bf16),
        "downH": V((z, dm.hf, d), bf16),
        "woF": V((z, lw, d), bf16),
        "hl": V((both, d), bf16),
        "act": V((both, dm.hid), bf16),
        "bg": V((both, dm.hid), bf16),
        "pool": V((dm.hid // tok * both, tok), f32),
        "fgf": V((both, d), bf16),
        "fs_s": V((2, own, d), bf16),
        "fs_r": V((2, own, d), bf16),
        "z1_s": V((own, d), f32),
        "srg_s": V((own, d), f32),
        "outT": V((rows, d, pt), bf16),
        "cgT": V((rows, d, pt), bf16),
        "og_s": V((z, lw, dm.ol), bf16),
        "og_r": V((z, lw, dm.ol), bf16),
        "doT": V((rows, lw, tok), bf16),
        "frT": V((rows, d, pt), f32),
        "dG": V((z, dm.hf, d), bf16),
        "uG": V((d, dm.hid), bf16),
        "oG": V((z, lw, dm.ol), bf16),
        "sv": V((16, d), f32),
        "low_s": V((rows, 3 * lw, tok), bf16),
        "delta": V((rows, 8, tok), f32),
        "tp_s": V((rows, d, tok), bf16),
        "tp_r": V((rows, z + 1, lw, tok), bf16),
        "ur": V((6, dm.uq, half_h), bf16),
        "dr": V((6, half_z, dm.dq, d), bf16),
        "orr": V((6, half_z, dm.oq, dm.ol), bf16),
        "u2": V((z + 1, dm.uq, dm.hf), bf16),
        "d2": V((z + 1, dm.dq, d), bf16),
        "o2": V((z + 1, dm.oq, dm.ol), bf16),
        "u_f": V((dm.uq, dm.hf), f32),
        "d_f": V((dm.dq, d), f32),
        "o_f": V((dm.oq, dm.ol), f32),
        "uP": V((dm.uq, dm.hf), bf16),
        "dP": V((dm.dq, d), bf16),
        "oP": V((dm.oq, dm.ol), bf16),
        "wP": V((dm.wr // 4, d // 2), bf16),
        "vp": V((16, d), f32),
        "vb": V((dm.nb, 16, d), f32),
        "vz": V((z, 16, d), f32),
        "vs": V((2, 16, d), f32),
        "wR": V((dm.wr // 2, d), bf16),
        "w1": V((dm.wr // 2, d), bf16),
        "wr": V((4, dm.wr // 4, d // 2), bf16),
        "bv_s": V((2, 8, 256), f32),
        "bvp": V((8, 256), f32),
        "bvb": V((dm.nb, 8, 256), f32),
        "w_acc": V((dm.wr, d), f32),
        "gu": V((dm.nb // 4, dm.uq, dm.hf), bf16),
        "gd": V((dm.nb // 4, dm.dq, d), bf16),
        "go": V((dm.nb // 4, dm.oq, dm.ol), bf16),
        "gw": V((dm.nb // 4, dm.wr // 4, d // 2), bf16),
        "kvc": V((2 * lw, tok), bf16),
        "local": pltpu.SemaphoreType.DMA((8,)),
        "sems": pltpu.SemaphoreType.DMA((540 + 24 * dm.nb,)),
    }
    if small:
        scratch["kv"], scratch["dkv_r"] = V(*kv), V(*received)
    names = (*in_names, *outs, *scratch)
    return pl.pallas_call(
        functools.partial(layer_kernel, dm, names),
        name="encoder_layer",
        out_shape=[shape(s, dtype) for s, dtype, _ in outs.values()],
        in_specs=[vmem] * 12 + [hbm] * 3,
        out_specs=[spec for _, _, spec in outs.values()],
        scratch_shapes=list(scratch.values()),
        compiler_params=pltpu.CompilerParams(
            collective_id=0, has_side_effects=True, vmem_limit_bytes=VMEM_LIMIT
        ),
    )(*inputs)


def shards(
    mesh, tokens, segment_ids, input_weight, input_bias, output_weight, output_bias, first_gain, first_shift,
    up_weight, up_bias, down_weight, down_bias, second_gain, second_shift, cotangent,
):
    dm = Dims(mesh, *tokens.shape, up_weight.shape[1])
    tokT = jnp.transpose(tokens, (0, 2, 1))
    cotT = jnp.transpose(cotangent, (0, 2, 1))
    loT, tgT, wF, fu, fd, fo, svF, bvF, *_ = run_layer(
        dm, tokT, segment_ids, jnp.transpose(input_weight, (0, 2, 1)), input_bias, cotT,
        output_bias, first_gain, first_shift, down_bias, second_gain, second_shift, up_bias,
        up_weight, down_weight, output_weight,
    )
    low = write_outputs(dm, loT, tgT, wF, fu, fd, fo, svF, bvF)
    layer_output, tokens_grad, w_grad, out_w, up_w, down_w, bias, ub, *vectors = low
    second_gain_g, second_shift_g, down_b, first_gain_g, first_shift_g, out_b = vectors
    return (
        jnp.transpose(layer_output, (0, 2, 1)),
        jnp.transpose(tokens_grad, (0, 2, 1)),
        jnp.transpose(w_grad, (0, 2, 1)),
        bias,
        out_w,
        out_b,
        first_gain_g,
        first_shift_g,
        up_w,
        ub,
        down_w,
        down_b,
        second_gain_g,
        second_shift_g,
    )


def output_kernel(dm, loT, tgT, wF, fu, fd, fo, svF, bvF, lo, tg, w_o, fo_o, fu_o, fd_o, bias, ub, *vectors):
    lo[...] = loT[...]
    tg[...] = tgT[...]
    w_o[...] = wF[...].reshape(3, dm.lw, dm.d).astype(f32)
    fu_o[...] = fu[...].astype(f32)
    fd_o[...] = fd[...].astype(f32)
    fo_o[...] = fo[...].astype(f32)
    bias[...] = bvF[0:2, 0 : dm.lw]
    for n, ref in enumerate(vectors):
        ref[...] = svF[n, :]
    t = lax.axis_index("tensor")
    for half in range(2):
        row = svF[pl.ds(6 + 2 * half + lax.div(t, 2), 1), cut(lax.rem(t, 2), dm.hf)]
        ub[pl.ds(dm.hf * half, dm.hf)] = row.reshape(dm.hf)


def write_outputs(dm, *inputs):
    shape = jax.ShapeDtypeStruct
    vmem = pl.BlockSpec(memory_space=pltpu.VMEM)
    outs = [
        shape((dm.rows, dm.lw, dm.tok), bf16),
        shape((dm.rows, dm.lw, dm.tok), f32),
        shape((3, dm.lw, dm.d), f32),
        shape((dm.lw, dm.d), f32),
        shape((dm.d, dm.ff), f32),
        shape((dm.ff, dm.d), f32),
        shape((2, dm.lw), f32),
        shape((dm.ff,), f32),
        *[shape((dm.d,), f32)] * 6,
    ]
    return pl.pallas_call(
        functools.partial(output_kernel, dm),
        name="write_outputs",
        out_shape=outs,
        in_specs=[vmem] * len(inputs),
        out_specs=[vmem] * len(outs),
        compiler_params=pltpu.CompilerParams(vmem_limit_bytes=VMEM_LIMIT),
    )(*inputs)


def solution(mesh):
    rows = P("dp", "blk", "tensor")
    placed = (
        rows, P("dp", "blk"), P(None, None, "tensor"), P(None, "tensor"), P("tensor", None), P(), P(), P(),
        P(None, "tensor"), P("tensor"), P("tensor", None), P(), P(), P(), rows,
    )
    results = (
        rows, rows, P(None, None, "tensor"), P(None, "tensor"), P("tensor", None), P(), P(), P(),
        P(None, "tensor"), P("tensor"), P("tensor", None), P(), P(), P(),
    )
    return jax.shard_map(
        functools.partial(shards, mesh), mesh=mesh, in_specs=placed, out_specs=results, check_vma=False
    )
```
